32 devices in a mesh: dp: 8 (over z, y), head: 4 (over x, core).
Axes of the slice: x: 2, y: 2, z: 4, core: 2. Of those that a mesh axis runs over, the one named last changes fastest.
Arguments:
- tokens: bfloat16 [16384, 768], P(('dp', 'head')), may hold values from -6 to 6
- seq_len: int32 [128], P('dp'), may hold values from 128 to 512, as said below
- norm1_gain: float32 [768], replicated, may hold values from 0.25 to 1.75
- norm1_bias: float32 [768], replicated, may hold values from -1.75 to 1.75
- f1_weight: bfloat16 [12, 768, 768], P('head'), may hold values from -0.21875 to 0.21875
- f1_bias: float32 [12, 768], P('head'), may hold values from -3 to 3
- f2_weight: bfloat16 [12, 768, 512], P('head'), may hold values from -0.4375 to 0.4375
- f2_bias: float32 [12, 512], P('head'), may hold values from -3 to 3
- value_weight: bfloat16 [768, 768], P(None, 'head'), may hold values from -0.21875 to 0.21875
- out_weight: bfloat16 [768, 768], replicated, may hold values from -0.875 to 0.875
- norm2_gain: float32 [768], replicated, may hold values from 0.25 to 1.75
- norm2_bias: float32 [768], replicated, may hold values from -1.75 to 1.75
- up_weight: bfloat16 [768, 3072], P(None, 'head'), may hold values from -0.21875 to 0.21875
- up_bias: float32 [3072], P('head'), may hold values from -3 to 3
- down_weight: bfloat16 [3072, 768], P('head'), may hold values from -0.109375 to 0.109375
- down_bias: float32 [768], replicated, may hold values from -1.75 to 1.75
- out_grad: bfloat16 [16384, 768], P(('dp', 'head')), may hold values from -6 to 6
Outputs:
- result: float32 [16384, 768], P(('dp', 'head'))
- input_grad: float32 [16384, 768], P(('dp', 'head'))
- norm1_gain_grad: float32 [768], replicated
- norm1_bias_grad: float32 [768], replicated
- f1_weight_grad: float32 [12, 768, 768], P('head', 'dp')
- f1_bias_grad: float32 [12, 768], replicated
- f2_weight_grad: float32 [12, 768, 512], P('head', 'dp')
- f2_bias_grad: float32 [12, 512], replicated
- value_weight_grad: float32 [768, 768], P('dp', 'head')
- out_weight_grad: float32 [768, 768], P('dp')
- norm2_gain_grad: float32 [768], replicated
- norm2_bias_grad: float32 [768], replicated
- up_weight_grad: float32 [768, 3072], P('dp', 'head')
- up_bias_grad: float32 [3072], replicated
- down_weight_grad: float32 [3072, 768], P('head', 'dp')
- down_bias_grad: float32 [768], replicated
The draws below stay inside these ranges and needn't reach their ends.
Inputs may be any that keep to these rules, and one draw needn't show every extreme that they name: `seq_len`: each aligned block of 512 rows is cut into sequences of 128, 256 or 512 rows, each starting at a multiple of its own length; every row of a sequence has its length.
All inputs are finite; a program needn't handle non-finite values.
Results may differ from the reference program's by a relative error of at most 0.017.
Values may be sent and summed in bfloat16 or wider, within the bound.
A program may use at most 256 MiB of HBM per device.

```python
import jax
import jax.numpy as jnp
from jax import lax

D = 768
HEADS = 12
HEAD_DIM = 64
FF = 3072
LMAX = 512
QUARTER = 128
TOK_DEV = 512
TOKENS = 16384
N_HEAD = 4


def draw_seq_len(key, part):
    slab_count = TOKENS // LMAX
    layout_pick = jax.random.randint(key, (slab_count,), 0, 5)
    layout_pick = layout_pick.at[0].set(0).at[1].set(4)
    layouts = jnp.array([[4, 4, 4, 4], [2, 2, 2, 2], [2, 2, 1, 1], [1, 1, 2, 2], [1, 1, 1, 1]], dtype=jnp.int32)
    chosen = layouts[layout_pick] * QUARTER
    return chosen.reshape(-1).astype(jnp.int32)


def block_scale(stream_key, shape, cuts, low, largest):
    def one(dim, parts):
        steps = jax.random.uniform(jax.random.fold_in(jax.random.fold_in(stream_key, 6), dim), (parts,), jnp.float32, low / len(cuts), largest / len(cuts))
        return jnp.repeat(jnp.exp(steps), shape[dim] // parts).reshape((-1,) + (1,) * (len(shape) - dim - 1))

    factor_of = one(*cuts[0])
    for cut in cuts[1:]:
        factor_of = factor_of * one(*cut)
    return factor_of


def gaussian(own_key, shape, scale, reach, shards=(), held_as=jnp.bfloat16):
    values = jax.random.normal(own_key, shape, jnp.float32) * scale
    if len(shards) > 0:
        values = block_scale(own_key, shape, shards, -0.22, 0.18) * values
    return jnp.clip(values, min=-reach, max=reach).astype(held_as)


def setup_inputs(seed: int = 0) -> dict:
    seeds = jax.random.split(jax.random.key(seed), 18)
    return {
        "tokens": gaussian(seeds[0], (TOKENS, D), 1.0, 6.0, ((0, 32),)),
        "seq_len": draw_seq_len(jax.random.fold_in(seeds[17], 71), 0),
        "norm1_gain": jnp.clip(1.0 + 0.15 * jax.random.normal(seeds[2], (D,), jnp.float32), 0.25, 1.75),
        "norm1_bias": gaussian(seeds[3], (D,), 0.3, 1.75, (), jnp.float32),
        "f1_weight": gaussian(seeds[4], (HEADS, D, D), D ** -0.5, 0.21875, ((0, 4),)),
        "f1_bias": gaussian(seeds[5], (HEADS, D), 0.5, 3.0, ((0, 4),), jnp.float32),
        "f2_weight": gaussian(seeds[6], (HEADS, D, LMAX), (D // 4) ** -0.5, 0.4375, ((0, 4),)),
        "f2_bias": gaussian(seeds[7], (HEADS, LMAX), 0.5, 3.0, ((0, 4),), jnp.float32),
        "value_weight": gaussian(seeds[8], (D, D), D ** -0.5, 0.21875, ((1, 4),)),
        "out_weight": gaussian(seeds[9], (D, D), (D // 16) ** -0.5, 0.875),
        "norm2_gain": jnp.clip(1.0 + 0.15 * jax.random.normal(seeds[10], (D,), jnp.float32), 0.25, 1.75),
        "norm2_bias": gaussian(seeds[11], (D,), 0.3, 1.75, (), jnp.float32),
        "up_weight": gaussian(seeds[12], (D, FF), D ** -0.5, 0.21875, ((1, 4),)),
        "up_bias": gaussian(seeds[13], (FF,), 0.5, 3.0, ((0, 4),), jnp.float32),
        "down_weight": gaussian(seeds[14], (FF, D), FF ** -0.5, 0.109375, ((0, 4),)),
        "down_bias": gaussian(seeds[15], (D,), 0.3, 1.75, (), jnp.float32),
        "out_grad": gaussian(seeds[16], (TOKENS, D), 1.0, 6.0, ((0, 32),)),
    }


@jax.custom_vjp
def low(v):
    return lax.optimization_barrier(v.astype(jnp.bfloat16)).astype(jnp.float32)

@jax.custom_vjp
def low_back(v):
    return v

def low_keep(v):
    return (low(v), None)

def low_pass(kept, grad):
    return (grad,)

def back_keep(v):
    return (v, None)

def back_low(kept, grad):
    return (low(grad),)
low.defvjp(low_keep, low_pass)
low_back.defvjp(back_keep, back_low)
HIGHEST = lax.Precision.HIGHEST

def normalize(values, gain, shift):
    centred = values - lax.optimization_barrier(jnp.mean(values, -1, keepdims=True))
    inv_std = lax.rsqrt(lax.optimization_barrier(jnp.mean(centred * centred, -1, keepdims=True)) + 1e-05)
    return centred * inv_std * gain + shift

def spread_scores(scores, row_len):
    half_len = LMAX // 2
    quarter_len = LMAX // 4
    twice = jnp.concatenate([scores[..., :half_len]] * 2, axis=-1)
    fourfold = jnp.concatenate([scores[..., :quarter_len]] * 4, axis=-1)
    return jnp.where(row_len == LMAX, scores, jnp.where(row_len == half_len, twice, fourfold))

def same_sequence(row_len):
    positions = jnp.arange(LMAX, dtype=jnp.int32)
    return positions[:, None] // row_len == positions[None, :] // row_len

def masked_softmax(spread, seq_mask):
    floor_val = lax.optimization_barrier(jnp.min(spread, -1, keepdims=True))
    top_val = lax.optimization_barrier(jnp.max(jnp.where(seq_mask, spread, floor_val), -1, keepdims=True))
    exp_val = jnp.where(seq_mask, jnp.exp(spread - top_val), 0.0)
    return exp_val / lax.optimization_barrier(jnp.sum(exp_val, -1, keepdims=True))

def forward(inputs_x, norm1_gain, norm1_bias, f1_weight, f1_bias, f2_weight, f2_bias, value_weight, out_weight, norm2_gain, norm2_bias, up_weight, up_bias, down_weight, down_bias, row_len):
    row_count = inputs_x.shape[0]
    slab_count = row_count // LMAX
    group_size = HEADS // N_HEAD
    ffn_width = FF // N_HEAD
    seq_mask = same_sequence(row_len)
    shared = low(normalize(inputs_x, norm1_gain, norm1_bias))
    pieces = []
    for member in range(N_HEAD):
        inputs = low_back(shared)
        first = member * group_size
        last = first + group_size
        pre_one = jnp.einsum('rd,hde->hre', inputs, f1_weight[first:last], precision=HIGHEST) + f1_bias[first:last][:, None, :]
        hidden = low(jax.nn.silu(low_back(pre_one)))
        scores = low_back(jnp.einsum('hre,hel->hrl', hidden, f2_weight[first:last], precision=HIGHEST) + f2_bias[first:last][:, None, :])
        value_cols = value_weight[:, first * HEAD_DIM:last * HEAD_DIM]
        values = low(low_back(jnp.dot(inputs, value_cols, precision=HIGHEST)))
        spread = spread_scores(scores.reshape(group_size, slab_count, LMAX, LMAX), row_len)
        weights = low(masked_softmax(spread, seq_mask))
        mixed = jnp.einsum('hnqk,nkhd->nqhd', weights, values.reshape(slab_count, LMAX, group_size, HEAD_DIM), precision=HIGHEST)
        pieces.append(low(low_back(mixed.reshape(row_count, group_size * HEAD_DIM))))
    attended = jnp.concatenate(pieces, axis=1)
    residual = inputs_x + low_back(jnp.dot(attended, out_weight, precision=HIGHEST))
    shared_mid = low(normalize(residual, norm2_gain, norm2_bias))
    total = residual + down_bias
    for member in range(N_HEAD):
        inputs = low_back(shared_mid)
        first = member * ffn_width
        last = first + ffn_width
        pre_up = jnp.dot(inputs, up_weight[:, first:last], precision=HIGHEST) + up_bias[first:last]
        act_val = low(jax.nn.silu(low_back(pre_up)))
        total = total + low(jnp.dot(act_val, down_weight[first:last], precision=HIGHEST))
    return total

def reference(tokens, seq_len, norm1_gain, norm1_bias, f1_weight, f1_bias, f2_weight, f2_bias, value_weight, out_weight, norm2_gain, norm2_bias, up_weight, up_bias, down_weight, down_bias, out_grad):
    params = tuple((weight_in.astype(jnp.float32) for weight_in in (norm1_gain, norm1_bias, f1_weight, f1_bias, f2_weight, f2_bias, value_weight, out_weight, norm2_gain, norm2_bias, up_weight, up_bias, down_weight, down_bias)))
    block_rows = N_HEAD * TOK_DEV
    block_count = TOKENS // block_rows
    token_blocks = tokens.astype(jnp.float32).reshape(block_count, block_rows, D)
    cotangent = out_grad.astype(jnp.float32).reshape(block_count, block_rows, D)
    length_rows = jnp.repeat(seq_len.astype(jnp.int32).reshape(block_count, block_rows // QUARTER), QUARTER, axis=1)
    length_rows = length_rows.reshape(block_count, block_rows // LMAX, LMAX, 1).astype(jnp.int32)

    def one_block(running, slices):
        block_x, block_len, block_cot = slices

        def apply(x_in, *weights_in):
            return forward(x_in, *weights_in, block_len)
        output, pullback = jax.vjp(apply, block_x, *params)
        gradients = pullback(block_cot)
        running = tuple((acc + grad_val for acc, grad_val in zip(running, gradients[1:])))
        return (running, (output, gradients[0]))
    zeroes = tuple((jnp.zeros_like(weight_in) for weight_in in params))
    totals, (outputs, input_grads) = lax.scan(one_block, zeroes, (token_blocks, length_rows, cotangent))
    return (outputs.reshape(TOKENS, D), input_grads.reshape(TOKENS, D), totals[0], totals[1], totals[2], totals[3], totals[4], totals[5], totals[6], totals[7], totals[8], totals[9], totals[10], totals[11], totals[12], totals[13])
```

```python
import functools

import jax
import jax.numpy as jnp
from jax import lax
from jax.experimental import pallas as pl
from jax.experimental.pallas import tpu as pltpu
from jax.sharding import PartitionSpec as P

F32 = jnp.float32
BF16 = jnp.bfloat16
BLOCK = 128
VMEM_LIMIT = 50 << 20


def mm(a, b):
    return lax.dot_general(a, b, (((1,), (0,)), ((), ())), preferred_element_type=F32)


def mm_nt(a, b):
    return lax.dot_general(a, b, (((1,), (1,)), ((), ())), preferred_element_type=F32)


def mm_tn(a, b):
    return lax.dot_general(a, b, (((0,), (0,)), ((), ())), preferred_element_type=F32)


def standardize(values):
    centred = values - jnp.mean(values, -1, keepdims=True)
    inv_std = lax.rsqrt(jnp.mean(centred * centred, -1, keepdims=True) + 1e-05)
    return centred * inv_std, inv_std


def norm_back(grad_out, scaled, inv_std, gain):
    grad_scaled = grad_out * gain
    centre_mean = jnp.mean(grad_scaled, -1, keepdims=True)
    cross_mean = jnp.mean(grad_scaled * scaled, -1, keepdims=True)
    return inv_std * (grad_scaled - centre_mean - scaled * cross_mean)


def silu_and_slope(pre_val):
    sigma = 0.5 + 0.5 * jnp.tanh(0.5 * pre_val)
    gated = pre_val * sigma
    return gated, sigma + gated * (1.0 - sigma)


def swap(value, axis, step):
    return lax.ppermute(value, axis, [(i, i ^ step) for i in range(lax.axis_size(axis))])


def whole(shape):
    return pl.BlockSpec(shape, lambda *_: (0,) * len(shape))


def params(steps=1):
    return pltpu.CompilerParams(
        dimension_semantics=("arbitrary",) * steps, vmem_limit_bytes=VMEM_LIMIT
    )


def cost(macs, bytes_accessed):
    return pl.CostEstimate(flops=2 * macs, bytes_accessed=bytes_accessed, transcendentals=0)


def head_forward_kernel(
    step,
    lens_ref,
    x_ref,
    gain_ref,
    bias_ref,
    f1_ref,
    f1b_ref,
    f2_ref,
    f2b_ref,
    vt_ref,
    *rest,
):
    n1_ref, n1t_ref, hid_ref, slope_ref, prob_ref, valt_ref, mixt_ref = rest[-7:]
    rows, longest = prob_ref.shape[-2:]
    blocks = longest // BLOCK

    @pl.when(pl.program_id(0) == 0)
    def _():
        scaled, _ = standardize(x_ref[...].astype(F32))
        low = (scaled * gain_ref[...] + bias_ref[...]).astype(BF16)
        n1_ref[...] = low
        n1t_ref[0] = low.T

    valt = mm(vt_ref[0], n1t_ref[0]).astype(BF16)
    valt_ref[0, 0] = valt
    pre = mm(n1_ref[...], f1_ref[0]) + f1b_ref[0]
    gated, slope = silu_and_slope(pre)
    hidden = gated.astype(BF16)
    hid_ref[0, 0] = hidden
    slope_ref[0, 0] = slope.astype(BF16)
    scores = mm(hidden, f2_ref[0]) + f2b_ref[0]
    first = jnp.bitwise_xor(lax.axis_index("head"), step) * blocks
    column = lax.broadcasted_iota(jnp.int32, (BLOCK, longest), 1)
    for b in range(rows // BLOCK):
        length = lens_ref[first + b]
        own = scores[b * BLOCK : (b + 1) * BLOCK]
        keep = column < length
        top = jnp.max(jnp.where(keep, own, -3.0e38), -1, keepdims=True)
        exp_val = jnp.where(keep, jnp.exp(own - top), 0.0)
        prob = exp_val * (1.0 / jnp.sum(exp_val, -1, keepdims=True))
        parts = [prob[:, c * BLOCK : (c + 1) * BLOCK] for c in range(blocks)]
        zero = jnp.zeros((BLOCK, BLOCK), F32)
        is_full = length == longest
        is_half = length == longest // 2
        for c in range(blocks):
            half = parts[c % 2] if c // 2 == b // 2 else zero
            quarter = parts[0] if c == b else zero
            cell = jnp.where(is_full, parts[c], jnp.where(is_half, half, quarter))
            prob_ref[0, 0, b * BLOCK : (b + 1) * BLOCK, c * BLOCK : (c + 1) * BLOCK] = cell.astype(
                BF16
            )
    mixt_ref[...] = mm_nt(valt, prob_ref[0, 0]).astype(BF16)


def head_forward(step, kept, seq_len, x, gain, bias, f1, f1b, f2, f2b, vt):
    heads, width, longest = f2.shape
    rows = x.shape[0]
    dim = vt.shape[1]
    slabs = lax.axis_size("head")
    stacked = [
        ((slabs, width, rows), (1, width, rows), lambda h: (step, 0, 0)),
        ((slabs, heads, rows, width), (1, 1, rows, width), lambda h: (step, h, 0, 0)),
        ((slabs, heads, rows, width), (1, 1, rows, width), lambda h: (step, h, 0, 0)),
        ((slabs, heads, rows, longest), (1, 1, rows, longest), lambda h: (step, h, 0, 0)),
        ((slabs, heads, dim, rows), (1, 1, dim, rows), lambda h: (step, h, 0, 0)),
    ]
    out_shape = (
        [jax.ShapeDtypeStruct((rows, width), BF16)]
        + [jax.ShapeDtypeStruct(shape, BF16) for shape, _, _ in stacked]
        + [jax.ShapeDtypeStruct((heads * dim, rows), BF16)]
    )
    out_specs = (
        [whole((rows, width))]
        + [pl.BlockSpec(block, index) for _, block, index in stacked]
        + [pl.BlockSpec((dim, rows), lambda h: (h, 0))]
    )
    in_specs = [
        pl.BlockSpec(memory_space=pltpu.SMEM),
        whole((rows, width)),
        whole((1, width)),
        whole((1, width)),
        pl.BlockSpec((1, width, width), lambda h: (h, 0, 0)),
        pl.BlockSpec((1, 1, width), lambda h: (h, 0, 0)),
        pl.BlockSpec((1, width, longest), lambda h: (h, 0, 0)),
        pl.BlockSpec((1, 1, longest), lambda h: (h, 0, 0)),
        pl.BlockSpec((1, dim, width), lambda h: (h, 0, 0)),
    ]
    args = [seq_len, x, gain, bias, f1, f1b, f2, f2b, vt]
    aliases = {}
    if kept is not None:
        for i, buffer in enumerate(kept):
            aliases[len(args)] = 1 + i
            args.append(buffer)
            in_specs.append(pl.BlockSpec(memory_space=pl.ANY))
    outs = pl.pallas_call(
        functools.partial(head_forward_kernel, step),
        grid=(heads,),
        out_shape=out_shape,
        in_specs=in_specs,
        out_specs=out_specs,
        input_output_aliases=aliases,
        compiler_params=params(),
        cost_estimate=cost(heads * rows * width * (width + longest + 128), 14 << 20),
        name="head_forward",
    )(*args)
    return outs[1:6], outs[6]


def residual_kernel(*refs):
    pieces = refs[:-7]
    x_ref, ow_ref, gain_ref, bias_ref, res_ref, n2_ref, attt_ref = refs[-7:]
    depth = pieces[0].shape[0]
    me = lax.axis_index("head")
    for j, piece in enumerate(pieces):
        start = pl.multiple_of(jnp.bitwise_xor(me, j) * depth, depth)
        attt_ref[pl.ds(start, depth), :] = piece[...]
    residual = x_ref[...].astype(F32) + mm_tn(attt_ref[...], ow_ref[...])
    res_ref[...] = residual
    scaled, _ = standardize(residual)
    n2_ref[...] = (scaled * gain_ref[...] + bias_ref[...]).astype(BF16)


def residual_and_norm(pieces, x, ow, gain, bias):
    rows, width = x.shape
    return pl.pallas_call(
        residual_kernel,
        out_shape=[
            jax.ShapeDtypeStruct((rows, width), F32),
            jax.ShapeDtypeStruct((rows, width), BF16),
            jax.ShapeDtypeStruct((width, rows), BF16),
        ],
        compiler_params=pltpu.CompilerParams(vmem_limit_bytes=VMEM_LIMIT),
        cost_estimate=cost(rows * width * width, 7 << 20),
        name="residual_and_norm",
    )(*pieces, x, ow, gain, bias)


def ffn_kernel(n2_ref, og_ref, up_ref, upb_ref, down_ref, n2g_ref, ffn_ref, act_ref, pug_ref):
    pre = mm(n2_ref[...], up_ref[...]) + upb_ref[...]
    gated, slope = silu_and_slope(pre)
    act = gated.astype(BF16)
    act_ref[...] = act
    pug = (mm_nt(og_ref[...], down_ref[...]) * slope).astype(BF16)
    pug_ref[...] = pug
    n2g_ref[...] = mm_nt(pug, up_ref[...]).astype(BF16)
    ffn_ref[...] = mm(act, down_ref[...]).astype(BF16)


def ffn(n2, og, up, upb, down):
    rows, width = n2.shape
    units = up.shape[1]
    shapes = [(rows, width), (rows, width), (rows, units), (rows, units)]
    return pl.pallas_call(
        ffn_kernel,
        out_shape=[jax.ShapeDtypeStruct(s, BF16) for s in shapes],
        compiler_params=pltpu.CompilerParams(vmem_limit_bytes=VMEM_LIMIT),
        cost_estimate=cost(4 * rows * width * units, 7 << 20),
        name="ffn",
    )(n2, og, up, upb, down)


def store_shards(keep_ref, send_ref, lanes, acc_ref):
    count, depth = keep_ref.shape[:2]
    me = lax.axis_index("dp")
    pair, parity = me // 2, me % 2
    for k in range(count):
        other = jnp.bitwise_xor(pair, k) * 2
        mine = pl.multiple_of((other + parity) * depth, 8)
        theirs = pl.multiple_of((other + 1 - parity) * depth, 8)
        keep_ref[k, :, lanes] = acc_ref[pl.ds(mine, depth), :].astype(BF16)
        send_ref[k, :, lanes] = acc_ref[pl.ds(theirs, depth), :].astype(BF16)


def shard_shape(width, lanes):
    members = lax.axis_size("dp")
    return jax.ShapeDtypeStruct((members // 2, width // members, lanes), BF16)


def ffn_grads_kernel(slabs, *refs):
    og, n2, act, pug = (refs[i * slabs : (i + 1) * slabs] for i in range(4))
    keep_ref, send_ref, upb_ref, down_acc, up_acc = refs[4 * slabs :]
    step = pl.program_id(0)
    tile = og[0].shape[1]
    units = act[0].shape[1]
    rows = pl.ds(pl.multiple_of(step * tile, tile), tile)
    down_acc[rows, :] = sum(mm_tn(og[j][...], act[j][...]) for j in range(slabs))
    up_acc[rows, :] = sum(mm_tn(n2[j][...], pug[j][...]) for j in range(slabs))

    @pl.when(step == pl.num_programs(0) - 1)
    def _():
        upb_ref[...] = sum(
            jnp.sum(pug[j][...].astype(F32), 0, keepdims=True) for j in range(slabs)
        )
        store_shards(keep_ref, send_ref, slice(0, units), down_acc)
        store_shards(keep_ref, send_ref, slice(units, 2 * units), up_acc)


def ffn_grads(og, n2, act, pug):
    slabs = len(og)
    rows, width = og[0].shape
    units = act[0].shape[1]
    tile = width // 2
    shards = shard_shape(width, 2 * units)
    left = pl.BlockSpec((rows, tile), lambda t: (0, t))
    return pl.pallas_call(
        functools.partial(ffn_grads_kernel, slabs),
        grid=(width // tile,),
        out_shape=[shards, shards, jax.ShapeDtypeStruct((1, units), F32)],
        in_specs=[left] * (2 * slabs) + [whole((rows, units))] * (2 * slabs),
        out_specs=[whole(shards.shape), whole(shards.shape), whole((1, units))],
        scratch_shapes=[pltpu.VMEM((width, units), F32)] * 2,
        compiler_params=params(),
        cost_estimate=cost(2 * slabs * rows * width * units, 18 << 20),
        name="ffn_grads",
    )(*og, *n2, *act, *pug)


def residual_back_kernel(
    t0_ref, t1_ref, t2_ref, res_ref, og_ref, gain_ref, ow_ref, *outs
):
    rg_ref, rl_ref, sums_ref, mgt_ref = outs[0], outs[1], outs[2], outs[-1]
    pieces = outs[3:-1]
    grad = t0_ref[...].astype(F32) + t1_ref[...].astype(F32) + t2_ref[...].astype(F32)
    scaled, inv_std = standardize(res_ref[...])
    cot = og_ref[...].astype(F32)
    res_grad = cot + norm_back(grad, scaled, inv_std, gain_ref[...])
    rg_ref[...] = res_grad
    low = res_grad.astype(BF16)
    rl_ref[...] = low
    sums_ref[0:1, :] = jnp.sum(grad * scaled, 0, keepdims=True)
    sums_ref[1:2, :] = jnp.sum(grad, 0, keepdims=True)
    sums_ref[2:3, :] = jnp.sum(cot, 0, keepdims=True)
    mgt_ref[...] = mm_nt(ow_ref[...], low).astype(BF16)
    depth = pieces[0].shape[0]
    me = lax.axis_index("head")
    for j, piece in enumerate(pieces):
        start = pl.multiple_of(jnp.bitwise_xor(me, j) * depth, depth)
        piece[...] = mgt_ref[pl.ds(start, depth), :]


def residual_back(terms, residual, og, gain, ow, members):
    rows, width = residual.shape
    piece = jax.ShapeDtypeStruct((width // members, rows), BF16)
    return pl.pallas_call(
        residual_back_kernel,
        out_shape=[
            jax.ShapeDtypeStruct((rows, width), F32),
            jax.ShapeDtypeStruct((rows, width), BF16),
            jax.ShapeDtypeStruct((3, width), F32),
        ]
        + [piece] * members,
        scratch_shapes=[pltpu.VMEM((width, rows), BF16)],
        compiler_params=pltpu.CompilerParams(vmem_limit_bytes=VMEM_LIMIT),
        cost_estimate=cost(rows * width * width, 9 << 20),
        name="residual_back",
    )(*terms, residual, og, gain, ow)


def out_grad_kernel(attt_ref, rl_ref, keep_ref, send_ref, acc_ref):
    acc_ref[...] = mm(attt_ref[...], rl_ref[...])
    store_shards(keep_ref, send_ref, slice(None), acc_ref)


def out_weight_grads(attt, low):
    width = attt.shape[0]
    shards = shard_shape(width, low.shape[1])
    return pl.pallas_call(
        out_grad_kernel,
        out_shape=[shards, shards],
        scratch_shapes=[pltpu.VMEM((width, low.shape[1]), F32)],
        compiler_params=pltpu.CompilerParams(vmem_limit_bytes=VMEM_LIMIT),
        cost_estimate=cost(attt.shape[1] * width * width, 3 << 20),
        name="out_weight_grads",
    )(attt, low)


def head_back_kernel(
    lens_ref,
    prob_ref,
    valt_ref,
    mgt_ref,
    hid_ref,
    slope_ref,
    n1t_ref,
    f2_ref,
    pog_ref,
    vgt_ref,
    f1b_ref,
    f2b_ref,
    keep_ref,
    send_ref,
    sg_ref,
    f1_acc,
    f2_acc,
    value_acc,
):
    j = pl.program_id(0)
    rows, longest = prob_ref.shape[-2:]
    blocks = longest // BLOCK

    @pl.when(j == 0)
    def _():
        f1_acc[...] = jnp.zeros_like(f1_acc)
        f2_acc[...] = jnp.zeros_like(f2_acc)
        value_acc[...] = jnp.zeros_like(value_acc)
        f1b_ref[...] = jnp.zeros_like(f1b_ref)
        f2b_ref[...] = jnp.zeros_like(f2b_ref)

    prob_low = prob_ref[0, 0]
    mgt = mgt_ref[0]
    vgt = mm(mgt, prob_low).astype(BF16)
    vgt_ref[0] = vgt
    probs_grad = mm_tn(mgt, valt_ref[0, 0])
    first = jnp.bitwise_xor(lax.axis_index("head"), j) * blocks
    for b in range(rows // BLOCK):
        length = lens_ref[first + b]
        own = slice(b * BLOCK, (b + 1) * BLOCK)
        prob = prob_low[own].astype(F32)
        grad = probs_grad[own]
        inner = jnp.sum(prob * grad, -1, keepdims=True)
        spread_grad = prob * (grad - inner)
        parts = [spread_grad[:, c * BLOCK : (c + 1) * BLOCK] for c in range(blocks)]
        zero = jnp.zeros((BLOCK, BLOCK), F32)
        is_full = length == longest
        is_half = length == longest // 2
        for c in range(blocks):
            half = parts[2 * (b // 2) + c] if c < 2 else zero
            quarter = parts[b] if c == 0 else zero
            cell = jnp.where(is_full, parts[c], jnp.where(is_half, half, quarter))
            sg_ref[own, c * BLOCK : (c + 1) * BLOCK] = cell.astype(BF16)
    scores_grad = sg_ref[...]
    f2b_ref[...] += jnp.sum(scores_grad.astype(F32), 0, keepdims=True)
    hidden_grad = mm_nt(scores_grad, f2_ref[0])
    pog = (hidden_grad * slope_ref[0, 0].astype(F32)).astype(BF16)
    pog_ref[0] = pog
    f1b_ref[...] += jnp.sum(pog.astype(F32), 0, keepdims=True)
    f2_acc[...] += mm_tn(hid_ref[0, 0], scores_grad)
    n1t = n1t_ref[0]
    f1_acc[...] += mm(n1t, pog)
    value_acc[...] += mm_nt(n1t, vgt)

    @pl.when(j == pl.num_programs(0) - 1)
    def _():
        width = f1_acc.shape[1]
        dim = value_acc.shape[1]
        store_shards(keep_ref, send_ref, slice(0, width), f1_acc)
        store_shards(keep_ref, send_ref, slice(width, width + longest), f2_acc)
        store_shards(
            keep_ref, send_ref, slice(width + longest, width + longest + dim), value_acc
        )


def head_back(h, seq_len, prob, valt, mgt, hid, slope, n1t, f2):
    slabs, heads, rows, longest = prob.shape
    width = hid.shape[3]
    dim = valt.shape[2]
    shards = shard_shape(width, width + longest + dim)
    by_head = lambda j: (j, h, 0, 0)
    by_slab = lambda j: (j, 0, 0)
    return pl.pallas_call(
        head_back_kernel,
        grid=(slabs,),
        out_shape=[
            jax.ShapeDtypeStruct((slabs, rows, width), BF16),
            jax.ShapeDtypeStruct((slabs, dim, rows), BF16),
            jax.ShapeDtypeStruct((1, width), F32),
            jax.ShapeDtypeStruct((1, longest), F32),
            shards,
            shards,
        ],
        in_specs=[
            pl.BlockSpec(memory_space=pltpu.SMEM),
            pl.BlockSpec((1, 1, rows, longest), by_head),
            pl.BlockSpec((1, 1, dim, rows), by_head),
            pl.BlockSpec((1, dim, rows), lambda j: (j, h, 0)),
            pl.BlockSpec((1, 1, rows, width), by_head),
            pl.BlockSpec((1, 1, rows, width), by_head),
            pl.BlockSpec((1, width, rows), by_slab),
            pl.BlockSpec((1, width, longest), lambda j: (h, 0, 0)),
        ],
        out_specs=[
            pl.BlockSpec((1, rows, width), by_slab),
            pl.BlockSpec((1, dim, rows), by_slab),
            whole((1, width)),
            whole((1, longest)),
            whole(shards.shape),
            whole(shards.shape),
        ],
        scratch_shapes=[
            pltpu.VMEM((rows, longest), BF16),
            pltpu.VMEM((width, width), F32),
            pltpu.VMEM((width, longest), F32),
            pltpu.VMEM((width, dim), F32),
        ],
        compiler_params=params(),
        cost_estimate=cost(slabs * rows * width * (width + 2 * longest + 256), 20 << 20),
        name="head_back",
    )(seq_len, prob, valt, mgt, hid, slope, n1t, f2)


def input_term_kernel(heads, *refs):
    pogs, vgts = refs[:heads], refs[heads : 2 * heads]
    f1_ref, vt_ref, x_ref, sums_in, out_ref, sums_ref = refs[2 * heads :]
    term = mm_nt(pogs[0][0], f1_ref[0])
    for h in range(1, heads):
        term += mm_nt(pogs[h][0], f1_ref[h])
    for h in range(heads):
        term += mm_tn(vgts[h][0], vt_ref[h])
    low = term.astype(BF16)
    out_ref[...] = low
    wide = low.astype(F32)
    scaled, _ = standardize(x_ref[...].astype(F32))
    sums_ref[0:1, :] = sums_in[0:1, :] + jnp.sum(wide * scaled, 0, keepdims=True)
    sums_ref[1:2, :] = sums_in[1:2, :] + jnp.sum(wide, 0, keepdims=True)


def input_term(j, pogs, vgts, f1, vt, x, sums):
    heads = len(pogs)
    slabs, rows, width = pogs[0].shape
    dim = vgts[0].shape[1]
    slab = lambda _: (j, 0, 0)
    return pl.pallas_call(
        functools.partial(input_term_kernel, heads),
        grid=(1,),
        out_shape=[
            jax.ShapeDtypeStruct((rows, width), BF16),
            jax.ShapeDtypeStruct((2, width), F32),
        ],
        in_specs=[pl.BlockSpec((1, rows, width), slab)] * heads
        + [pl.BlockSpec((1, dim, rows), slab)] * heads
        + [whole(f1.shape), whole(vt.shape), whole((rows, width)), whole((2, width))],
        out_specs=[whole((rows, width)), whole((2, width))],
        compiler_params=params(),
        cost_estimate=cost(heads * rows * width * (width + 256), 8 << 20),
        name="input_term",
    )(*pogs, *vgts, f1, vt, x, sums)


def input_back_kernel(t0_ref, t1_ref, t2_ref, x_ref, rg_ref, gain_ref, out_ref):
    grad = t0_ref[...].astype(F32) + t1_ref[...].astype(F32) + t2_ref[...].astype(F32)
    scaled, inv_std = standardize(x_ref[...].astype(F32))
    out_ref[...] = rg_ref[...] + norm_back(grad, scaled, inv_std, gain_ref[...])


def input_back(terms, x, res_grad, gain):
    return pl.pallas_call(
        input_back_kernel,
        out_shape=jax.ShapeDtypeStruct(res_grad.shape, F32),
        compiler_params=pltpu.CompilerParams(vmem_limit_bytes=VMEM_LIMIT),
        cost_estimate=cost(0, 7 << 20),
        name="input_back",
    )(*terms, x, res_grad, gain)


def gather_group(own):
    near = swap(own, "head", 1)
    far = swap(own, "head", 2)
    return [own, near, far, swap(far, "head", 1)]


def add_low(a, b):
    return (a.astype(F32) + b.astype(F32)).astype(BF16)


def scatter_terms(terms):
    cross = swap(add_low(terms[2], swap(terms[3], "head", 1)), "head", 2)
    return [terms[0], swap(terms[1], "head", 1), cross]


def reduce_over_dp(keep, send):
    both = keep.astype(F32) + swap(send, "dp", 1).astype(F32)
    total = both[0]
    low = both.astype(BF16)
    for k in range(1, keep.shape[0]):
        total = total + swap(low[k], "dp", 2 * k).astype(F32)
    return total


def local(
    tokens,
    seq_len,
    norm1_gain,
    norm1_bias,
    f1_weight,
    f1_bias,
    f2_weight,
    f2_bias,
    value_weight,
    out_weight,
    norm2_gain,
    norm2_bias,
    up_weight,
    up_bias,
    down_weight,
    down_bias,
    out_grad,
):
    members = lax.axis_size("head")
    heads, width, longest = f2_weight.shape
    units = up_weight.shape[1]
    dim = value_weight.shape[1] // heads
    row = lambda v: v.reshape(1, -1)
    vt = value_weight.T.reshape(heads, dim, width)
    f1b = f1_bias.reshape(heads, 1, width)
    f2b = f2_bias.reshape(heads, 1, longest)

    xs = gather_group(tokens)
    cot, _ = lax.optimization_barrier((out_grad, xs[2]))
    kept = None
    pieces = []
    for j in range(members):
        kept, mixt = head_forward(
            j,
            kept,
            seq_len,
            xs[j],
            row(norm1_gain),
            row(norm1_bias),
            f1_weight,
            f1b,
            f2_weight,
            f2b,
            vt,
        )
        pieces.append(mixt if j == 0 else swap(mixt, "head", j))
    n1t, hid, slope, prob, valt = kept
    residual, n2, attt = residual_and_norm(
        pieces, tokens, out_weight, row(norm2_gain), row(norm2_bias)
    )
    ogs = gather_group(cot)
    n2s = gather_group(n2)
    n2g, ffn_out, act, pug = zip(
        *[ffn(n2s[j], ogs[j], up_weight, row(up_bias), down_weight) for j in range(members)]
    )
    grad_terms = scatter_terms(n2g)
    ffn_keep, ffn_send, upb = ffn_grads(ogs, n2s, act, pug)
    res_grad, res_low, sums2, *mgts = residual_back(
        grad_terms, residual, out_grad, row(norm2_gain), out_weight, members
    )
    mgt = jnp.stack([m if j == 0 else swap(m, "head", j) for j, m in enumerate(mgts)])
    out_keep, out_send = out_weight_grads(attt, res_low)
    ffn_terms = scatter_terms(ffn_out)
    result = residual + sum(t.astype(F32) for t in ffn_terms) + down_bias

    backs = [
        head_back(h, seq_len, prob, valt, mgt, hid, slope, n1t, f2_weight) for h in range(heads)
    ]
    pogs, vgts, f1bg, f2bg, head_keep, head_send = zip(*backs)
    sums1 = jnp.zeros((2, width), F32)
    terms = [None] * members
    for j in reversed(range(members)):
        terms[j], sums1 = input_term(j, pogs, vgts, f1_weight, vt, xs[j], sums1)
    input_grad = input_back(scatter_terms(terms), tokens, res_grad, row(norm1_gain))

    ffn_total = reduce_over_dp(ffn_keep, ffn_send)
    out_total = reduce_over_dp(out_keep, out_send)
    head_totals = [reduce_over_dp(k, s) for k, s in zip(head_keep, head_send)]
    low = out_total.astype(BF16)
    low = add_low(low, swap(low, "head", 1))
    out_piece = low.astype(F32) + swap(low, "head", 2).astype(F32)

    own = jnp.concatenate(
        [v.reshape(-1) for v in f1bg] + [v.reshape(-1) for v in f2bg] + [upb.reshape(-1)]
    )
    shared = jnp.concatenate([sums1.reshape(-1), sums2.reshape(-1)])
    split = own.shape[0]
    vec = jnp.concatenate([own, shared]).reshape(-1, 128)
    step = 1
    while step < lax.axis_size("dp"):
        vec = vec + swap(vec, "dp", step)
        step *= 2
    flat = vec.reshape(-1)
    own, shared = flat[:split].reshape(1, -1), flat[split:]
    step = 1
    while step < members:
        got = swap(jnp.concatenate([own.reshape(-1), shared]).reshape(-1, 128), "head", step)
        got = got.reshape(-1)
        shared = shared + got[own.size :]
        own = jnp.concatenate([own, got[: own.size].reshape(own.shape)])
        step *= 2
    order = jnp.bitwise_xor(jnp.arange(members), lax.axis_index("head"))
    own = own[order]
    f1b_all = own[:, : heads * width].reshape(members * heads, width)
    f2b_all = own[:, heads * width : heads * (width + longest)].reshape(members * heads, longest)
    upb_all = own[:, heads * (width + longest) :].reshape(members * units)
    shared = shared.reshape(5, width)

    f1_piece = jnp.stack([t[:, :width] for t in head_totals])
    f2_piece = jnp.stack([t[:, width : width + longest] for t in head_totals])
    value_piece = jnp.concatenate([t[:, width + longest :] for t in head_totals], 1)
    return (
        result,
        input_grad,
        shared[0],
        shared[1],
        f1_piece,
        f1b_all,
        f2_piece,
        f2b_all,
        value_piece,
        out_piece,
        shared[2],
        shared[3],
        ffn_total[:, units:],
        upb_all,
        ffn_total[:, :units].T,
        shared[4],
    )


def solution(mesh):
    placed = (
        P(("dp", "head"), None),
        P("dp"),
        P(),
        P(),
        P("head", None, None),
        P("head", None),
        P("head", None, None),
        P("head", None),
        P(None, "head"),
        P(),
        P(),
        P(),
        P(None, "head"),
        P("head"),
        P("head", None),
        P(),
        P(("dp", "head"), None),
    )
    return jax.shard_map(
        local,
        mesh=mesh,
        in_specs=placed,
        out_specs=(
            P(("dp", "head"), None),
            P(("dp", "head"), None),
            P(),
            P(),
            P("head", "dp", None),
            P(),
            P("head", "dp", None),
            P(),
            P("dp", "head"),
            P("dp", None),
            P(),
            P(),
            P("dp", "head"),
            P(),
            P("head", "dp"),
            P(),
        ),
        check_vma=False,
    )
```

```python
import functools
import types

import jax
import jax.numpy as jnp
from jax import lax
from jax.experimental import pallas as pl
from jax.experimental.pallas import tpu as pltpu
from jax.sharding import PartitionSpec as P

F32 = jnp.float32
BF16 = jnp.bfloat16
BLOCK = 128
VMEM_LIMIT = 50 << 20
FRONT_LIMIT = 62 << 20


def mm(a, b):
    return lax.dot_general(a, b, (((1,), (0,)), ((), ())), preferred_element_type=F32)


def mm_nt(a, b):
    return lax.dot_general(a, b, (((1,), (1,)), ((), ())), preferred_element_type=F32)


def mm_tn(a, b):
    return lax.dot_general(a, b, (((0,), (0,)), ((), ())), preferred_element_type=F32)


def standardize(values):
    centred = values - jnp.mean(values, -1, keepdims=True)
    inv_std = lax.rsqrt(jnp.mean(centred * centred, -1, keepdims=True) + 1e-05)
    return centred * inv_std, inv_std


def norm_back(grad_out, scaled, inv_std, gain):
    grad_scaled = grad_out * gain
    centre_mean = jnp.mean(grad_scaled, -1, keepdims=True)
    cross_mean = jnp.mean(grad_scaled * scaled, -1, keepdims=True)
    return inv_std * (grad_scaled - centre_mean - scaled * cross_mean)


def silu_and_slope(pre_val):
    sigma = 0.5 + 0.5 * jnp.tanh(0.5 * pre_val)
    gated = pre_val * sigma
    return gated, sigma + gated * (1.0 - sigma)


def add_low(a, b):
    return (a.astype(F32) + b.astype(F32)).astype(BF16)


def swap(value, axis, step):
    return lax.ppermute(value, axis, [(i, i ^ step) for i in range(lax.axis_size(axis))])


def whole(shape):
    return pl.BlockSpec(shape, lambda *_: (0,) * len(shape))


def params(steps=1):
    return pltpu.CompilerParams(
        dimension_semantics=("arbitrary",) * steps, vmem_limit_bytes=VMEM_LIMIT
    )


def cost(macs, bytes_accessed):
    return pl.CostEstimate(flops=2 * macs, bytes_accessed=bytes_accessed, transcendentals=0)


def store_shards(keep_ref, send_ref, lanes, acc_ref):
    count, depth = keep_ref.shape[:2]
    me = lax.axis_index("dp")
    pair, parity = me // 2, me % 2
    for k in range(count):
        other = jnp.bitwise_xor(pair, k) * 2
        mine = pl.multiple_of((other + parity) * depth, 8)
        theirs = pl.multiple_of((other + 1 - parity) * depth, 8)
        keep_ref[k, :, lanes] = acc_ref[pl.ds(mine, depth), :].astype(BF16)
        send_ref[k, :, lanes] = acc_ref[pl.ds(theirs, depth), :].astype(BF16)


def shard_shape(width, lanes):
    members = lax.axis_size("dp")
    return jax.ShapeDtypeStruct((members // 2, width // members, lanes), BF16)


FRONT_IN = (
    "lens", "x", "og", "gain1", "bias1", "f1b", "f2b", "vt", "gain2", "bias2", "upb", "f1", "f2",
    "ow", "up", "down",
)
FRONT_OUT = (
    "xs_o", "n1t_o", "hid_o", "slope_o", "prob_o", "valt_o", "mgt_o", "f_o", "rg_o", "res_o",
    "fkeep_o", "fsend_o", "okeep_o", "osend_o", "upb_sum", "sums",
)
FRONT_SCRATCH = (
    "xs", "n1", "n1t", "f1v", "f2v", "hidb", "slopeb", "probb", "valt", "mixt", "attt", "owv",
    "upv", "downv", "ogs", "n2s", "act", "pug", "near1", "near3", "crossb", "crossr",
    "fterms", "res", "low", "mgt", "mgts", "acc", "fkeep", "fsend", "okeep", "osend", "send",
    "recv", "load", "spill", "store",
)


def split_prob(parts, length, longest, b, zero):
    is_full = length == longest
    is_half = length == longest // 2
    for c in range(len(parts)):
        half = parts[c % 2] if c // 2 == b // 2 else zero
        quarter = parts[0] if c == b else zero
        yield c, jnp.where(is_full, parts[c], jnp.where(is_half, half, quarter))


def cells(row):
    return [row[:, c : c + BLOCK] for c in range(0, row.shape[1], BLOCK)]


def front_kernel(*refs):
    r = types.SimpleNamespace(**dict(zip(FRONT_IN + FRONT_OUT + FRONT_SCRATCH, refs)))
    r.terms = r.xs
    slabs, rows, width = r.xs.shape
    heads, _, longest = r.f2v.shape
    depth = r.mixt.shape[1]
    dim = depth // heads
    half = rows // 2
    blocks = rows // BLOCK
    me = lax.axis_index("head")

    def remote(index, src, dst, step):
        return pltpu.make_async_remote_copy(
            src_ref=src,
            dst_ref=dst,
            send_sem=r.send.at[index],
            recv_sem=r.recv.at[index],
            device_id={"head": jnp.bitwise_xor(me, step)},
            device_id_type=pl.DeviceIdType.MESH,
        )

    def cut(c):
        return pl.ds(c * half, half)

    my_rows = pl.ds(pl.multiple_of(me * depth, depth), depth)
    moves = {
        "x1": remote(0, r.x, r.xs.at[1], 1),
        "x2": remote(1, r.x, r.xs.at[2], 2),
        "x3": remote(2, r.xs.at[2], r.xs.at[3], 1),
        "o1": remote(3, r.og, r.ogs.at[1], 1),
        "o2": remote(4, r.og, r.ogs.at[2], 2),
        "o3": remote(5, r.ogs.at[2], r.ogs.at[3], 1),
        "t1": remote(15, r.terms.at[1], r.near1, 1),
    }
    for j in range(1, slabs):
        moves[f"m{j}"] = remote(5 + j, r.mixt.at[j], r.attt.at[my_rows], j)
        piece = pl.ds(pl.multiple_of(jnp.bitwise_xor(me, j) * depth, depth), depth)
        moves[f"g{j}"] = remote(19 + j, r.mgt.at[piece], r.mgts.at[j], j)
    for c in range(2):
        part = cut(c)
        moves[f"n1{c}"] = remote(9 + c, r.n2s.at[0, part], r.n2s.at[1, part], 1)
        moves[f"n2{c}"] = remote(11 + c, r.n2s.at[0, part], r.n2s.at[2, part], 2)
        moves[f"n3{c}"] = remote(13 + c, r.n2s.at[2, part], r.n2s.at[3, part], 1)
        moves[f"t3{c}"] = remote(16 + c, r.terms.at[3, part], r.near3.at[part], 1)
        moves[f"c{c}"] = remote(18 + c, r.crossb.at[part], r.crossr.at[part], 2)

    loads = [pltpu.make_async_copy(r.x, r.xs.at[0], r.load.at[0])]
    for h in range(heads):
        loads.append(pltpu.make_async_copy(r.f1.at[h], r.f1v.at[h], r.load.at[1 + 2 * h]))
        loads.append(pltpu.make_async_copy(r.f2.at[h], r.f2v.at[h], r.load.at[2 + 2 * h]))
    base = 1 + 2 * heads
    late = [
        pltpu.make_async_copy(r.ow, r.owv, r.load.at[base]),
        pltpu.make_async_copy(r.up, r.upv, r.load.at[base + 1]),
        pltpu.make_async_copy(r.down, r.downv, r.load.at[base + 2]),
        pltpu.make_async_copy(r.og, r.ogs.at[0], r.load.at[base + 3]),
    ]
    for copy in loads:
        copy.start()
    barrier = pltpu.get_barrier_semaphore()
    for step in range(1, slabs):
        pl.semaphore_signal(
            barrier,
            1,
            device_id={"head": jnp.bitwise_xor(me, step)},
            device_id_type=pl.DeviceIdType.MESH,
        )
    pl.semaphore_wait(barrier, slabs - 1)
    moves["x2"].start()
    moves["x1"].start()
    for copy in late:
        copy.start()
    loads[0].wait()

    def spills(j, h, slot):
        return [
            pltpu.make_async_copy(r.hidb.at[slot], r.hid_o.at[j, h], r.spill.at[slot, 0]),
            pltpu.make_async_copy(r.slopeb.at[slot], r.slope_o.at[j, h], r.spill.at[slot, 1]),
            pltpu.make_async_copy(r.probb.at[slot], r.prob_o.at[j, h], r.spill.at[slot, 2]),
        ]

    def slab_step(j, carry):
        @pl.when(j == 1)
        def _():
            moves["x1"].wait_recv()

        @pl.when(j == 2)
        def _():
            moves["x2"].wait_recv()
            moves["x3"].start()
            moves["o2"].start()
            moves["o1"].start()

        @pl.when(j == 3)
        def _():
            moves["x3"].wait_recv()

        scaled, _ = standardize(r.xs[j].astype(F32))
        low = (scaled * r.gain1[...] + r.bias1[...]).astype(BF16)
        r.n1[...] = low
        r.n1t[j] = low.T
        r.valt[j] = mm(r.vt[...], r.n1t[j]).astype(BF16)

        def head_step(h, carry):
            turn = j * heads + h
            slot = turn % 2

            @pl.when(j == 0)
            def _():
                pltpu.make_async_copy(r.f1.at[h], r.f1v.at[h], r.load.at[1 + 2 * h]).wait()
                pltpu.make_async_copy(r.f2.at[h], r.f2v.at[h], r.load.at[2 + 2 * h]).wait()

            @pl.when(turn >= 2)
            def _():
                for copy in spills(j, h, slot):
                    copy.wait()

            first = jnp.bitwise_xor(me, j) * blocks
            column = lax.broadcasted_iota(jnp.int32, (BLOCK, longest), 1)
            zero = jnp.zeros((BLOCK, BLOCK), F32)
            for c in range(2):
                part = slice(c * half, (c + 1) * half)
                gated, slope = silu_and_slope(mm(r.n1[part], r.f1v[h]) + r.f1b[h])
                hidden = gated.astype(BF16)
                r.hidb[slot, part] = hidden
                r.slopeb[slot, part] = slope.astype(BF16)
                scores = mm(hidden, r.f2v[h]) + r.f2b[h]
                for i in range(half // BLOCK):
                    b = c * (half // BLOCK) + i
                    length = r.lens[first + b]
                    own = scores[i * BLOCK : (i + 1) * BLOCK]
                    keep = column < length
                    top = jnp.max(jnp.where(keep, own, -3.0e38), -1, keepdims=True)
                    exp_val = jnp.where(keep, jnp.exp(own - top), 0.0)
                    prob = exp_val * (1.0 / jnp.sum(exp_val, -1, keepdims=True))
                    for k, cell in split_prob(cells(prob), length, longest, b, zero):
                        r.probb[
                            slot, b * BLOCK : (b + 1) * BLOCK, k * BLOCK : (k + 1) * BLOCK
                        ] = cell.astype(BF16)
            own_rows = pl.ds(pl.multiple_of(h * dim, dim), dim)
            r.mixt[j, own_rows] = mm_nt(r.valt[j, own_rows], r.probb[slot]).astype(BF16)
            for copy in spills(j, h, slot):
                copy.start()
            return carry

        lax.fori_loop(0, heads, head_step, 0)
        for k in range(1, slabs):

            @pl.when(j == k)
            def _(k=k):
                moves[f"m{k}"].start()

        return carry

    lax.fori_loop(0, slabs, slab_step, 0)
    stores = [
        pltpu.make_async_copy(r.xs, r.xs_o, r.store.at[0]),
        pltpu.make_async_copy(r.n1t, r.n1t_o, r.store.at[1]),
        pltpu.make_async_copy(r.valt, r.valt_o, r.store.at[2]),
    ]
    for copy in stores:
        copy.start()
    r.attt[my_rows] = r.mixt[0]
    moves["o2"].wait_recv()
    moves["o3"].start()
    for copy in late:
        copy.wait()
    for j in range(1, slabs):
        moves[f"m{j}"].wait_recv()

    for c in range(2):
        part = slice(c * half, (c + 1) * half)
        residual = r.xs[0, part].astype(F32) + mm_tn(r.attt[:, part], r.owv[...])
        r.res[part] = residual
        scaled, _ = standardize(residual)
        r.n2s[0, part] = (scaled * r.gain2[...] + r.bias2[...]).astype(BF16)
        moves[f"n2{c}"].start()
        moves[f"n1{c}"].start()

    stores.pop(0).wait()
    moves.pop("x3").wait_send()

    def ffn_step(u, carry):
        v = u - 4
        j = jnp.where(u < 4, u // 2, 2 + v % 2)
        c = jnp.where(u < 4, u % 2, v // 2)

        @pl.when(u == 2)
        def _():
            moves["n10"].wait_recv()
            moves["o1"].wait_recv()

        @pl.when(u == 3)
        def _():
            moves["n11"].wait_recv()

        @pl.when(u == 4)
        def _():
            moves["n20"].wait_recv()
            moves["n30"].start()

        @pl.when(u == 5)
        def _():
            moves["o3"].wait_recv()
            moves["n30"].wait_recv()

        @pl.when(u == 6)
        def _():
            moves["n21"].wait_recv()
            moves["n31"].start()

        @pl.when(u == 7)
        def _():
            moves["n31"].wait_recv()

        part = pl.ds(pl.multiple_of(c * half, half), half)
        gated, slope = silu_and_slope(mm(r.n2s[j, part], r.upv[...]) + r.upb[...])
        act = gated.astype(BF16)
        r.act[j, part] = act
        pug = (mm_nt(r.ogs[j, part], r.downv[...]) * slope).astype(BF16)
        r.pug[j, part] = pug
        r.terms[j, part] = mm_nt(pug, r.upv[...]).astype(BF16)
        r.fterms[j, part] = mm(act, r.downv[...]).astype(BF16)

        @pl.when(u == 3)
        def _():
            moves["t1"].start()

        @pl.when(u == 5)
        def _():
            moves["t30"].start()

        @pl.when(u == 6)
        def _():
            moves["t30"].wait_recv()
            r.crossb[0:half] = add_low(r.terms[2, 0:half], r.near3[0:half])
            moves["c0"].start()

        @pl.when(u == 7)
        def _():
            moves["t31"].start()

        return carry

    lax.fori_loop(0, 8, ffn_step, 0)
    flat = (slabs * rows, width)
    units = r.act.shape[2]
    r.upb_sum[...] = jnp.sum(r.pug[...].reshape(flat).astype(F32), 0, keepdims=True)
    moves["t31"].wait_recv()
    r.crossb[half:] = add_low(r.terms[2, half:], r.near3[half:])
    moves["c1"].start()
    r.acc[...] = mm_tn(r.ogs[...].reshape(flat), r.act[...].reshape(flat))
    store_shards(r.fkeep, r.fsend, slice(0, units), r.acc)
    r.acc[...] = mm_tn(r.n2s[...].reshape(flat), r.pug[...].reshape(flat))
    store_shards(r.fkeep, r.fsend, slice(units, 2 * units), r.acc)
    more = [
        pltpu.make_async_copy(r.fkeep, r.fkeep_o, r.store.at[3]),
        pltpu.make_async_copy(r.fsend, r.fsend_o, r.store.at[4]),
        pltpu.make_async_copy(r.fterms, r.f_o, r.store.at[5]),
        pltpu.make_async_copy(r.res, r.res_o, r.store.at[6]),
    ]
    for copy in more:
        copy.start()
    stores += more
    cot = r.ogs[0].astype(F32)
    r.sums[2:3] = jnp.sum(cot, 0, keepdims=True)
    moves["t1"].wait_recv()
    moves["c0"].wait_recv()
    moves["c1"].wait_recv()

    grad = r.terms[0].astype(F32) + r.near1[...].astype(F32) + r.crossr[...].astype(F32)
    scaled, inv_std = standardize(r.res[...])
    res_grad = cot + norm_back(grad, scaled, inv_std, r.gain2[...])
    r.rg_o[...] = res_grad
    r.low[...] = res_grad.astype(BF16)
    r.sums[0:1] = jnp.sum(grad * scaled, 0, keepdims=True)
    r.sums[1:2] = jnp.sum(grad, 0, keepdims=True)
    r.mgt[...] = mm_nt(r.owv[...], r.low[...]).astype(BF16)
    for j in (2, 3, 1):
        moves[f"g{j}"].start()
    r.mgts[0] = r.mgt[my_rows]
    r.acc[...] = mm(r.attt[...], r.low[...])
    store_shards(r.okeep, r.osend, slice(None), r.acc)
    more = [
        pltpu.make_async_copy(r.okeep, r.okeep_o, r.store.at[7]),
        pltpu.make_async_copy(r.osend, r.osend_o, r.store.at[8]),
    ]
    for copy in more:
        copy.start()
    stores += more
    for j in range(1, slabs):
        moves[f"g{j}"].wait_recv()
    last = pltpu.make_async_copy(r.mgts, r.mgt_o, r.store.at[9])
    last.start()
    for copy in stores + [last]:
        copy.wait()
    total = slabs * heads
    for turn in (total - 2, total - 1):
        for copy in spills(turn // heads, turn % heads, turn % 2):
            copy.wait()
    for move in moves.values():
        move.wait_send()


def front(lens, x, og, gain1, bias1, f1b, f2b, vt, gain2, bias2, upb, f1, f2, ow, up, down):
    rows, width = x.shape
    heads, _, longest = f2.shape
    depth = vt.shape[0]
    units = up.shape[1]
    slabs = lax.axis_size("head")
    fsh, osh = shard_shape(width, 2 * units), shard_shape(width, width)
    group = (slabs, rows, width)
    anywhere = pl.BlockSpec(memory_space=pl.ANY)
    vmem = pl.BlockSpec(memory_space=pltpu.VMEM)
    low = lambda *s: jax.ShapeDtypeStruct(s, BF16)
    wide = lambda *s: jax.ShapeDtypeStruct(s, F32)
    out_shape = [
        low(*group),
        low(slabs, width, rows),
        low(slabs, heads, rows, width),
        low(slabs, heads, rows, width),
        low(slabs, heads, rows, longest),
        low(slabs, depth, rows),
        low(slabs, depth, rows),
        low(*group),
        wide(rows, width),
        wide(rows, width),
        fsh,
        fsh,
        osh,
        osh,
        wide(1, units),
        wide(3, width),
    ]
    out_specs = [vmem if n in ("rg_o", "upb_sum", "sums") else anywhere for n in FRONT_OUT]
    vl = lambda *s: pltpu.VMEM(s, BF16)
    vw = lambda *s: pltpu.VMEM(s, F32)
    scratch = dict(
        xs=vl(*group),
        n1=vl(rows, width),
        n1t=vl(slabs, width, rows),
        f1v=vl(heads, width, width),
        f2v=vl(heads, width, longest),
        hidb=vl(2, rows, width),
        slopeb=vl(2, rows, width),
        probb=vl(2, rows, longest),
        valt=vl(slabs, depth, rows),
        mixt=vl(slabs, depth, rows),
        attt=vl(width, rows),
        owv=vl(width, width),
        upv=vl(width, units),
        downv=vl(units, width),
        ogs=vl(*group),
        n2s=vl(*group),
        act=vl(slabs, rows, units),
        pug=vl(slabs, rows, units),
        near1=vl(rows, width),
        near3=vl(rows, width),
        crossb=vl(rows, width),
        crossr=vl(rows, width),
        fterms=vl(*group),
        res=vw(rows, width),
        low=vl(rows, width),
        mgt=vl(width, rows),
        mgts=vl(slabs, depth, rows),
        acc=vw(width, width),
        fkeep=vl(*fsh.shape),
        fsend=vl(*fsh.shape),
        okeep=vl(*osh.shape),
        osend=vl(*osh.shape),
        send=pltpu.SemaphoreType.DMA((23,)),
        recv=pltpu.SemaphoreType.DMA((23,)),
        load=pltpu.SemaphoreType.DMA((5 + 2 * heads,)),
        spill=pltpu.SemaphoreType.DMA((2, 3)),
        store=pltpu.SemaphoreType.DMA((10,)),
    )
    smem = pl.BlockSpec(memory_space=pltpu.SMEM)
    return pl.pallas_call(
        front_kernel,
        out_shape=out_shape,
        in_specs=[smem] + [anywhere] * 2 + [vmem] * 8 + [anywhere] * 5,
        out_specs=out_specs,
        scratch_shapes=[scratch[n] for n in FRONT_SCRATCH],
        compiler_params=pltpu.CompilerParams(
            collective_id=0, has_side_effects=True, vmem_limit_bytes=FRONT_LIMIT
        ),
        cost_estimate=cost(
            slabs * rows * width * (heads * (width + longest) + 6 * units), 60 << 20
        ),
        name="front",
    )(lens, x, og, gain1, bias1, f1b, f2b, vt, gain2, bias2, upb, f1, f2, ow, up, down)


def head_back_kernel(
    lens_ref,
    prob_ref,
    valt_ref,
    mgt_ref,
    hid_ref,
    slope_ref,
    n1t_ref,
    f2_ref,
    pog_ref,
    vgt_ref,
    f1b_ref,
    f2b_ref,
    keep_ref,
    send_ref,
    sg_ref,
    f1_acc,
    f2_acc,
    value_acc,
):
    j = pl.program_id(0)
    rows, longest = prob_ref.shape[-2:]
    blocks = longest // BLOCK

    @pl.when(j == 0)
    def _():
        f1_acc[...] = jnp.zeros_like(f1_acc)
        f2_acc[...] = jnp.zeros_like(f2_acc)
        value_acc[...] = jnp.zeros_like(value_acc)
        f1b_ref[...] = jnp.zeros_like(f1b_ref)
        f2b_ref[...] = jnp.zeros_like(f2b_ref)

    prob_low = prob_ref[0, 0]
    mgt = mgt_ref[0]
    vgt = mm(mgt, prob_low).astype(BF16)
    vgt_ref[0] = vgt
    probs_grad = mm_tn(mgt, valt_ref[0])
    first = jnp.bitwise_xor(lax.axis_index("head"), j) * blocks
    for b in range(rows // BLOCK):
        length = lens_ref[first + b]
        own = slice(b * BLOCK, (b + 1) * BLOCK)
        prob = prob_low[own].astype(F32)
        grad = probs_grad[own]
        inner = jnp.sum(prob * grad, -1, keepdims=True)
        spread_grad = prob * (grad - inner)
        parts = [spread_grad[:, c * BLOCK : (c + 1) * BLOCK] for c in range(blocks)]
        zero = jnp.zeros((BLOCK, BLOCK), F32)
        is_full = length == longest
        is_half = length == longest // 2
        for c in range(blocks):
            half = parts[2 * (b // 2) + c] if c < 2 else zero
            quarter = parts[b] if c == 0 else zero
            cell = jnp.where(is_full, parts[c], jnp.where(is_half, half, quarter))
            sg_ref[own, c * BLOCK : (c + 1) * BLOCK] = cell.astype(BF16)
    scores_grad = sg_ref[...]
    f2b_ref[...] += jnp.sum(scores_grad.astype(F32), 0, keepdims=True)
    hidden_grad = mm_nt(scores_grad, f2_ref[0])
    pog = (hidden_grad * slope_ref[0, 0].astype(F32)).astype(BF16)
    pog_ref[0] = pog
    f1b_ref[...] += jnp.sum(pog.astype(F32), 0, keepdims=True)
    f2_acc[...] += mm_tn(hid_ref[0, 0], scores_grad)
    n1t = n1t_ref[0]
    f1_acc[...] += mm(n1t, pog)
    value_acc[...] += mm_nt(n1t, vgt)

    @pl.when(j == pl.num_programs(0) - 1)
    def _():
        width = f1_acc.shape[1]
        dim = value_acc.shape[1]
        store_shards(keep_ref, send_ref, slice(0, width), f1_acc)
        store_shards(keep_ref, send_ref, slice(width, width + longest), f2_acc)
        store_shards(
            keep_ref, send_ref, slice(width + longest, width + longest + dim), value_acc
        )


def head_back(h, seq_len, prob, valt, mgt, hid, slope, n1t, f2):
    slabs, heads, rows, longest = prob.shape
    width = hid.shape[3]
    dim = valt.shape[1] // heads
    shards = shard_shape(width, width + longest + dim)
    by_head = lambda j: (j, h, 0, 0)
    by_slab = lambda j: (j, 0, 0)
    return pl.pallas_call(
        head_back_kernel,
        grid=(slabs,),
        out_shape=[
            jax.ShapeDtypeStruct((slabs, rows, width), BF16),
            jax.ShapeDtypeStruct((slabs, dim, rows), BF16),
            jax.ShapeDtypeStruct((1, width), F32),
            jax.ShapeDtypeStruct((1, longest), F32),
            shards,
            shards,
        ],
        in_specs=[
            pl.BlockSpec(memory_space=pltpu.SMEM),
            pl.BlockSpec((1, 1, rows, longest), by_head),
            pl.BlockSpec((1, dim, rows), lambda j: (j, h, 0)),
            pl.BlockSpec((1, dim, rows), lambda j: (j, h, 0)),
            pl.BlockSpec((1, 1, rows, width), by_head),
            pl.BlockSpec((1, 1, rows, width), by_head),
            pl.BlockSpec((1, width, rows), by_slab),
            pl.BlockSpec((1, width, longest), lambda j: (h, 0, 0)),
        ],
        out_specs=[
            pl.BlockSpec((1, rows, width), by_slab),
            pl.BlockSpec((1, dim, rows), by_slab),
            whole((1, width)),
            whole((1, longest)),
            whole(shards.shape),
            whole(shards.shape),
        ],
        scratch_shapes=[
            pltpu.VMEM((rows, longest), BF16),
            pltpu.VMEM((width, width), F32),
            pltpu.VMEM((width, longest), F32),
            pltpu.VMEM((width, dim), F32),
        ],
        compiler_params=params(),
        cost_estimate=cost(slabs * rows * width * (width + 2 * longest + 256), 20 << 20),
        name="head_back",
    )(seq_len, prob, valt, mgt, hid, slope, n1t, f2)


def input_term_kernel(heads, *refs):
    pogs, vgts = refs[:heads], refs[heads : 2 * heads]
    f1_ref, vt_ref, x_ref, sums_in, out_ref, sums_ref = refs[2 * heads :]
    term = mm_nt(pogs[0][0], f1_ref[0])
    for h in range(1, heads):
        term += mm_nt(pogs[h][0], f1_ref[h])
    for h in range(heads):
        term += mm_tn(vgts[h][0], vt_ref[h])
    low = term.astype(BF16)
    out_ref[...] = low
    wide = low.astype(F32)
    scaled, _ = standardize(x_ref[...].astype(F32))
    sums_ref[0:1, :] = sums_in[0:1, :] + jnp.sum(wide * scaled, 0, keepdims=True)
    sums_ref[1:2, :] = sums_in[1:2, :] + jnp.sum(wide, 0, keepdims=True)


def input_term(j, pogs, vgts, f1, vt, x, sums):
    heads = len(pogs)
    slabs, rows, width = pogs[0].shape
    dim = vgts[0].shape[1]
    slab = lambda _: (j, 0, 0)
    return pl.pallas_call(
        functools.partial(input_term_kernel, heads),
        grid=(1,),
        out_shape=[
            jax.ShapeDtypeStruct((rows, width), BF16),
            jax.ShapeDtypeStruct((2, width), F32),
        ],
        in_specs=[pl.BlockSpec((1, rows, width), slab)] * heads
        + [pl.BlockSpec((1, dim, rows), slab)] * heads
        + [whole(f1.shape), whole(vt.shape), whole((rows, width)), whole((2, width))],
        out_specs=[whole((rows, width)), whole((2, width))],
        compiler_params=params(),
        cost_estimate=cost(heads * rows * width * (width + 256), 8 << 20),
        name="input_term",
    )(*pogs, *vgts, f1, vt, x, sums)


def input_back_kernel(t0_ref, t1_ref, t2_ref, x_ref, rg_ref, gain_ref, out_ref):
    grad = t0_ref[...].astype(F32) + t1_ref[...].astype(F32) + t2_ref[...].astype(F32)
    scaled, inv_std = standardize(x_ref[...].astype(F32))
    out_ref[...] = rg_ref[...] + norm_back(grad, scaled, inv_std, gain_ref[...])


def input_back(terms, x, res_grad, gain):
    return pl.pallas_call(
        input_back_kernel,
        out_shape=jax.ShapeDtypeStruct(res_grad.shape, F32),
        compiler_params=pltpu.CompilerParams(vmem_limit_bytes=VMEM_LIMIT),
        cost_estimate=cost(0, 7 << 20),
        name="input_back",
    )(*terms, x, res_grad, gain)


def scatter_terms(terms):
    cross = swap(add_low(terms[2], swap(terms[3], "head", 1)), "head", 2)
    return [terms[0], swap(terms[1], "head", 1), cross]


def reduce_over_dp(keep, send):
    both = keep.astype(F32) + swap(send, "dp", 1).astype(F32)
    total = both[0]
    low = both.astype(BF16)
    for k in range(1, keep.shape[0]):
        total = total + swap(low[k], "dp", 2 * k).astype(F32)
    return total


def local(
    tokens,
    seq_len,
    norm1_gain,
    norm1_bias,
    f1_weight,
    f1_bias,
    f2_weight,
    f2_bias,
    value_weight,
    out_weight,
    norm2_gain,
    norm2_bias,
    up_weight,
    up_bias,
    down_weight,
    down_bias,
    out_grad,
):
    members = lax.axis_size("head")
    heads, width, longest = f2_weight.shape
    units = up_weight.shape[1]
    dim = value_weight.shape[1] // heads
    row = lambda v: v.reshape(1, -1)
    vt = value_weight.T.reshape(heads, dim, width)
    f1b = f1_bias.reshape(heads, 1, width)
    f2b = f2_bias.reshape(heads, 1, longest)

    (
        xs,
        n1t,
        hid,
        slope,
        prob,
        valt,
        mgt,
        ffn_out,
        res_grad,
        residual,
        ffn_keep,
        ffn_send,
        out_keep,
        out_send,
        upb,
        sums2,
    ) = front(
        seq_len,
        tokens,
        out_grad,
        row(norm1_gain),
        row(norm1_bias),
        f1b,
        f2b,
        vt.reshape(heads * dim, width),
        row(norm2_gain),
        row(norm2_bias),
        row(up_bias),
        f1_weight,
        f2_weight,
        out_weight,
        up_weight,
        down_weight,
    )
    ffn_terms = scatter_terms([ffn_out[j] for j in range(members)])
    result = residual + sum(t.astype(F32) for t in ffn_terms) + down_bias

    backs = [
        head_back(h, seq_len, prob, valt, mgt, hid, slope, n1t, f2_weight) for h in range(heads)
    ]
    pogs, vgts, f1bg, f2bg, head_keep, head_send = zip(*backs)
    sums1 = jnp.zeros((2, width), F32)
    terms = [None] * members
    for j in reversed(range(members)):
        terms[j], sums1 = input_term(j, pogs, vgts, f1_weight, vt, xs[j], sums1)
    input_grad = input_back(scatter_terms(terms), tokens, res_grad, row(norm1_gain))

    ffn_total = reduce_over_dp(ffn_keep, ffn_send)
    out_total = reduce_over_dp(out_keep, out_send)
    head_totals = [reduce_over_dp(k, s) for k, s in zip(head_keep, head_send)]
    low = out_total.astype(BF16)
    low = add_low(low, swap(low, "head", 1))
    out_piece = low.astype(F32) + swap(low, "head", 2).astype(F32)

    own = jnp.concatenate(
        [v.reshape(-1) for v in f1bg] + [v.reshape(-1) for v in f2bg] + [upb.reshape(-1)]
    )
    shared = jnp.concatenate([sums1.reshape(-1), sums2.reshape(-1)])
    split = own.shape[0]
    vec = jnp.concatenate([own, shared]).reshape(-1, 128)
    step = 1
    while step < lax.axis_size("dp"):
        vec = vec + swap(vec, "dp", step)
        step *= 2
    flat = vec.reshape(-1)
    own, shared = flat[:split].reshape(1, -1), flat[split:]
    step = 1
    while step < members:
        got = swap(jnp.concatenate([own.reshape(-1), shared]).reshape(-1, 128), "head", step)
        got = got.reshape(-1)
        shared = shared + got[own.size :]
        own = jnp.concatenate([own, got[: own.size].reshape(own.shape)])
        step *= 2
    order = jnp.bitwise_xor(jnp.arange(members), lax.axis_index("head"))
    own = own[order]
    f1b_all = own[:, : heads * width].reshape(members * heads, width)
    f2b_all = own[:, heads * width : heads * (width + longest)].reshape(members * heads, longest)
    upb_all = own[:, heads * (width + longest) :].reshape(members * units)
    shared = shared.reshape(5, width)

    f1_piece = jnp.stack([t[:, :width] for t in head_totals])
    f2_piece = jnp.stack([t[:, width : width + longest] for t in head_totals])
    value_piece = jnp.concatenate([t[:, width + longest :] for t in head_totals], 1)
    return (
        result,
        input_grad,
        shared[0],
        shared[1],
        f1_piece,
        f1b_all,
        f2_piece,
        f2b_all,
        value_piece,
        out_piece,
        shared[2],
        shared[3],
        ffn_total[:, units:],
        upb_all,
        ffn_total[:, :units].T,
        shared[4],
    )


def solution(mesh):
    placed = (
        P(("dp", "head"), None),
        P("dp"),
        P(),
        P(),
        P("head", None, None),
        P("head", None),
        P("head", None, None),
        P("head", None),
        P(None, "head"),
        P(),
        P(),
        P(),
        P(None, "head"),
        P("head"),
        P("head", None),
        P(),
        P(("dp", "head"), None),
    )
    return jax.shard_map(
        local,
        mesh=mesh,
        in_specs=placed,
        out_specs=(
            P(("dp", "head"), None),
            P(("dp", "head"), None),
            P(),
            P(),
            P("head", "dp", None),
            P(),
            P("head", "dp", None),
            P(),
            P("dp", "head"),
            P("dp", None),
            P(),
            P(),
            P("dp", "head"),
            P(),
            P("head", "dp"),
            P(),
        ),
        check_vma=False,
    )
```

```python
import types

import jax
import jax.numpy as jnp
from jax import lax
from jax.experimental import pallas as pl
from jax.experimental.pallas import tpu as pltpu
from jax.sharding import PartitionSpec as P

F32 = jnp.float32
BF16 = jnp.bfloat16
BLOCK = 128
VMEM_LIMIT = 50 << 20
FUSED_LIMIT = 62 << 20


def mm(a, b):
    return lax.dot_general(a, b, (((1,), (0,)), ((), ())), preferred_element_type=F32)


def mm_nt(a, b):
    return lax.dot_general(a, b, (((1,), (1,)), ((), ())), preferred_element_type=F32)


def mm_tn(a, b):
    return lax.dot_general(a, b, (((0,), (0,)), ((), ())), preferred_element_type=F32)


def standardize(values):
    centred = values - jnp.mean(values, -1, keepdims=True)
    inv_std = lax.rsqrt(jnp.mean(centred * centred, -1, keepdims=True) + 1e-05)
    return centred * inv_std, inv_std


def norm_back(grad_out, scaled, inv_std, gain):
    grad_scaled = grad_out * gain
    centre_mean = jnp.mean(grad_scaled, -1, keepdims=True)
    cross_mean = jnp.mean(grad_scaled * scaled, -1, keepdims=True)
    return inv_std * (grad_scaled - centre_mean - scaled * cross_mean)


def silu_and_slope(pre_val):
    sigma = 0.5 + 0.5 * jnp.tanh(0.5 * pre_val)
    gated = pre_val * sigma
    return gated, sigma + gated * (1.0 - sigma)


def add_low(a, b):
    return (a.astype(F32) + b.astype(F32)).astype(BF16)


def swap(value, axis, step):
    return lax.ppermute(value, axis, [(i, i ^ step) for i in range(lax.axis_size(axis))])


def cost(macs, bytes_accessed):
    return pl.CostEstimate(flops=2 * macs, bytes_accessed=bytes_accessed, transcendentals=0)


def store_shards(keep_ref, send_ref, lanes, acc_ref):
    count, depth = keep_ref.shape[:2]
    me = lax.axis_index("dp")
    pair, parity = me // 2, me % 2
    for k in range(count):
        other = jnp.bitwise_xor(pair, k) * 2
        mine = pl.multiple_of((other + parity) * depth, 8)
        theirs = pl.multiple_of((other + 1 - parity) * depth, 8)
        keep_ref[k, :, lanes] = acc_ref[pl.ds(mine, depth), :].astype(BF16)
        send_ref[k, :, lanes] = acc_ref[pl.ds(theirs, depth), :].astype(BF16)


def shard_shape(width, lanes):
    members = lax.axis_size("dp")
    return jax.ShapeDtypeStruct((members // 2, width // members, lanes), BF16)


class Wires:
    def __init__(self, send, recv):
        self.send, self.recv, self.used = send, recv, 0
        self.all = []

    def remote(self, src, dst, axis, step):
        index = self.used
        self.used += 1
        move = pltpu.make_async_remote_copy(
            src_ref=src,
            dst_ref=dst,
            send_sem=self.send.at[index],
            recv_sem=self.recv.at[index],
            device_id={axis: jnp.bitwise_xor(lax.axis_index(axis), step)},
            device_id_type=pl.DeviceIdType.MESH,
        )
        self.all.append(move)
        return move


class Shards:
    def __init__(self, wires, keep, send, got, out, local_sem):
        self.keep, self.got, self.out = keep, got, out
        self.count = keep.shape[0]
        self.first = wires.remote(send, got, "dp", 1)
        self.rest = [
            wires.remote(keep.at[k], out.at[k], "dp", 2 * k) for k in range(1, self.count)
        ]
        self.own = pltpu.make_async_copy(keep.at[0], out.at[0], local_sem)

    def start(self):
        self.first.start()

    def second(self):
        self.first.wait_recv()
        for k in list(range(1, self.count)) + [0]:
            self.keep[k] = add_low(self.keep[k], self.got[k])
            (self.rest[k - 1] if k else self.own).start()

    def finish(self):
        for move in self.rest:
            move.wait_recv()
        self.own.wait()


def greet(axes):
    barrier = pltpu.get_barrier_semaphore()
    for axis, step in axes:
        pl.semaphore_signal(
            barrier,
            1,
            device_id={axis: jnp.bitwise_xor(lax.axis_index(axis), step)},
            device_id_type=pl.DeviceIdType.MESH,
        )
    pl.semaphore_wait(barrier, len(axes))


def partners():
    over_dp = [1] + list(range(2, lax.axis_size("dp"), 2))
    return [("head", s) for s in range(1, lax.axis_size("head"))] + [("dp", s) for s in over_dp]


FRONT_IN = (
    "lens", "x", "og", "vecs", "f1b", "f2b", "vt", "f1", "f2",
    "ow", "up", "down",
)
FRONT_OUT = (
    "xs_o", "n1t_o", "hid_o", "slope_o", "prob_o", "valt_o", "mgt_o", "f_o", "rg_o", "res_o",
    "down_o", "up_o", "okeep_o", "osend_o", "upb_sum", "sums",
)
FRONT_SCRATCH = (
    "xs", "n1", "n1t", "f1v", "f2v", "hidb", "slopeb", "probb", "valt", "mixt", "attt", "owv",
    "upv", "downv", "ogs", "n2s", "act", "pug", "near1", "near3", "crossb", "crossr",
    "fterms", "res", "low", "mgt", "mgts", "acc", "dkeep", "dsend", "dgot", "ukeep", "usend", "ugot", "okeep", "osend", "send",
    "recv", "load", "spill", "store",
)


def split_prob(parts, length, longest, b, zero):
    is_full = length == longest
    is_half = length == longest // 2
    for c in range(len(parts)):
        half = parts[c % 2] if c // 2 == b // 2 else zero
        quarter = parts[0] if c == b else zero
        yield c, jnp.where(is_full, parts[c], jnp.where(is_half, half, quarter))


def cells(row):
    return [row[:, c : c + BLOCK] for c in range(0, row.shape[1], BLOCK)]


def front_kernel(*refs):
    r = types.SimpleNamespace(**dict(zip(FRONT_IN + FRONT_OUT + FRONT_SCRATCH, refs)))
    r.terms = r.xs
    slabs, rows, width = r.xs.shape
    heads, _, longest = r.f2v.shape
    depth = r.mixt.shape[1]
    dim = depth // heads
    half = rows // 2
    blocks = rows // BLOCK
    me = lax.axis_index("head")

    w = Wires(r.send, r.recv)
    down_group = Shards(w, r.dkeep, r.dsend, r.dgot, r.down_o, r.store.at[3])
    up_group = Shards(w, r.ukeep, r.usend, r.ugot, r.up_o, r.store.at[4])

    def remote(src, dst, step):
        return w.remote(src, dst, "head", step)

    def cut(c):
        return pl.ds(c * half, half)

    my_rows = pl.ds(pl.multiple_of(me * depth, depth), depth)
    moves = {
        "x1": remote(r.x, r.xs.at[1], 1),
        "x2": remote(r.x, r.xs.at[2], 2),
        "x3": remote(r.xs.at[2], r.xs.at[3], 1),
        "o1": remote(r.og, r.ogs.at[1], 1),
        "o2": remote(r.og, r.ogs.at[2], 2),
        "o3": remote(r.ogs.at[2], r.ogs.at[3], 1),
        "t1": remote(r.terms.at[1], r.near1, 1),
    }
    for j in range(1, slabs):
        moves[f"m{j}"] = remote(r.mixt.at[j], r.attt.at[my_rows], j)
        piece = pl.ds(pl.multiple_of(jnp.bitwise_xor(me, j) * depth, depth), depth)
        moves[f"g{j}"] = remote(r.mgt.at[piece], r.mgts.at[j], j)
    for c in range(2):
        part = cut(c)
        moves[f"n1{c}"] = remote(r.n2s.at[0, part], r.n2s.at[1, part], 1)
        moves[f"n2{c}"] = remote(r.n2s.at[0, part], r.n2s.at[2, part], 2)
        moves[f"n3{c}"] = remote(r.n2s.at[2, part], r.n2s.at[3, part], 1)
        moves[f"t3{c}"] = remote(r.terms.at[3, part], r.near3.at[part], 1)
        moves[f"c{c}"] = remote(r.crossb.at[part], r.crossr.at[part], 2)

    loads = [pltpu.make_async_copy(r.x, r.xs.at[0], r.load.at[0])]
    for h in range(heads):
        loads.append(pltpu.make_async_copy(r.f1.at[h], r.f1v.at[h], r.load.at[1 + 2 * h]))
        loads.append(pltpu.make_async_copy(r.f2.at[h], r.f2v.at[h], r.load.at[2 + 2 * h]))
    base = 1 + 2 * heads
    late = [
        pltpu.make_async_copy(r.ow, r.owv, r.load.at[base]),
        pltpu.make_async_copy(r.up, r.upv, r.load.at[base + 1]),
        pltpu.make_async_copy(r.down, r.downv, r.load.at[base + 2]),
        pltpu.make_async_copy(r.og, r.ogs.at[0], r.load.at[base + 3]),
    ]
    for copy in loads:
        copy.start()
    greet(partners())
    moves["x2"].start()
    moves["x1"].start()
    for copy in late:
        copy.start()
    loads[0].wait()

    def spills(j, h, slot):
        return [
            pltpu.make_async_copy(r.hidb.at[slot], r.hid_o.at[j, h], r.spill.at[slot, 0]),
            pltpu.make_async_copy(r.slopeb.at[slot], r.slope_o.at[j, h], r.spill.at[slot, 1]),
            pltpu.make_async_copy(r.probb.at[slot], r.prob_o.at[j, h], r.spill.at[slot, 2]),
        ]

    def slab_step(j, carry):
        @pl.when(j == 1)
        def _():
            moves["x1"].wait_recv()

        @pl.when(j == 2)
        def _():
            moves["x2"].wait_recv()
            moves["x3"].start()
            moves["o2"].start()
            moves["o1"].start()

        @pl.when(j == 3)
        def _():
            moves["x3"].wait_recv()

        scaled, _ = standardize(r.xs[j].astype(F32))
        low = (scaled * r.vecs[0:1] + r.vecs[1:2]).astype(BF16)
        r.n1[...] = low
        r.n1t[j] = low.T
        r.valt[j] = mm(r.vt[...], r.n1t[j]).astype(BF16)

        def head_step(h, carry):
            turn = j * heads + h
            slot = turn % 2

            @pl.when(j == 0)
            def _():
                pltpu.make_async_copy(r.f1.at[h], r.f1v.at[h], r.load.at[1 + 2 * h]).wait()
                pltpu.make_async_copy(r.f2.at[h], r.f2v.at[h], r.load.at[2 + 2 * h]).wait()

            @pl.when(turn >= 2)
            def _():
                for copy in spills(j, h, slot):
                    copy.wait()

            first = jnp.bitwise_xor(me, j) * blocks
            column = lax.broadcasted_iota(jnp.int32, (BLOCK, longest), 1)
            zero = jnp.zeros((BLOCK, BLOCK), F32)
            for c in range(2):
                part = slice(c * half, (c + 1) * half)
                gated, slope = silu_and_slope(mm(r.n1[part], r.f1v[h]) + r.f1b[pl.ds(h, 1)])
                hidden = gated.astype(BF16)
                r.hidb[slot, part] = hidden
                r.slopeb[slot, part] = slope.astype(BF16)
                scores = mm(hidden, r.f2v[h]) + r.f2b[pl.ds(h, 1)]
                for i in range(half // BLOCK):
                    b = c * (half // BLOCK) + i
                    length = r.lens[first + b]
                    own = scores[i * BLOCK : (i + 1) * BLOCK]
                    keep = column < length
                    top = jnp.max(jnp.where(keep, own, -3.0e38), -1, keepdims=True)
                    exp_val = jnp.where(keep, jnp.exp(own - top), 0.0)
                    prob = exp_val * (1.0 / jnp.sum(exp_val, -1, keepdims=True))
                    for k, cell in split_prob(cells(prob), length, longest, b, zero):
                        r.probb[
                            slot, b * BLOCK : (b + 1) * BLOCK, k * BLOCK : (k + 1) * BLOCK
                        ] = cell.astype(BF16)
            own_rows = pl.ds(pl.multiple_of(h * dim, dim), dim)
            r.mixt[j, own_rows] = mm_nt(r.valt[j, own_rows], r.probb[slot]).astype(BF16)
            for copy in spills(j, h, slot):
                copy.start()
            return carry

        lax.fori_loop(0, heads, head_step, 0)
        for k in range(1, slabs):

            @pl.when(j == k)
            def _(k=k):
                moves[f"m{k}"].start()

        return carry

    lax.fori_loop(0, slabs, slab_step, 0)
    stores = [
        pltpu.make_async_copy(r.xs, r.xs_o, r.store.at[0]),
        pltpu.make_async_copy(r.n1t, r.n1t_o, r.store.at[1]),
        pltpu.make_async_copy(r.valt, r.valt_o, r.store.at[2]),
    ]
    for copy in stores:
        copy.start()
    r.attt[my_rows] = r.mixt[0]
    moves["o2"].wait_recv()
    moves["o3"].start()
    for copy in late:
        copy.wait()
    for j in range(1, slabs):
        moves[f"m{j}"].wait_recv()

    for c in range(2):
        part = slice(c * half, (c + 1) * half)
        residual = r.xs[0, part].astype(F32) + mm_tn(r.attt[:, part], r.owv[...])
        r.res[part] = residual
        scaled, _ = standardize(residual)
        r.n2s[0, part] = (scaled * r.vecs[2:3] + r.vecs[3:4]).astype(BF16)
        moves[f"n2{c}"].start()
        moves[f"n1{c}"].start()

    stores.pop(0).wait()
    sent = moves["x3"]
    sent.wait_send()

    def ffn_step(u, carry):
        v = u - 4
        j = jnp.where(u < 4, u // 2, 2 + v % 2)
        c = jnp.where(u < 4, u % 2, v // 2)

        @pl.when(u == 2)
        def _():
            moves["n10"].wait_recv()
            moves["o1"].wait_recv()

        @pl.when(u == 3)
        def _():
            moves["n11"].wait_recv()

        @pl.when(u == 4)
        def _():
            moves["n20"].wait_recv()
            moves["n30"].start()

        @pl.when(u == 5)
        def _():
            moves["o3"].wait_recv()
            moves["n30"].wait_recv()

        @pl.when(u == 6)
        def _():
            moves["n21"].wait_recv()
            moves["n31"].start()

        @pl.when(u == 7)
        def _():
            moves["n31"].wait_recv()

        part = pl.ds(pl.multiple_of(c * half, half), half)
        gated, slope = silu_and_slope(mm(r.n2s[j, part], r.upv[...]) + r.vecs[4:5])
        act = gated.astype(BF16)
        r.act[j, part] = act
        pug = (mm_nt(r.ogs[j, part], r.downv[...]) * slope).astype(BF16)
        r.pug[j, part] = pug
        r.terms[j, part] = mm_nt(pug, r.upv[...]).astype(BF16)
        r.fterms[j, part] = mm(act, r.downv[...]).astype(BF16)

        @pl.when(u == 3)
        def _():
            moves["t1"].start()

        @pl.when(u == 5)
        def _():
            moves["t30"].start()

        @pl.when(u == 6)
        def _():
            moves["t30"].wait_recv()
            r.crossb[0:half] = add_low(r.terms[2, 0:half], r.near3[0:half])
            moves["c0"].start()

        @pl.when(u == 7)
        def _():
            moves["t31"].start()

        return carry

    lax.fori_loop(0, 8, ffn_step, 0)
    flat = (slabs * rows, width)
    units = r.act.shape[2]
    r.upb_sum[...] = jnp.sum(r.pug[...].reshape(flat).astype(F32), 0, keepdims=True)
    moves["t31"].wait_recv()
    r.crossb[half:] = add_low(r.terms[2, half:], r.near3[half:])
    moves["c1"].start()
    r.acc[...] = mm_tn(r.ogs[...].reshape(flat), r.act[...].reshape(flat))
    store_shards(r.dkeep, r.dsend, slice(None), r.acc)
    down_group.start()
    r.acc[...] = mm_tn(r.n2s[...].reshape(flat), r.pug[...].reshape(flat))
    store_shards(r.ukeep, r.usend, slice(None), r.acc)
    up_group.start()
    more = [
        pltpu.make_async_copy(r.fterms, r.f_o, r.store.at[5]),
        pltpu.make_async_copy(r.res, r.res_o, r.store.at[6]),
    ]
    for copy in more:
        copy.start()
    stores += more
    cot = r.ogs[0].astype(F32)
    r.sums[2:3] = jnp.sum(cot, 0, keepdims=True)
    moves["t1"].wait_recv()
    moves["c0"].wait_recv()
    moves["c1"].wait_recv()

    grad = r.terms[0].astype(F32) + r.near1[...].astype(F32) + r.crossr[...].astype(F32)
    scaled, inv_std = standardize(r.res[...])
    res_grad = cot + norm_back(grad, scaled, inv_std, r.vecs[2:3])
    r.rg_o[...] = res_grad
    r.low[...] = res_grad.astype(BF16)
    r.sums[0:1] = jnp.sum(grad * scaled, 0, keepdims=True)
    r.sums[1:2] = jnp.sum(grad, 0, keepdims=True)
    r.mgt[...] = mm_nt(r.owv[...], r.low[...]).astype(BF16)
    for j in (2, 3, 1):
        moves[f"g{j}"].start()
    down_group.second()
    r.mgts[0] = r.mgt[my_rows]
    r.acc[...] = mm(r.attt[...], r.low[...])
    store_shards(r.okeep, r.osend, slice(None), r.acc)
    more = [
        pltpu.make_async_copy(r.okeep, r.okeep_o, r.store.at[7]),
        pltpu.make_async_copy(r.osend, r.osend_o, r.store.at[8]),
    ]
    for copy in more:
        copy.start()
    stores += more
    for j in range(1, slabs):
        moves[f"g{j}"].wait_recv()
    last = pltpu.make_async_copy(r.mgts, r.mgt_o, r.store.at[9])
    last.start()
    up_group.second()
    down_group.finish()
    up_group.finish()
    for copy in stores + [last]:
        copy.wait()
    total = slabs * heads
    for turn in (total - 2, total - 1):
        for copy in spills(turn // heads, turn % heads, turn % 2):
            copy.wait()
    for move in w.all:
        if move is not sent:
            move.wait_send()


def front(lens, x, og, vecs, f1b, f2b, vt, f1, f2, ow, up, down):
    rows, width = x.shape
    heads, _, longest = f2.shape
    depth = vt.shape[0]
    units = up.shape[1]
    slabs = lax.axis_size("head")
    osh = shard_shape(width, width)
    dsh = shard_shape(width, units)
    group = (slabs, rows, width)
    anywhere = pl.BlockSpec(memory_space=pl.ANY)
    vmem = pl.BlockSpec(memory_space=pltpu.VMEM)
    low = lambda *s: jax.ShapeDtypeStruct(s, BF16)
    wide = lambda *s: jax.ShapeDtypeStruct(s, F32)
    out_shape = [
        low(*group),
        low(slabs, width, rows),
        low(slabs, heads, rows, width),
        low(slabs, heads, rows, width),
        low(slabs, heads, rows, longest),
        low(slabs, depth, rows),
        low(slabs, depth, rows),
        low(*group),
        wide(rows, width),
        wide(rows, width),
        dsh,
        dsh,
        osh,
        osh,
        wide(1, units),
        wide(3, width),
    ]
    out_specs = [vmem if n in ("rg_o", "upb_sum", "sums") else anywhere for n in FRONT_OUT]
    vl = lambda *s: pltpu.VMEM(s, BF16)
    vw = lambda *s: pltpu.VMEM(s, F32)
    scratch = dict(
        xs=vl(*group),
        n1=vl(rows, width),
        n1t=vl(slabs, width, rows),
        f1v=vl(heads, width, width),
        f2v=vl(heads, width, longest),
        hidb=vl(2, rows, width),
        slopeb=vl(2, rows, width),
        probb=vl(2, rows, longest),
        valt=vl(slabs, depth, rows),
        mixt=vl(slabs, depth, rows),
        attt=vl(width, rows),
        owv=vl(width, width),
        upv=vl(width, units),
        downv=vl(units, width),
        ogs=vl(*group),
        n2s=vl(*group),
        act=vl(slabs, rows, units),
        pug=vl(slabs, rows, units),
        near1=vl(rows, width),
        near3=vl(rows, width),
        crossb=vl(rows, width),
        crossr=vl(rows, width),
        fterms=vl(*group),
        res=vw(rows, width),
        low=vl(rows, width),
        mgt=vl(width, rows),
        mgts=vl(slabs, depth, rows),
        acc=vw(width, width),
        dkeep=vl(*dsh.shape),
        dsend=vl(*dsh.shape),
        dgot=vl(*dsh.shape),
        ukeep=vl(*dsh.shape),
        usend=vl(*dsh.shape),
        ugot=vl(*dsh.shape),
        okeep=vl(*osh.shape),
        osend=vl(*osh.shape),
        send=pltpu.SemaphoreType.DMA((23 + 2 * osh.shape[0],)),
        recv=pltpu.SemaphoreType.DMA((23 + 2 * osh.shape[0],)),
        load=pltpu.SemaphoreType.DMA((5 + 2 * heads,)),
        spill=pltpu.SemaphoreType.DMA((2, 3)),
        store=pltpu.SemaphoreType.DMA((10,)),
    )
    smem = pl.BlockSpec(memory_space=pltpu.SMEM)
    return pl.pallas_call(
        front_kernel,
        out_shape=out_shape,
        in_specs=[smem] + [anywhere] * 2 + [vmem] * 4 + [anywhere] * 5,
        out_specs=out_specs,
        scratch_shapes=[scratch[n] for n in FRONT_SCRATCH],
        compiler_params=pltpu.CompilerParams(
            collective_id=0, has_side_effects=True, vmem_limit_bytes=FUSED_LIMIT
        ),
        cost_estimate=cost(
            slabs * rows * width * (heads * (width + longest) + 6 * units), 60 << 20
        ),
        name="front",
    )(lens, x, og, vecs, f1b, f2b, vt, f1, f2, ow, up, down)


BACK_IN = (
    "lens", "upb_sum", "sums", "hid", "slope", "prob", "n1t", "valt", "mgt", "f1", "f2", "vt",
    "xs", "fterms", "okeep", "osend",
)
BACK_OUT = (
    "t_o", "tnear_o", "tcross_o", "fnear_o", "fcross_o", "ow_o", "f1_o", "f2_o", "val_o",
    "small_o",
)
BACK_SCRATCH = (
    "n1tv", "valtv", "mgtv", "vgt", "f1v", "f2v", "vtv", "hidb", "slopeb", "probb", "sg", "pog",
    "acc1", "acc2", "acc3", "xb", "terms", "near3", "crossb", "fb", "fnear3", "ok", "ogot",
    "akeep", "asend", "agot", "bkeep", "bsend", "bgot", "vkeep", "vsend", "vgot", "small",
    "small_y", "small_z", "send", "recv", "load", "fetch", "store",
)


def back_kernel(*refs):
    r = types.SimpleNamespace(**dict(zip(BACK_IN + BACK_OUT + BACK_SCRATCH, refs)))
    slabs, heads, rows, width = r.pog.shape
    longest = r.probb.shape[2]
    depth = r.vgt.shape[1]
    dim = depth // heads
    blocks = rows // BLOCK
    count = r.ok.shape[0]
    me = lax.axis_index("head")
    turns = slabs * heads
    w = Wires(r.send, r.recv)
    out_group = Shards(w, r.ok, r.osend, r.ogot, r.ow_o, r.store.at[0])
    f1_group = [
        Shards(w, r.akeep.at[h], r.asend.at[h], r.agot.at[h], r.f1_o.at[h], r.store.at[1 + h])
        for h in range(heads)
    ]
    f2_group = [
        Shards(
            w, r.bkeep.at[h], r.bsend.at[h], r.bgot.at[h], r.f2_o.at[h], r.store.at[1 + heads + h]
        )
        for h in range(heads)
    ]
    val_group = Shards(w, r.vkeep, r.vsend, r.vgot, r.val_o, r.store.at[1 + 2 * heads])
    fterm1 = w.remote(r.fterms.at[1], r.fnear_o, "head", 1)
    fterm3 = w.remote(r.fterms.at[3], r.fnear3, "head", 1)
    fcross = w.remote(r.fb, r.fcross_o, "head", 2)
    term1 = w.remote(r.terms.at[1], r.tnear_o, "head", 1)
    term3 = w.remote(r.terms.at[3], r.near3, "head", 1)
    cross = w.remote(r.crossb, r.tcross_o, "head", 2)
    small_y = w.remote(r.small, r.small_y, "dp", 1)
    small_z = [
        w.remote(r.small_z.at[0], r.small_z.at[k], "dp", 2 * k) for k in range(1, count)
    ]
    small_x = [
        w.remote(r.small, r.small_o.at[j], "head", j) for j in range(1, slabs)
    ]
    own_term = pltpu.make_async_copy(r.terms.at[0], r.t_o, r.store.at[2 + 2 * heads])
    own_small = pltpu.make_async_copy(r.small, r.small_o.at[0], r.store.at[3 + 2 * heads])

    def load(index, src, dst):
        return pltpu.make_async_copy(src, dst, r.load.at[index])

    loads = [
        load(0, r.mgt, r.mgtv),
        load(1, r.valt, r.valtv),
        load(2, r.f2, r.f2v),
        load(3, r.n1t, r.n1tv),
        load(4, r.okeep, r.ok),
        load(5, r.fterms.at[2], r.fb),
        load(6, r.f1, r.f1v),
        load(7, r.vt, r.vtv),
        load(8, r.xs.at[3], r.xb),
    ]

    def fetches(turn):
        h, j, slot = turn // slabs, turn % slabs, turn % 2
        return [
            pltpu.make_async_copy(r.prob.at[j, h], r.probb.at[slot], r.fetch.at[slot, 0]),
            pltpu.make_async_copy(r.slope.at[j, h], r.slopeb.at[slot], r.fetch.at[slot, 1]),
            pltpu.make_async_copy(r.hid.at[j, h], r.hidb.at[slot], r.fetch.at[slot, 2]),
        ]

    for copy in loads[:2] + fetches(0) + loads[2:]:
        copy.start()
    greet(partners())
    out_group.start()
    fterm3.start()
    fterm1.start()
    r.small[...] = jnp.zeros_like(r.small)
    r.small[2 * heads : 2 * heads + 1] = r.upb_sum[...]
    r.small[2 * heads + 3 : 2 * heads + 6] = r.sums[...]
    for copy in loads[:6]:
        copy.wait()

    def turn_step(turn, carry):
        h, j, slot = turn // slabs, turn % slabs, turn % 2
        for copy in fetches(turn):
            copy.wait()

        @pl.when(turn + 1 < turns)
        def _():
            for copy in fetches(turn + 1):
                copy.start()

        @pl.when(j == 0)
        def _():
            r.acc1[...] = jnp.zeros_like(r.acc1)
            r.acc2[...] = jnp.zeros_like(r.acc2)

        head_rows = pl.ds(pl.multiple_of(h * dim, dim), dim)
        mgt = r.mgtv[j, head_rows]
        r.vgt[j, head_rows] = mm(mgt, r.probb[slot]).astype(BF16)
        probs_grad = mm_tn(mgt, r.valtv[j, head_rows])
        first = jnp.bitwise_xor(me, j) * blocks
        zero = jnp.zeros((BLOCK, BLOCK), F32)
        for b in range(blocks):
            length = r.lens[first + b]
            own = slice(b * BLOCK, (b + 1) * BLOCK)
            prob = r.probb[slot, own].astype(F32)
            grad = probs_grad[own]
            inner = jnp.sum(prob * grad, -1, keepdims=True)
            parts = cells(prob * (grad - inner))
            is_full = length == longest
            is_half = length == longest // 2
            for c in range(blocks):
                half = parts[2 * (b // 2) + c] if c < 2 else zero
                quarter = parts[b] if c == 0 else zero
                cell = jnp.where(is_full, parts[c], jnp.where(is_half, half, quarter))
                r.sg[own, c * BLOCK : (c + 1) * BLOCK] = cell.astype(BF16)
        scores_grad = r.sg[...]
        row = pl.ds(h, 1)
        pog = (mm_nt(scores_grad, r.f2v[h]) * r.slopeb[slot].astype(F32)).astype(BF16)
        r.pog[j, h] = pog
        r.small[row] += jnp.sum(pog.astype(F32), 0, keepdims=True)
        row = pl.ds(heads + h, 1)
        r.small[row, 0:longest] += jnp.sum(scores_grad.astype(F32), 0, keepdims=True)
        r.acc2[...] += mm_tn(r.hidb[slot], scores_grad)
        r.acc1[...] += mm(r.n1tv[j], pog)

        for k in range(heads):

            @pl.when(turn == slabs * k + slabs - 1)
            def _(k=k):
                store_shards(r.bkeep.at[k], r.bsend.at[k], slice(None), r.acc2)
                if k < heads - 1:
                    f2_group[k].start()
                store_shards(r.akeep.at[k], r.asend.at[k], slice(None), r.acc1)
                if k < heads - 1:
                    f1_group[k].start()

        @pl.when(turn == 1)
        def _():
            fterm3.wait_recv()
            r.fb[...] = add_low(r.fb[...], r.fnear3[...])
            fcross.start()

        @pl.when(turn == slabs + 1)
        def _():
            out_group.second()

        return carry

    lax.fori_loop(0, turns, turn_step, 0)
    f2_group[0].second()
    f1_group[0].second()
    for copy in loads[6:]:
        copy.wait()

    def term_step(i, carry):
        j = slabs - 1 - i

        @pl.when(i > 0)
        def _():
            load(8, r.xs.at[j], r.xb).wait()

        term = mm_tn(r.vgt[j], r.vtv[...])
        for h in range(heads):
            term += mm_nt(r.pog[j, h], r.f1v[h])
        low = term.astype(BF16)
        r.terms[j] = low
        wide = low.astype(F32)
        scaled, _ = standardize(r.xb[...].astype(F32))
        base = 2 * heads + 1
        r.small[base : base + 1] += jnp.sum(wide * scaled, 0, keepdims=True)
        r.small[base + 1 : base + 2] += jnp.sum(wide, 0, keepdims=True)

        @pl.when(i < slabs - 1)
        def _():
            load(8, r.xs.at[j - 1], r.xb).start()

        @pl.when(i == 0)
        def _():
            term3.start()

        @pl.when(i == 1)
        def _():
            term3.wait_recv()
            r.crossb[...] = add_low(r.terms[2], r.near3[...])
            cross.start()

        @pl.when(i == 2)
        def _():
            term1.start()

        return carry

    lax.fori_loop(0, slabs, term_step, 0)
    own_term.start()
    small_y.start()
    f2_group[-1].start()
    f1_group[-1].start()
    flat = (depth, slabs * rows)
    total = mm_nt(r.n1tv[0], r.vgt[0])
    for j in range(1, slabs):
        total += mm_nt(r.n1tv[j], r.vgt[j])
    r.acc3[...] = total
    store_shards(r.vkeep, r.vsend, slice(None), r.acc3)
    val_group.start()
    for h in range(1, heads - 1):
        f2_group[h].second()
        f1_group[h].second()
    small_y.wait_recv()
    r.small_z[0] = r.small[...] + r.small_y[...]
    for move in small_z:
        move.start()
    f2_group[-1].second()
    for move in small_z:
        move.wait_recv()
    small_y.wait_send()
    r.small[...] = sum(r.small_z[k] for k in range(count))
    for move in small_x:
        move.start()
    own_small.start()
    f1_group[-1].second()
    val_group.second()
    for group in [out_group] + f1_group + f2_group + [val_group]:
        group.finish()
    for move in [fterm1, fcross, term1, cross] + small_x:
        move.wait_recv()
    own_term.wait()
    own_small.wait()
    for move in w.all:
        if move is not small_y:
            move.wait_send()


def low_shape(*shape):
    return jax.ShapeDtypeStruct(shape, BF16)


def wide_shape(*shape):
    return jax.ShapeDtypeStruct(shape, F32)


def back(lens, upb_sum, sums, hid, slope, prob, n1t, valt, mgt, f1, f2, vt, xs, fterms, okeep, osend):
    slabs, heads, rows, width = hid.shape
    longest = f2.shape[2]
    depth = vt.shape[0]
    count, part, _ = okeep.shape
    small = (2 * heads + 6 + 7) // 8 * 8
    low, wide = low_shape, wide_shape
    out_shape = [
        low(rows, width),
        low(rows, width),
        low(rows, width),
        low(rows, width),
        low(rows, width),
        low(count, part, width),
        low(heads, count, part, width),
        low(heads, count, part, longest),
        low(count, part, depth),
        wide(slabs, small, width),
    ]
    vl = lambda *s: pltpu.VMEM(s, BF16)
    vw = lambda *s: pltpu.VMEM(s, F32)
    moves = 4 + (count - 1) + (2 * heads + 2) * count + 6
    scratch = dict(
        n1tv=vl(slabs, width, rows),
        valtv=vl(slabs, depth, rows),
        mgtv=vl(slabs, depth, rows),
        vgt=vl(slabs, depth, rows),
        f1v=vl(heads, width, width),
        f2v=vl(heads, width, longest),
        vtv=vl(depth, width),
        hidb=vl(2, rows, width),
        slopeb=vl(2, rows, width),
        probb=vl(2, rows, longest),
        sg=vl(rows, longest),
        pog=vl(slabs, heads, rows, width),
        acc1=vw(width, width),
        acc2=vw(width, longest),
        acc3=vw(width, depth),
        xb=vl(rows, width),
        terms=vl(slabs, rows, width),
        near3=vl(rows, width),
        crossb=vl(rows, width),
        fb=vl(rows, width),
        fnear3=vl(rows, width),
        ok=vl(count, part, width),
        ogot=vl(count, part, width),
        akeep=vl(heads, count, part, width),
        asend=vl(heads, count, part, width),
        agot=vl(heads, count, part, width),
        bkeep=vl(heads, count, part, longest),
        bsend=vl(heads, count, part, longest),
        bgot=vl(heads, count, part, longest),
        vkeep=vl(count, part, depth),
        vsend=vl(count, part, depth),
        vgot=vl(count, part, depth),
        small=vw(small, width),
        small_y=vw(small, width),
        small_z=vw(count, small, width),
        send=pltpu.SemaphoreType.DMA((moves,)),
        recv=pltpu.SemaphoreType.DMA((moves,)),
        load=pltpu.SemaphoreType.DMA((9,)),
        fetch=pltpu.SemaphoreType.DMA((2, 3)),
        store=pltpu.SemaphoreType.DMA((4 + 2 * heads,)),
    )
    smem = pl.BlockSpec(memory_space=pltpu.SMEM)
    anywhere = pl.BlockSpec(memory_space=pl.ANY)
    vmem = pl.BlockSpec(memory_space=pltpu.VMEM)
    return pl.pallas_call(
        back_kernel,
        out_shape=out_shape,
        in_specs=[smem, vmem, vmem] + [anywhere] * 13,
        out_specs=[anywhere] * len(out_shape),
        scratch_shapes=[scratch[n] for n in BACK_SCRATCH],
        compiler_params=pltpu.CompilerParams(
            collective_id=1, has_side_effects=True, vmem_limit_bytes=FUSED_LIMIT
        ),
        cost_estimate=cost(slabs * rows * width * heads * (3 * width + 2 * longest), 60 << 20),
        name="back",
    )(lens, upb_sum, sums, hid, slope, prob, n1t, valt, mgt, f1, f2, vt, xs, fterms, okeep, osend)


def finish_kernel(*refs):
    (
        t0, t1, t2, x, rg, gain, e0, e1, e2, res, downb, small, down, up, ow, f1, f2, val,
    ) = refs[:18]
    (
        result_o, input_o, f1b_o, f2b_o, upb_o, shared_o, down_o, up_o, ow_o, f1_o, f2_o, val_o,
    ) = refs[18:]
    add3 = lambda a, b, c: a[...].astype(F32) + b[...].astype(F32) + c[...].astype(F32)
    result_o[...] = res[...] + (add3(e0, e1, e2) + downb[...])
    scaled, inv_std = standardize(x[...].astype(F32))
    input_o[...] = rg[...] + norm_back(add3(t0, t1, t2), scaled, inv_std, gain[...])
    slabs = small.shape[0]
    heads = f1.shape[0]
    longest = f2.shape[3]
    count = f1.shape[1]
    me = lax.axis_index("head")
    for j in range(slabs):
        owner = jnp.bitwise_xor(me, j)
        upb_o[pl.ds(owner, 1)] = small[j, 2 * heads : 2 * heads + 1]
        for h in range(heads):
            f1b_o[pl.ds(owner * heads + h, 1)] = small[j, h : h + 1]
            f2b_o[pl.ds(owner * heads + h, 1)] = small[j, heads + h : heads + h + 1, 0:longest]
    first = 2 * heads + 1
    shared_o[...] = sum(small[j, first : first + 5] for j in range(slabs))
    for src, dst in ((down, down_o), (up, up_o), (ow, ow_o), (val, val_o)):
        dst[...] = sum(src[k].astype(F32) for k in range(count))
    for h in range(heads):
        f1_o[h] = sum(f1[h, k].astype(F32) for k in range(count))
        f2_o[h] = sum(f2[h, k].astype(F32) for k in range(count))


def finish(members, *args):
    t0, f1, f2, val = args[0], args[15], args[16], args[17]
    rows, width = t0.shape
    heads, _, part, longest = f2.shape
    wide = wide_shape
    return pl.pallas_call(
        finish_kernel,
        out_shape=[
            wide(rows, width),
            wide(rows, width),
            wide(members * heads, width),
            wide(members * heads, longest),
            wide(members, width),
            wide(5, width),
            wide(part, width),
            wide(part, width),
            wide(part, width),
            wide(heads, part, width),
            wide(heads, part, longest),
            wide(part, val.shape[2]),
        ],
        compiler_params=pltpu.CompilerParams(vmem_limit_bytes=VMEM_LIMIT),
        cost_estimate=cost(0, 20 << 20),
        name="finish",
    )(*args)


def local(
    tokens,
    seq_len,
    norm1_gain,
    norm1_bias,
    f1_weight,
    f1_bias,
    f2_weight,
    f2_bias,
    value_weight,
    out_weight,
    norm2_gain,
    norm2_bias,
    up_weight,
    up_bias,
    down_weight,
    down_bias,
    out_grad,
):
    members = lax.axis_size("head")
    vt = value_weight.T
    vecs = jnp.stack([norm1_gain, norm1_bias, norm2_gain, norm2_bias, up_bias, down_bias])
    (
        xs, n1t, hid, slope, prob, valt, mgt, fterms, res_grad, residual, down_parts, up_parts,
        out_keep, out_send, upb, sums2,
    ) = front(
        seq_len, tokens, out_grad, vecs, f1_bias, f2_bias, vt, f1_weight, f2_weight, out_weight,
        up_weight, down_weight,
    )
    (
        t0, tnear, tcross, fnear, fcross, ow_parts, f1_parts, f2_parts, val_parts, small,
    ) = back(
        seq_len, upb, sums2, hid, slope, prob, n1t, valt, mgt, f1_weight, f2_weight, vt, xs,
        fterms, out_keep, out_send,
    )
    (
        result, input_grad, f1b_all, f2b_all, upb_all, shared, down_t, up_piece, ow_piece,
        f1_piece, f2_piece, value_piece,
    ) = finish(
        members, t0, tnear, tcross, tokens, res_grad, vecs[0:1], fterms[0], fnear, fcross,
        residual, vecs[5:6], small, down_parts, up_parts, ow_parts, f1_parts, f2_parts, val_parts,
    )
    low = ow_piece.astype(BF16)
    low = add_low(low, swap(low, "head", 1))
    out_piece = low.astype(F32) + swap(low, "head", 2).astype(F32)
    return (
        result,
        input_grad,
        shared[0],
        shared[1],
        f1_piece,
        f1b_all,
        f2_piece,
        f2b_all,
        value_piece,
        out_piece,
        shared[2],
        shared[3],
        up_piece,
        upb_all.reshape(-1),
        down_t.T,
        shared[4],
    )


def solution(mesh):
    placed = (
        P(("dp", "head"), None),
        P("dp"),
        P(),
        P(),
        P("head", None, None),
        P("head", None),
        P("head", None, None),
        P("head", None),
        P(None, "head"),
        P(),
        P(),
        P(),
        P(None, "head"),
        P("head"),
        P("head", None),
        P(),
        P(("dp", "head"), None),
    )
    return jax.shard_map(
        local,
        mesh=mesh,
        in_specs=placed,
        out_specs=(
            P(("dp", "head"), None),
            P(("dp", "head"), None),
            P(),
            P(),
            P("head", "dp", None),
            P(),
            P("head", "dp", None),
            P(),
            P("dp", "head"),
            P("dp", None),
            P(),
            P(),
            P("dp", "head"),
            P(),
            P("head", "dp"),
            P(),
        ),
        check_vma=False,
    )
```

```python
import types

import jax
import jax.numpy as jnp
from jax import lax
from jax.experimental import pallas as pl
from jax.experimental.pallas import tpu as pltpu
from jax.sharding import PartitionSpec as P

F32 = jnp.float32
BF16 = jnp.bfloat16
BLOCK = 128
FUSED_LIMIT = 63 << 20


def mm(a, b):
    return lax.dot_general(a, b, (((1,), (0,)), ((), ())), preferred_element_type=F32)


def mm_nt(a, b):
    return lax.dot_general(a, b, (((1,), (1,)), ((), ())), preferred_element_type=F32)


def mm_tn(a, b):
    return lax.dot_general(a, b, (((0,), (0,)), ((), ())), preferred_element_type=F32)


def standardize(values):
    centred = values - jnp.mean(values, -1, keepdims=True)
    inv_std = lax.rsqrt(jnp.mean(centred * centred, -1, keepdims=True) + 1e-05)
    return centred * inv_std, inv_std


def norm_back(grad_out, scaled, inv_std, gain):
    grad_scaled = grad_out * gain
    centre_mean = jnp.mean(grad_scaled, -1, keepdims=True)
    cross_mean = jnp.mean(grad_scaled * scaled, -1, keepdims=True)
    return inv_std * (grad_scaled - centre_mean - scaled * cross_mean)


def silu_and_slope(pre_val):
    sigma = 0.5 + 0.5 * jnp.tanh(0.5 * pre_val)
    gated = pre_val * sigma
    return gated, sigma + gated * (1.0 - sigma)


def add_low(a, b):
    return (a.astype(F32) + b.astype(F32)).astype(BF16)


def cost(macs, bytes_accessed):
    return pl.CostEstimate(flops=2 * macs, bytes_accessed=bytes_accessed, transcendentals=0)


def store_shards(both, acc):
    _, count, depth, _ = both.shape
    me = lax.axis_index("dp")
    for d in range(2 * count):
        side = jnp.bitwise_xor(me % 2, d % 2)
        place = jnp.bitwise_xor(me // 2, d // 2)
        both[side, place] = acc[d * depth : (d + 1) * depth].astype(BF16)


def shard_shape(width, lanes):
    members = lax.axis_size("dp")
    return jax.ShapeDtypeStruct((2, members // 2, width // members, lanes), BF16)


class Wires:
    def __init__(self, send, recv):
        self.send, self.recv, self.used = send, recv, 0
        self.all = []

    def remote(self, src, dst, axis, step):
        index = self.used
        self.used += 1
        move = pltpu.make_async_remote_copy(
            src_ref=src,
            dst_ref=dst,
            send_sem=self.send.at[index],
            recv_sem=self.recv.at[index],
            device_id={axis: jnp.bitwise_xor(lax.axis_index(axis), step)},
            device_id_type=pl.DeviceIdType.MESH,
        )
        self.all.append(move)
        return move


class Shards:
    def __init__(self, wires, keep, send, got, out, local_sem):
        self.keep, self.got = keep, got
        self.count = keep.shape[0]
        self.first = wires.remote(send, got, "dp", 1)
        self.rest = [
            wires.remote(keep.at[k], out.at[k], "dp", 2 * k) for k in range(1, self.count)
        ]
        self.own = pltpu.make_async_copy(keep.at[0], out.at[0], local_sem)

    def start(self):
        self.first.start()

    def second(self):
        self.first.wait_recv()
        for k in list(range(1, self.count)) + [0]:
            self.keep[k] = add_low(self.keep[k], self.got[k])
            (self.rest[k - 1] if k else self.own).start()

    def finish(self):
        for move in self.rest:
            move.wait_recv()
        self.own.wait()


def add_got(keep, got):
    for k in range(keep.shape[0]):
        keep[k] = add_low(keep[k], got[k])


def greet(axes):
    barrier = pltpu.get_barrier_semaphore()
    for axis, step in axes:
        pl.semaphore_signal(
            barrier,
            1,
            device_id={axis: jnp.bitwise_xor(lax.axis_index(axis), step)},
            device_id_type=pl.DeviceIdType.MESH,
        )
    pl.semaphore_wait(barrier, len(axes))


def partners():
    over_dp = [1] + list(range(2, lax.axis_size("dp"), 2))
    return [("head", s) for s in range(1, lax.axis_size("head"))] + [("dp", s) for s in over_dp]


FRONT_IN = (
    "lens", "x", "og", "gain1", "bias1", "gain2", "bias2", "upb", "f1b", "f2b", "vw", "f1", "f2",
    "ow", "up", "down",
)
FRONT_OUT = (
    "xs_o", "n1t_o", "hid_o", "slope_o", "prob_o", "valt_o", "mgt_o", "f_o", "rg_o", "res_o",
    "down_o", "up_o", "ow_o", "upb_sum", "sums",
)
FRONT_SCRATCH = (
    "xs", "n1", "n1t", "big", "f2v", "vwv", "hidb", "slopeb", "probb", "valt", "attt", "owv", "upv",
    "downv", "ogs", "n2s", "pug", "near1", "near3", "crossb", "crossr", "fterms", "res", "mgts",
    "acc", "vt", "ohalf", "osent", "ogot", "dboth", "dgot", "uboth", "oboth", "send", "recv",
    "load", "spill", "store",
)


def flat_row(ref):
    return ref[...].reshape(1, -1)


def split_prob(parts, length, longest, b, zero):
    is_full = length == longest
    is_half = length == longest // 2
    for c in range(len(parts)):
        half = parts[c % 2] if c // 2 == b // 2 else zero
        quarter = parts[0] if c == b else zero
        yield c, jnp.where(is_full, parts[c], jnp.where(is_half, half, quarter))


def cells(row):
    return [row[:, c : c + BLOCK] for c in range(0, row.shape[1], BLOCK)]


def front_kernel(*refs):
    r = types.SimpleNamespace(**dict(zip(FRONT_IN + FRONT_OUT + FRONT_SCRATCH, refs)))
    r.low = r.n1
    r.terms = r.xs
    slabs, rows, width = r.xs.shape
    heads, _, longest = r.f2v.shape
    depth = r.valt.shape[1]
    dim = depth // heads
    half = rows // 2
    blocks = rows // BLOCK
    me = lax.axis_index("head")

    w = Wires(r.send, r.recv)
    down_first = w.remote(r.dboth.at[1], r.dgot, "dp", 1)

    def remote(src, dst, step):
        return w.remote(src, dst, "head", step)

    def cut(c):
        return pl.ds(c * half, half)

    def share(step):
        return pl.ds(pl.multiple_of(jnp.bitwise_xor(me, step) * depth, depth), depth)

    my_rows = share(0)
    r.mgt = r.n1t.at[0]
    moves = {
        "x1": remote(r.x, r.xs.at[1], 1),
        "x2": remote(r.x, r.xs.at[2], 2),
        "x3": remote(r.xs.at[2], r.xs.at[3], 1),
        "o1": remote(r.og, r.ogs.at[1], 1),
        "o2": remote(r.og, r.ogs.at[2], 2),
        "o3": remote(r.ogs.at[2], r.ogs.at[3], 1),
        "t1": remote(r.terms.at[1], r.near1, 1),
    }
    columns = remote(r.osent, r.ogot, 1)
    near, far, onward = [], [], []
    for j in range(slabs):
        near.append(remote(r.attt.at[j, my_rows], r.attt.at[j ^ 1, my_rows], 1))
        far.append(remote(r.attt.at[j, my_rows], r.attt.at[j ^ 2, my_rows], 2))
        onward.append(remote(r.attt.at[j, share(2)], r.attt.at[j ^ 1, share(2)], 1))
    for j in range(1, slabs):
        moves[f"g{j}"] = remote(r.mgt.at[share(j)], r.mgts.at[j], j)
    for c in range(2):
        part = cut(c)
        moves[f"t3{c}"] = remote(r.terms.at[3, part], r.near3.at[part], 1)
        moves[f"c{c}"] = remote(r.crossb.at[part], r.crossr.at[part], 2)

    def f1_load(h):
        rows_of = pl.ds(pl.multiple_of(h * width, width), width)
        return pltpu.make_async_copy(r.f1.at[h], r.big.at[rows_of], r.load.at[1 + 2 * h])

    def f2_load(h):
        return pltpu.make_async_copy(r.f2.at[h], r.f2v.at[h], r.load.at[2 + 2 * h])

    loads = [pltpu.make_async_copy(r.x, r.xs.at[0], r.load.at[0])]
    for h in range(heads):
        loads += [f1_load(h), f2_load(h)]
    base = 1 + 2 * heads
    late = [
        pltpu.make_async_copy(r.ow, r.owv, r.load.at[base]),
        pltpu.make_async_copy(r.up, r.upv, r.load.at[base + 1]),
        pltpu.make_async_copy(r.down, r.downv, r.load.at[base + 2]),
        pltpu.make_async_copy(r.og, r.ogs.at[0], r.load.at[base + 3]),
    ]
    columns_load = pltpu.make_async_copy(r.vw, r.vwv, r.load.at[base + 4])
    columns_load.start()
    for copy in loads:
        copy.start()
    greet(partners())
    moves["x2"].start()
    moves["x1"].start()
    for copy in late:
        copy.start()
    columns_load.wait()
    r.vt[...] = r.vwv[...].T
    loads[0].wait()

    def spills(j, h, slot):
        return [
            pltpu.make_async_copy(r.hidb.at[slot], r.hid_o.at[j, h], r.spill.at[slot, 0]),
            pltpu.make_async_copy(r.slopeb.at[slot], r.slope_o.at[j, h], r.spill.at[slot, 1]),
            pltpu.make_async_copy(r.probb.at[slot], r.prob_o.at[j, h], r.spill.at[slot, 2]),
        ]

    def slab_step(j, carry):
        @pl.when(j == 1)
        def _():
            moves["x1"].wait_recv()

        @pl.when(j == 2)
        def _():
            moves["x2"].wait_recv()
            moves["x3"].start()
            moves["o2"].start()
            moves["o1"].start()

        @pl.when(j == 3)
        def _():
            moves["x3"].wait_recv()
            for k in range(2):
                far[k].wait_recv()
                onward[k ^ 2].start()

        scaled, _ = standardize(r.xs[j].astype(F32))
        low = (scaled * flat_row(r.gain1) + flat_row(r.bias1)).astype(BF16)
        r.n1[...] = low
        r.n1t[j] = low.T
        r.valt[j] = mm(r.vt[...], r.n1t[j]).astype(BF16)

        def head_step(h, carry):
            turn = j * heads + h
            slot = turn % 2

            @pl.when(j == 0)
            def _():
                f1_load(h).wait()
                f2_load(h).wait()

            @pl.when(turn >= 2)
            def _():
                for copy in spills(j, h, slot):
                    copy.wait()

            first = jnp.bitwise_xor(me, j) * blocks
            column = lax.broadcasted_iota(jnp.int32, (BLOCK, longest), 1)
            zero = jnp.zeros((BLOCK, BLOCK), F32)
            f1_rows = pl.ds(pl.multiple_of(h * width, width), width)
            for c in range(2):
                part = slice(c * half, (c + 1) * half)
                gated, slope = silu_and_slope(mm(r.n1[part], r.big[f1_rows]) + r.f1b[pl.ds(h, 1)])
                hidden = gated.astype(BF16)
                r.hidb[slot, part] = hidden
                r.slopeb[slot, part] = slope.astype(BF16)
                scores = mm(hidden, r.f2v[h]) + r.f2b[pl.ds(h, 1)]
                for i in range(half // BLOCK):
                    b = c * (half // BLOCK) + i
                    length = r.lens[first + b]
                    own = scores[i * BLOCK : (i + 1) * BLOCK]
                    keep = column < length
                    top = jnp.max(jnp.where(keep, own, -3.0e38), -1, keepdims=True)
                    exp_val = jnp.where(keep, jnp.exp(own - top), 0.0)
                    prob = exp_val * (1.0 / jnp.sum(exp_val, -1, keepdims=True))
                    for k, cell in split_prob(cells(prob), length, longest, b, zero):
                        r.probb[
                            slot, b * BLOCK : (b + 1) * BLOCK, k * BLOCK : (k + 1) * BLOCK
                        ] = cell.astype(BF16)
            own_rows = pl.ds(pl.multiple_of(h * dim, dim), dim)
            mixed = mm_nt(r.valt[j, own_rows], r.probb[slot])
            place = pl.ds(pl.multiple_of(me * depth + h * dim, dim), dim)
            r.attt[j, place] = mixed.astype(BF16)
            for copy in spills(j, h, slot):
                copy.start()
            return carry

        lax.fori_loop(0, heads, head_step, 0)
        for k in range(slabs):

            @pl.when(j == k)
            def _(k=k):
                far[k].start()
                near[k].start()

        return carry

    lax.fori_loop(0, slabs, slab_step, 0)
    stores = [
        pltpu.make_async_copy(r.xs, r.xs_o, r.store.at[0]),
        pltpu.make_async_copy(r.n1t, r.n1t_o, r.store.at[1]),
        pltpu.make_async_copy(r.valt, r.valt_o, r.store.at[2]),
    ]
    for copy in stores:
        copy.start()
    for k in (2, 3):
        near[k].wait_recv()
        onward[k].wait_recv()
    for copy in late:
        copy.wait()
    for copy in stores:
        copy.wait()
    stores = []
    sent = moves["x3"]
    sent.wait_send()

    def residual_step(j, carry):
        residual = r.xs[j].astype(F32) + mm_tn(r.attt[j], r.owv[...])

        @pl.when(j == 0)
        def _():
            r.res[...] = residual

        scaled, _ = standardize(residual)
        r.n2s[j] = (scaled * flat_row(r.gain2) + flat_row(r.bias2)).astype(BF16)
        return carry

    lax.fori_loop(2, 4, residual_step, 0)
    moves["o2"].wait_recv()
    moves["o3"].start()

    def ffn_step(u, carry):
        j = jnp.where(u < 4, 2 + u % 2, (u - 4) // 2)
        c = jnp.where(u < 4, u // 2, u % 2)

        @pl.when(u == 1)
        def _():
            moves["o3"].wait_recv()

        @pl.when(u == 2)
        def _():
            for k in (2, 3):
                far[k].wait_recv()
                onward[k ^ 2].start()

        @pl.when(u == 4)
        def _():
            for k in (0, 1):
                near[k].wait_recv()
                onward[k].wait_recv()
            moves["o1"].wait_recv()
            lax.fori_loop(0, 2, residual_step, 0)

        part = pl.ds(pl.multiple_of(c * half, half), half)
        gated, slope = silu_and_slope(mm(r.n2s[j, part], r.upv[...]) + flat_row(r.upb))
        act = gated.astype(BF16)
        r.big[pl.ds(pl.multiple_of(j * rows + c * half, half), half)] = act
        pug = (mm_nt(r.ogs[j, part], r.downv[...]) * slope).astype(BF16)
        r.pug[j, part] = pug
        r.terms[j, part] = mm_nt(pug, r.upv[...]).astype(BF16)
        r.fterms[j, part] = mm(act, r.downv[...]).astype(BF16)

        for c in range(2):

            @pl.when(u == 2 * c + 1)
            def _(c=c):
                moves[f"t3{c}"].start()

            @pl.when(u == 2 * c + 2)
            def _(c=c):
                moves[f"t3{c}"].wait_recv()
                part = cut(c)
                r.crossb[part] = add_low(r.terms[2, part], r.near3[part])
                moves[f"c{c}"].start()

        @pl.when(u == 7)
        def _():
            moves["t1"].start()

        return carry

    lax.fori_loop(0, 8, ffn_step, 0)
    flat = (slabs * rows, width)
    r.acc[...] = mm_tn(r.ogs[...].reshape(flat), r.big[0 : slabs * rows])
    store_shards(r.dboth, r.acc)
    down_first.start()
    stores = [
        pltpu.make_async_copy(r.fterms, r.f_o, r.store.at[5]),
        pltpu.make_async_copy(r.res, r.res_o, r.store.at[6]),
    ]
    for copy in stores:
        copy.start()
    cot = r.ogs[0].astype(F32)
    r.sums[2:3] = jnp.sum(cot, 0, keepdims=True)
    moves["t1"].wait_recv()
    moves["c0"].wait_recv()
    moves["c1"].wait_recv()

    grad = r.terms[0].astype(F32) + r.near1[...].astype(F32) + r.crossr[...].astype(F32)
    scaled, inv_std = standardize(r.res[...])
    res_grad = cot + norm_back(grad, scaled, inv_std, flat_row(r.gain2))
    r.rg_o[...] = res_grad
    r.low[...] = res_grad.astype(BF16)
    r.sums[0:1] = jnp.sum(grad * scaled, 0, keepdims=True)
    r.sums[1:2] = jnp.sum(grad, 0, keepdims=True)
    r.mgt[...] = mm_nt(r.owv[...], r.low[...]).astype(BF16)
    for j in (2, 3, 1):
        moves[f"g{j}"].start()
        r.mgts[0] = r.mgt[my_rows]
    mixed = r.attt[0]
    r.acc[...] = mm(mixed, r.low[...])
    span = width // 2
    mine = pl.ds(pl.multiple_of(me % 2 * span, BLOCK), span)
    theirs = pl.ds(pl.multiple_of((1 - me % 2) * span, BLOCK), span)
    r.osent[...] = r.acc[:, theirs].astype(BF16)
    columns.start()
    r.ohalf[...] = r.acc[:, mine]
    r.acc[...] = mm_tn(r.n2s[...].reshape(flat), r.pug[...].reshape(flat))
    store_shards(r.uboth, r.acc)
    r.upb_sum[...] = jnp.sum(r.pug[...].reshape(flat).astype(F32), 0, keepdims=True)
    columns.wait_recv()
    r.ohalf[...] += r.ogot[...].astype(F32)
    store_shards(r.oboth, r.ohalf)
    more = [
        pltpu.make_async_copy(r.uboth, r.up_o, r.store.at[4]),
        pltpu.make_async_copy(r.oboth, r.ow_o, r.store.at[7]),
    ]
    for copy in more:
        copy.start()
    stores += more
    for j in range(1, slabs):
        moves[f"g{j}"].wait_recv()
    stores.append(pltpu.make_async_copy(r.mgts, r.mgt_o, r.store.at[8]))
    stores[-1].start()
    down_first.wait_recv()
    add_got(r.dboth.at[0], r.dgot)
    stores.append(pltpu.make_async_copy(r.dboth.at[0], r.down_o, r.store.at[9]))
    stores[-1].start()
    for copy in stores:
        copy.wait()
    total = slabs * heads
    for turn in (total - 2, total - 1):
        for copy in spills(turn // heads, turn % heads, turn % 2):
            copy.wait()
    for move in w.all:
        if move is not sent:
            move.wait_send()


def front(lens, x, og, gain1, bias1, gain2, bias2, upb, f1b, f2b, vw, f1, f2, ow, up, down):
    rows, width = x.shape
    heads, _, longest = f2.shape
    depth = vw.shape[1]
    units = up.shape[1]
    slabs = lax.axis_size("head")
    osh = shard_shape(width, width // 2)
    dsh = shard_shape(width, units)
    group = (slabs, rows, width)
    anywhere = pl.BlockSpec(memory_space=pl.ANY)
    vmem = pl.BlockSpec(memory_space=pltpu.VMEM)
    low = lambda *s: jax.ShapeDtypeStruct(s, BF16)
    wide = lambda *s: jax.ShapeDtypeStruct(s, F32)
    out_shape = [
        low(*group),
        low(slabs, width, rows),
        low(slabs, heads, rows, width),
        low(slabs, heads, rows, width),
        low(slabs, heads, rows, longest),
        low(slabs, depth, rows),
        low(slabs, depth, rows),
        low(*group),
        wide(rows, width),
        wide(rows, width),
        jax.ShapeDtypeStruct(dsh.shape[1:], BF16),
        dsh,
        osh,
        wide(1, units),
        wide(3, width),
    ]
    out_specs = [vmem if n in ("rg_o", "upb_sum", "sums") else anywhere for n in FRONT_OUT]
    vl = lambda *s: pltpu.VMEM(s, BF16)
    vf = lambda *s: pltpu.VMEM(s, F32)
    scratch = dict(
        xs=vl(*group),
        n1=vl(rows, width),
        n1t=vl(slabs, width, rows),
        big=vl(max(heads * width, slabs * rows), width),
        f2v=vl(heads, width, longest),
        hidb=vl(2, rows, width),
        slopeb=vl(2, rows, width),
        probb=vl(2, rows, longest),
        valt=vl(slabs, depth, rows),
        vwv=vl(width, depth),
        attt=vl(slabs, width, rows),
        owv=vl(width, width),
        upv=vl(width, units),
        downv=vl(units, width),
        ogs=vl(*group),
        n2s=vl(*group),
        pug=vl(slabs, rows, units),
        near1=vl(rows, width),
        near3=vl(rows, width),
        crossb=vl(rows, width),
        crossr=vl(rows, width),
        fterms=vl(*group),
        res=vf(rows, width),
        mgts=vl(slabs, depth, rows),
        acc=vf(width, width),
        vt=vl(depth, width),
        ohalf=vf(width, width // 2),
        osent=vl(width, width // 2),
        ogot=vl(width, width // 2),
        dboth=vl(*dsh.shape),
        dgot=vl(*dsh.shape[1:]),
        uboth=vl(*dsh.shape),
        oboth=vl(*osh.shape),
        send=pltpu.SemaphoreType.DMA((12 + 4 * slabs,)),
        recv=pltpu.SemaphoreType.DMA((12 + 4 * slabs,)),
        load=pltpu.SemaphoreType.DMA((6 + 2 * heads,)),
        spill=pltpu.SemaphoreType.DMA((2, 3)),
        store=pltpu.SemaphoreType.DMA((10,)),
    )
    smem = pl.BlockSpec(memory_space=pltpu.SMEM)
    return pl.pallas_call(
        front_kernel,
        out_shape=out_shape,
        in_specs=[smem] + [anywhere] * 2 + [vmem] * 7 + [anywhere] * 6,
        out_specs=out_specs,
        scratch_shapes=[scratch[n] for n in FRONT_SCRATCH],
        compiler_params=pltpu.CompilerParams(
            collective_id=0, has_side_effects=True, vmem_limit_bytes=FUSED_LIMIT
        ),
        cost_estimate=cost(
            slabs * rows * width * (heads * (width + longest) + 6 * units), 60 << 20
        ),
        name="front",
    )(lens, x, og, gain1, bias1, gain2, bias2, upb, f1b, f2b, vw, f1, f2, ow, up, down)


BACK_IN = (
    "lens", "upb_sum", "sums", "gain1", "downb", "vw", "hid", "slope", "prob", "n1t", "valt", "mgt",
    "f1", "f2", "xs", "fterms", "down", "up", "ow", "res", "rg",
)
BACK_OUT = ("result", "input", "ow_o", "down_o", "up_o", "f1_o", "f2_o", "val_o", "small_o")
BACK_SCRATCH = (
    "n1tv", "valtv", "mgtv", "vgt", "f1v", "f2v", "vtv", "terms", "probb", "sg", "pog",
    "acc1", "acc2", "acc3", "xb", "near3", "crossb", "near1", "crossr", "fb", "fnear3",
    "fnear1", "fcrossr", "resv", "rgv", "dk", "uk", "ugot", "ok", "ogot", "oall", "olow", "aboth",
    "agot", "bboth", "bgot", "vboth", "vgot", "small", "small_y", "small_z", "send",
    "recv", "load", "fetch", "store",
)


def back_kernel(*refs):
    r = types.SimpleNamespace(**dict(zip(BACK_IN + BACK_OUT + BACK_SCRATCH, refs)))
    slabs, heads, rows, width = r.pog.shape
    longest = r.probb.shape[2]
    depth = r.vgt.shape[1]
    dim = depth // heads
    blocks = rows // BLOCK
    count = r.ok.shape[0]
    me = lax.axis_index("head")
    turns = slabs * heads
    w = Wires(r.send, r.recv)
    up_group = Shards(w, r.uk, r.up.at[1], r.ugot, r.up_o, r.store.at[4 + 2 * heads])
    out_group = Shards(w, r.ok, r.ow.at[1], r.ogot, r.oall, r.store.at[0])
    out_heads = [w.remote(r.olow, r.ow_o.at[j], "head", j) for j in range(1, slabs)]
    down_rest = [w.remote(r.dk.at[k], r.down_o.at[k], "dp", 2 * k) for k in range(1, count)]
    f1_group, f2_group = [], []
    for h in range(heads):
        both, sem = r.bboth.at[h], r.store.at[1 + heads + h]
        f2_group.append(Shards(w, both.at[0], both.at[1], r.bgot.at[h], r.f2_o.at[h], sem))
        both, sem = r.aboth.at[h], r.store.at[1 + h]
        f1_group.append(Shards(w, both.at[0], both.at[1], r.agot.at[h], r.f1_o.at[h], sem))
    sem = r.store.at[1 + 2 * heads]
    val_group = Shards(w, r.vboth.at[0], r.vboth.at[1], r.vgot, r.val_o, sem)
    fterm1 = w.remote(r.fterms.at[1], r.fnear1, "head", 1)
    fterm3 = w.remote(r.fterms.at[3], r.fnear3, "head", 1)
    fcross = w.remote(r.fb, r.fcrossr, "head", 2)
    term1 = w.remote(r.terms.at[1], r.near1, "head", 1)
    term3 = w.remote(r.terms.at[3], r.near3, "head", 1)
    cross = w.remote(r.crossb, r.crossr, "head", 2)
    small_y = w.remote(r.small, r.small_y, "dp", 1)
    small_z = [
        w.remote(r.small_z.at[0], r.small_z.at[k], "dp", 2 * k) for k in range(1, count)
    ]
    small_x = [
        w.remote(r.small, r.small_o.at[j], "head", j) for j in range(1, slabs)
    ]
    own_low = pltpu.make_async_copy(r.olow, r.ow_o.at[0], r.store.at[2 + 2 * heads])
    own_down = pltpu.make_async_copy(r.dk.at[0], r.down_o.at[0], r.store.at[7 + 2 * heads])
    own_small = pltpu.make_async_copy(r.small, r.small_o.at[0], r.store.at[3 + 2 * heads])

    def load(index, src, dst):
        return pltpu.make_async_copy(src, dst, r.load.at[index])

    loads = [
        load(0, r.mgt, r.mgtv),
        load(1, r.valt, r.valtv),
        load(2, r.f2, r.f2v),
        load(3, r.n1t, r.n1tv),
        load(4, r.down, r.dk),
        load(5, r.fterms.at[2], r.fb),
        load(6, r.f1, r.f1v),
        load(7, r.xs.at[3], r.xb),
        load(8, r.res, r.resv),
        load(9, r.rg, r.rgv),
        load(10, r.up.at[0], r.uk),
        load(11, r.ow.at[0], r.ok),
    ]

    def fetches(turn):
        h, j, slot = turn // slabs, turn % slabs, turn % 2
        return [
            pltpu.make_async_copy(r.prob.at[j, h], r.probb.at[slot], r.fetch.at[slot, 0]),
            pltpu.make_async_copy(r.slope.at[j, h], r.terms.at[2 + slot], r.fetch.at[slot, 1]),
            pltpu.make_async_copy(r.hid.at[j, h], r.terms.at[slot], r.fetch.at[slot, 2]),
        ]

    for copy in loads[:2] + fetches(0) + loads[2:]:
        copy.start()
    r.vtv[...] = r.vw[...].T
    greet(partners())
    up_group.start()
    out_group.start()
    fterm3.start()
    fterm1.start()
    r.small[...] = jnp.zeros_like(r.small)
    r.small[2 * heads : 2 * heads + 1] = r.upb_sum[...]
    r.small[2 * heads + 3 : 2 * heads + 6] = r.sums[...]
    for copy in loads[:6]:
        copy.wait()
    for move in down_rest:
        move.start()
    own_down.start()

    def turn_step(turn, carry):
        h, j, slot = turn // slabs, turn % slabs, turn % 2
        for copy in fetches(turn):
            copy.wait()

        @pl.when(turn + 1 < turns)
        def _():
            for copy in fetches(turn + 1):
                copy.start()

        @pl.when(j == 0)
        def _():
            r.acc1[...] = jnp.zeros_like(r.acc1)
            r.acc2[...] = jnp.zeros_like(r.acc2)

        head_rows = pl.ds(pl.multiple_of(h * dim, dim), dim)
        mgt = r.mgtv[j, head_rows]
        r.vgt[j, head_rows] = mm(mgt, r.probb[slot]).astype(BF16)
        probs_grad = mm_tn(mgt, r.valtv[j, head_rows])
        first = jnp.bitwise_xor(me, j) * blocks
        zero = jnp.zeros((BLOCK, BLOCK), F32)
        for b in range(blocks):
            length = r.lens[first + b]
            own = slice(b * BLOCK, (b + 1) * BLOCK)
            prob = r.probb[slot, own].astype(F32)
            grad = probs_grad[own]
            inner = jnp.sum(prob * grad, -1, keepdims=True)
            parts = cells(prob * (grad - inner))
            is_full = length == longest
            is_half = length == longest // 2
            for c in range(blocks):
                half = parts[2 * (b // 2) + c] if c < 2 else zero
                quarter = parts[b] if c == 0 else zero
                cell = jnp.where(is_full, parts[c], jnp.where(is_half, half, quarter))
                r.sg[own, c * BLOCK : (c + 1) * BLOCK] = cell.astype(BF16)
        scores_grad = r.sg[...]
        row = pl.ds(h, 1)
        pog = (mm_nt(scores_grad, r.f2v[h]) * r.terms[2 + slot].astype(F32)).astype(BF16)
        r.pog[j, h] = pog
        r.small[row] += jnp.sum(pog.astype(F32), 0, keepdims=True)
        row = pl.ds(heads + h, 1)
        r.small[row, 0:longest] += jnp.sum(scores_grad.astype(F32), 0, keepdims=True)
        r.acc2[...] += mm_tn(r.terms[slot], scores_grad)
        r.acc1[...] += mm(r.n1tv[j], pog)

        for k in range(heads):

            @pl.when(turn == slabs * k + slabs - 1)
            def _(k=k):
                store_shards(r.bboth.at[k], r.acc2)
                f2_group[k].start()
                store_shards(r.aboth.at[k], r.acc1)
                f1_group[k].start()

        @pl.when(turn == 1)
        def _():
            fterm3.wait_recv()
            r.fb[...] = add_low(r.fb[...], r.fnear3[...])
            fcross.start()

        @pl.when(turn == slabs)
        def _():
            for copy in loads[10:]:
                copy.wait()
            up_group.second()

        @pl.when(turn == slabs + 2)
        def _():
            out_group.second()

        @pl.when(turn == 2 * slabs)
        def _():
            out_group.finish()
            r.olow[...] = sum(r.oall[k].astype(F32) for k in range(count)).astype(BF16)
            for move in out_heads:
                move.start()
            own_low.start()
            f2_group[0].second()

        return carry

    lax.fori_loop(0, turns, turn_step, 0)
    f1_group[0].second()
    for copy in loads[6:8]:
        copy.wait()

    def term_step(i, carry):
        j = slabs - 1 - i

        @pl.when(i > 0)
        def _():
            load(7, r.xs.at[j], r.xb).wait()

        term = mm_tn(r.vgt[j], r.vtv[...])
        for h in range(heads):
            term += mm_nt(r.pog[j, h], r.f1v[h])
        low = term.astype(BF16)
        r.terms[j] = low
        wide = low.astype(F32)
        scaled, _ = standardize(r.xb[...].astype(F32))
        base = 2 * heads + 1
        r.small[base : base + 1] += jnp.sum(wide * scaled, 0, keepdims=True)
        r.small[base + 1 : base + 2] += jnp.sum(wide, 0, keepdims=True)

        @pl.when(i < slabs - 1)
        def _():
            load(7, r.xs.at[j - 1], r.xb).start()

        @pl.when(i == 0)
        def _():
            term3.start()

        @pl.when(i == 1)
        def _():
            term3.wait_recv()
            r.crossb[...] = add_low(r.terms[2], r.near3[...])
            cross.start()

        @pl.when(i == 2)
        def _():
            term1.start()
            f2_group[1].second()

        return carry

    lax.fori_loop(0, slabs, term_step, 0)
    small_y.start()
    total = mm_nt(r.n1tv[0], r.vgt[0])
    for j in range(1, slabs):
        total += mm_nt(r.n1tv[j], r.vgt[j])
    r.acc3[...] = total
    store_shards(r.vboth, r.acc3)
    val_group.start()
    fcross.wait_send()
    own_fterm = load(12, r.fterms.at[0], r.fb)
    own_fterm.start()
    for copy in loads[8:10] + [own_fterm]:
        copy.wait()
    fterm1.wait_recv()
    fcross.wait_recv()
    others = r.fnear1[...].astype(F32) + r.fcrossr[...].astype(F32)
    r.resv[...] += r.fb[...].astype(F32) + others + flat_row(r.downb)
    finals = [pltpu.make_async_copy(r.resv, r.result, r.store.at[5 + 2 * heads])]
    finals[0].start()
    f1_group[1].second()
    for h in range(2, heads - 1):
        f2_group[h].second()
        f1_group[h].second()
    term1.wait_recv()
    cross.wait_recv()
    grad = r.terms[0].astype(F32) + r.near1[...].astype(F32) + r.crossr[...].astype(F32)
    scaled, inv_std = standardize(r.xb[...].astype(F32))
    r.rgv[...] += norm_back(grad, scaled, inv_std, flat_row(r.gain1))
    finals.append(pltpu.make_async_copy(r.rgv, r.input, r.store.at[6 + 2 * heads]))
    finals[1].start()
    small_y.wait_recv()
    r.small_z[0] = r.small[...] + r.small_y[...]
    for move in small_z:
        move.start()
    f2_group[-1].second()
    for move in small_z:
        move.wait_recv()
    small_y.wait_send()
    r.small[...] = sum(r.small_z[k] for k in range(count))
    for move in small_x:
        move.start()
    own_small.start()
    f1_group[-1].second()
    val_group.second()
    for group in [up_group, val_group] + f1_group + f2_group:
        group.finish()
    for move in down_rest + out_heads + small_x:
        move.wait_recv()
    for copy in finals + [own_down, own_low, own_small]:
        copy.wait()
    for move in w.all:
        if move is not small_y and move is not fcross:
            move.wait_send()


def low_shape(*shape):
    return jax.ShapeDtypeStruct(shape, BF16)


def wide_shape(*shape):
    return jax.ShapeDtypeStruct(shape, F32)


def back(*args):
    hid, f2, vw, ow = args[6], args[13], args[5], args[18]
    slabs, heads, rows, width = hid.shape
    longest = f2.shape[2]
    depth = vw.shape[1]
    _, count, part, span = ow.shape
    small = (2 * heads + 6 + 7) // 8 * 8
    low, wide = low_shape, wide_shape
    out_shape = [
        wide(rows, width),
        wide(rows, width),
        low(slabs, part, span),
        low(count, part, width),
        low(count, part, width),
        low(heads, count, part, width),
        low(heads, count, part, longest),
        low(count, part, depth),
        wide(slabs, small, width),
    ]
    vl = lambda *s: pltpu.VMEM(s, BF16)
    vf = lambda *s: pltpu.VMEM(s, F32)
    moves = 2 * (slabs - 1) + 2 * (count - 1) + (2 * heads + 3) * count + 7
    scratch = dict(
        n1tv=vl(slabs, width, rows),
        valtv=vl(slabs, depth, rows),
        mgtv=vl(slabs, depth, rows),
        vgt=vl(slabs, depth, rows),
        f1v=vl(heads, width, width),
        f2v=vl(heads, width, longest),
        vtv=vl(depth, width),
        probb=vl(2, rows, longest),
        sg=vl(rows, longest),
        pog=vl(slabs, heads, rows, width),
        acc1=vf(width, width),
        acc2=vf(width, longest),
        acc3=vf(width, depth),
        xb=vl(rows, width),
        terms=vl(slabs, rows, width),
        near3=vl(rows, width),
        crossb=vl(rows, width),
        near1=vl(rows, width),
        crossr=vl(rows, width),
        fb=vl(rows, width),
        fnear3=vl(rows, width),
        fnear1=vl(rows, width),
        fcrossr=vl(rows, width),
        resv=vf(rows, width),
        rgv=vf(rows, width),
        ok=vl(count, part, span),
        ogot=vl(count, part, span),
        oall=vl(count, part, span),
        olow=vl(part, span),
        dk=vl(count, part, width),
        uk=vl(count, part, width),
        ugot=vl(count, part, width),
        aboth=vl(heads, 2, count, part, width),
        agot=vl(heads, count, part, width),
        bboth=vl(heads, 2, count, part, longest),
        bgot=vl(heads, count, part, longest),
        vboth=vl(2, count, part, depth),
        vgot=vl(count, part, depth),
        small=vf(small, width),
        small_y=vf(small, width),
        small_z=vf(count, small, width),
        send=pltpu.SemaphoreType.DMA((moves,)),
        recv=pltpu.SemaphoreType.DMA((moves,)),
        load=pltpu.SemaphoreType.DMA((13,)),
        fetch=pltpu.SemaphoreType.DMA((2, 3)),
        store=pltpu.SemaphoreType.DMA((8 + 2 * heads,)),
    )
    smem = pl.BlockSpec(memory_space=pltpu.SMEM)
    anywhere = pl.BlockSpec(memory_space=pl.ANY)
    vmem = pl.BlockSpec(memory_space=pltpu.VMEM)
    return pl.pallas_call(
        back_kernel,
        out_shape=out_shape,
        in_specs=[smem] + [vmem] * 5 + [anywhere] * 15,
        out_specs=[anywhere] * len(out_shape),
        scratch_shapes=[scratch[n] for n in BACK_SCRATCH],
        compiler_params=pltpu.CompilerParams(
            collective_id=1, has_side_effects=True, vmem_limit_bytes=FUSED_LIMIT
        ),
        cost_estimate=cost(slabs * rows * width * heads * (3 * width + 2 * longest), 60 << 20),
        name="back",
    )(*args)


def finish_kernel(*refs):
    result, inp, small, down, up, ow, f1, f2, val = refs[:9]
    (
        result_o, input_o, f1b_o, f2b_o, upb_o, down_o, up_o, ow_o, f1_o, f2_o, val_o,
    ) = refs[9:20]
    shared = refs[20:25]
    result_o[...] = result[...]
    input_o[...] = inp[...]
    slabs = small.shape[0]
    heads = f1.shape[0]
    longest = f2.shape[3]
    count = f1.shape[1]
    me = lax.axis_index("head")
    for j in range(slabs):
        owner = jnp.bitwise_xor(me, j)
        upb_o[pl.ds(owner, 1)] = small[j, 2 * heads : 2 * heads + 1]
        for h in range(heads):
            f1b_o[pl.ds(owner * heads + h, 1)] = small[j, h : h + 1]
            f2b_o[pl.ds(owner * heads + h, 1)] = small[j, heads + h : heads + h + 1, 0:longest]
    first = 2 * heads + 1
    for i, ref in enumerate(shared):
        ref[...] = sum(small[j, first + i] for j in range(slabs))
    span = ow.shape[2]
    mine = pl.ds(pl.multiple_of(me % 2 * span, BLOCK), span)
    theirs = pl.ds(pl.multiple_of((1 - me % 2) * span, BLOCK), span)
    ow_o[:, mine] = sum(ow[j].astype(F32) for j in range(0, slabs, 2))
    ow_o[:, theirs] = sum(ow[j].astype(F32) for j in range(1, slabs, 2))
    total = lambda ref: sum(ref[k].astype(F32) for k in range(count))
    down_o[...] = total(down).T
    up_o[...] = total(up)
    val_o[...] = total(val)
    for h in range(heads):
        f1_o[h] = total(f1.at[h])
        f2_o[h] = total(f2.at[h])


def finish(members, *args):
    f1, f2, val = args[6:]
    rows, width = args[0].shape
    heads, _, part, longest = f2.shape
    wide = wide_shape
    return pl.pallas_call(
        finish_kernel,
        out_shape=[
            wide(rows, width),
            wide(rows, width),
            wide(members * heads, width),
            wide(members * heads, longest),
            wide(members, width),
            wide(width, part),
            wide(part, width),
            wide(part, width),
            wide(heads, part, width),
            wide(heads, part, longest),
            wide(part, val.shape[2]),
        ]
        + [wide(width)] * 5,
        compiler_params=pltpu.CompilerParams(vmem_limit_bytes=FUSED_LIMIT),
        cost_estimate=cost(0, 20 << 20),
        name="finish",
    )(*args)


def local(
    tokens,
    seq_len,
    norm1_gain,
    norm1_bias,
    f1_weight,
    f1_bias,
    f2_weight,
    f2_bias,
    value_weight,
    out_weight,
    norm2_gain,
    norm2_bias,
    up_weight,
    up_bias,
    down_weight,
    down_bias,
    out_grad,
):
    members = lax.axis_size("head")
    (
        xs, n1t, hid, slope, prob, valt, mgt, fterms, res_grad, residual, down_y, up_y, ow_y, upb,
        sums2,
    ) = front(
        seq_len, tokens, out_grad, norm1_gain, norm1_bias, norm2_gain, norm2_bias, up_bias, f1_bias,
        f2_bias, value_weight, f1_weight, f2_weight, out_weight, up_weight, down_weight,
    )
    (
        result, input_grad, ow_parts, down_parts, up_parts, f1_parts, f2_parts, val_parts, small,
    ) = back(
        seq_len, upb, sums2, norm1_gain, down_bias, value_weight, hid, slope, prob, n1t, valt, mgt,
        f1_weight, f2_weight, xs, fterms, down_y, up_y, ow_y, residual, res_grad,
    )
    (
        result, input_grad, f1b_all, f2b_all, upb_all, down_piece, up_piece, out_piece, f1_piece,
        f2_piece, value_piece, gain1_g, bias1_g, gain2_g, bias2_g, downb_g,
    ) = finish(
        members, result, input_grad, small, down_parts, up_parts, ow_parts, f1_parts, f2_parts,
        val_parts,
    )
    return (
        result,
        input_grad,
        gain1_g,
        bias1_g,
        f1_piece,
        f1b_all,
        f2_piece,
        f2b_all,
        value_piece,
        out_piece,
        gain2_g,
        bias2_g,
        up_piece,
        upb_all.reshape(-1),
        down_piece,
        downb_g,
    )


def solution(mesh):
    placed = (
        P(("dp", "head"), None),
        P("dp"),
        P(),
        P(),
        P("head", None, None),
        P("head", None),
        P("head", None, None),
        P("head", None),
        P(None, "head"),
        P(),
        P(),
        P(),
        P(None, "head"),
        P("head"),
        P("head", None),
        P(),
        P(("dp", "head"), None),
    )
    return jax.shard_map(
        local,
        mesh=mesh,
        in_specs=placed,
        out_specs=(
            P(("dp", "head"), None),
            P(("dp", "head"), None),
            P(),
            P(),
            P("head", "dp", None),
            P(),
            P("head", "dp", None),
            P(),
            P("dp", "head"),
            P("dp", None),
            P(),
            P(),
            P("dp", "head"),
            P(),
            P("head", "dp"),
            P(),
        ),
        check_vma=False,
    )
```

```python
import types

import jax
import jax.numpy as jnp
from jax import lax
from jax.experimental import pallas as pl
from jax.experimental.pallas import tpu as pltpu
from jax.sharding import PartitionSpec as P

F32 = jnp.float32
BF16 = jnp.bfloat16
BLOCK = 128
FUSED_LIMIT = 63 << 20


def mm(a, b):
    return lax.dot_general(a, b, (((1,), (0,)), ((), ())), preferred_element_type=F32)


def mm_nt(a, b):
    return lax.dot_general(a, b, (((1,), (1,)), ((), ())), preferred_element_type=F32)


def mm_tn(a, b):
    return lax.dot_general(a, b, (((0,), (0,)), ((), ())), preferred_element_type=F32)


def standardize(values):
    centred = values - jnp.mean(values, -1, keepdims=True)
    inv_std = lax.rsqrt(jnp.mean(centred * centred, -1, keepdims=True) + 1e-05)
    return centred * inv_std, inv_std


def norm_back(grad_out, scaled, inv_std, gain):
    grad_scaled = grad_out * gain
    centre_mean = jnp.mean(grad_scaled, -1, keepdims=True)
    cross_mean = jnp.mean(grad_scaled * scaled, -1, keepdims=True)
    return inv_std * (grad_scaled - centre_mean - scaled * cross_mean)


def silu_and_slope(pre_val):
    sigma = 0.5 + 0.5 * jnp.tanh(0.5 * pre_val)
    gated = pre_val * sigma
    return gated, sigma + gated * (1.0 - sigma)


def add_low(a, b):
    return (a.astype(F32) + b.astype(F32)).astype(BF16)


def cost(macs, bytes_accessed):
    return pl.CostEstimate(flops=2 * macs, bytes_accessed=bytes_accessed, transcendentals=0)


def store_shards(both, acc):
    _, count, depth, _ = both.shape
    me = lax.axis_index("dp")
    for d in range(2 * count):
        side = jnp.bitwise_xor(me % 2, d % 2)
        other = jnp.bitwise_xor(me // 2, d // 2)
        gray = jnp.bitwise_xor(other, other // 2)
        place, size, bit = 0, count // 2, 1
        while size:
            place = place + gray // bit % 2 * size
            size, bit = size // 2, bit * 2
        both[side, place] = acc[d * depth : (d + 1) * depth].astype(BF16)


def shard_shape(width, lanes):
    members = lax.axis_size("dp")
    return jax.ShapeDtypeStruct((2, members // 2, width // members, lanes), BF16)


class Wires:
    def __init__(self, send, recv):
        self.send, self.recv, self.used = send, recv, 0
        self.all = []

    def remote(self, src, dst, axis, step):
        index = self.used
        self.used += 1
        move = pltpu.make_async_remote_copy(
            src_ref=src,
            dst_ref=dst,
            send_sem=self.send.at[index],
            recv_sem=self.recv.at[index],
            device_id={axis: jnp.bitwise_xor(lax.axis_index(axis), step)},
            device_id_type=pl.DeviceIdType.MESH,
        )
        self.all.append(move)
        return move


def masks(count):
    found = [1]
    while 2 ** (len(found) + 1) <= count:
        found.append(2 * found[-1] + 1)
    return found


class Shards:
    def __init__(self, wires, keep, send, got, out, own_sem, load_sem):
        self.keep, self.got, self.out, self.load_sem = keep, got, out, load_sem
        self.count = keep.shape[0]
        self.first = None if send is None else wires.remote(send, got, "dp", 1)
        self.steps = []
        size = self.count
        for mask in masks(self.count):
            size //= 2
            part = pl.ds(size, size)
            move = wires.remote(keep.at[part], out.at[part], "dp", 2 * mask)
            self.steps.append((size, move))
        self.own = pltpu.make_async_copy(keep.at[0], out.at[0], own_sem)

    def start(self):
        self.first.start()

    def add(self, size):
        for k in range(size):
            self.keep[k] = add_low(self.keep[k], self.got[k])

    def second(self):
        if self.first is not None:
            self.first.wait_recv()
            self.add(self.count)
        self.steps[0][1].start()

    def third(self):
        for (size, move), (_, after) in zip(self.steps, self.steps[1:]):
            move.wait_recv()
            part = pl.ds(0, size)
            copy = pltpu.make_async_copy(
                self.out.at[pl.ds(size, size)], self.got.at[part], self.load_sem
            )
            copy.start()
            copy.wait()
            self.add(size)
            after.start()
        self.own.start()

    def finish(self):
        self.steps[-1][1].wait_recv()
        self.own.wait()


def add_got(keep, got):
    for k in range(keep.shape[0]):
        keep[k] = add_low(keep[k], got[k])


def greet(axes):
    barrier = pltpu.get_barrier_semaphore()
    for axis, step in axes:
        pl.semaphore_signal(
            barrier,
            1,
            device_id={axis: jnp.bitwise_xor(lax.axis_index(axis), step)},
            device_id_type=pl.DeviceIdType.MESH,
        )
    pl.semaphore_wait(barrier, len(axes))


def partners(far):
    over_dp = [1] + [2 * mask for mask in masks(lax.axis_size("dp") // 2) if far]
    return [("head", s) for s in range(1, lax.axis_size("head"))] + [("dp", s) for s in over_dp]


FRONT_IN = (
    "lens", "x", "og", "gain1", "bias1", "gain2", "bias2", "upb", "f1b", "f2b", "vt", "f1", "f2",
    "ow", "up", "down",
)
FRONT_OUT = (
    "xs_o", "n1t_o", "hid_o", "slope_o", "prob_o", "valt_o", "mgt_o", "f_o", "rg_o", "res_o",
    "down_o", "up_o", "ow_o", "upb_sum", "sums",
)
FRONT_SCRATCH = (
    "xs", "n1", "n1t", "big", "f2v", "hidb", "slopeb", "probb", "valt", "attt", "owv", "upv",
    "downv", "ogs", "n2s", "pug", "near1", "near3", "crossb", "crossr", "fterms", "res", "mgts",
    "acc", "ohalf", "osent", "ogot", "dboth", "dgot", "uboth", "oboth", "send", "recv",
    "load", "spill", "store",
)


def flat_row(ref):
    return ref[...].reshape(1, -1)


def split_prob(parts, length, longest, b, zero):
    is_full = length == longest
    is_half = length == longest // 2
    for c in range(len(parts)):
        half = parts[c % 2] if c // 2 == b // 2 else zero
        quarter = parts[0] if c == b else zero
        yield c, jnp.where(is_full, parts[c], jnp.where(is_half, half, quarter))


def cells(row):
    return [row[:, c : c + BLOCK] for c in range(0, row.shape[1], BLOCK)]


def front_kernel(*refs):
    r = types.SimpleNamespace(**dict(zip(FRONT_IN + FRONT_OUT + FRONT_SCRATCH, refs)))
    r.low = r.n1
    r.terms = r.xs
    slabs, rows, width = r.xs.shape
    heads, _, longest = r.f2v.shape
    depth = r.valt.shape[1]
    dim = depth // heads
    half = rows // 2
    blocks = rows // BLOCK
    me = lax.axis_index("head")

    w = Wires(r.send, r.recv)
    down_first = w.remote(r.dboth.at[1], r.dgot, "dp", 1)

    def remote(src, dst, step):
        return w.remote(src, dst, "head", step)

    def cut(c):
        return pl.ds(c * half, half)

    def share(step):
        return pl.ds(pl.multiple_of(jnp.bitwise_xor(me, step) * depth, depth), depth)

    my_rows = share(0)
    r.mgt = r.n1t.at[0]
    moves = {
        "x1": remote(r.x, r.xs.at[1], 1),
        "x2": remote(r.x, r.xs.at[2], 2),
        "x3": remote(r.xs.at[2], r.xs.at[3], 1),
        "o1": remote(r.og, r.ogs.at[1], 1),
        "o2": remote(r.og, r.ogs.at[2], 2),
        "o3": remote(r.ogs.at[2], r.ogs.at[3], 1),
        "t1": remote(r.terms.at[1], r.near1, 1),
    }
    columns = remote(r.osent, r.ogot, 1)
    near, far, onward = [], [], []
    for j in range(slabs):
        near.append(remote(r.attt.at[j, my_rows], r.attt.at[j ^ 1, my_rows], 1))
        far.append(remote(r.attt.at[j, my_rows], r.attt.at[j ^ 2, my_rows], 2))
        onward.append(remote(r.attt.at[j, share(2)], r.attt.at[j ^ 1, share(2)], 1))
    for j in range(1, slabs):
        moves[f"g{j}"] = remote(r.mgt.at[share(j)], r.mgts.at[j], j)
    for c in range(2):
        part = cut(c)
        moves[f"t3{c}"] = remote(r.terms.at[3, part], r.near3.at[part], 1)
        moves[f"c{c}"] = remote(r.crossb.at[part], r.crossr.at[part], 2)

    def f1_load(h):
        rows_of = pl.ds(pl.multiple_of(h * width, width), width)
        return pltpu.make_async_copy(r.f1.at[h], r.big.at[rows_of], r.load.at[1 + 2 * h])

    def f2_load(h):
        return pltpu.make_async_copy(r.f2.at[h], r.f2v.at[h], r.load.at[2 + 2 * h])

    loads = [pltpu.make_async_copy(r.x, r.xs.at[0], r.load.at[0])]
    for h in range(heads):
        loads += [f1_load(h), f2_load(h)]
    base = 1 + 2 * heads
    late = [
        pltpu.make_async_copy(r.ow, r.owv, r.load.at[base]),
        pltpu.make_async_copy(r.up, r.upv, r.load.at[base + 1]),
        pltpu.make_async_copy(r.down, r.downv, r.load.at[base + 2]),
        pltpu.make_async_copy(r.og, r.ogs.at[0], r.load.at[base + 3]),
    ]
    for copy in loads:
        copy.start()
    greet(partners(False))
    moves["x2"].start()
    moves["x1"].start()
    for copy in late:
        copy.start()
    loads[0].wait()

    def spills(j, h, slot):
        return [
            pltpu.make_async_copy(r.hidb.at[slot], r.hid_o.at[j, h], r.spill.at[slot, 0]),
            pltpu.make_async_copy(r.slopeb.at[slot], r.slope_o.at[j, h], r.spill.at[slot, 1]),
            pltpu.make_async_copy(r.probb.at[slot], r.prob_o.at[j, h], r.spill.at[slot, 2]),
        ]

    def slab_step(j, carry):
        @pl.when(j == 1)
        def _():
            moves["x1"].wait_recv()

        @pl.when(j == 2)
        def _():
            moves["x2"].wait_recv()
            moves["x3"].start()
            moves["o2"].start()
            moves["o1"].start()

        @pl.when(j == 3)
        def _():
            moves["x3"].wait_recv()
            for k in range(2):
                far[k].wait_recv()
                onward[k ^ 2].start()

        scaled, _ = standardize(r.xs[j].astype(F32))
        low = (scaled * flat_row(r.gain1) + flat_row(r.bias1)).astype(BF16)
        r.n1[...] = low
        r.n1t[j] = low.T
        r.valt[j] = mm(r.vt[...], r.n1t[j]).astype(BF16)

        def head_step(h, carry):
            turn = j * heads + h
            slot = turn % 2

            @pl.when(j == 0)
            def _():
                f1_load(h).wait()
                f2_load(h).wait()

            @pl.when(turn >= 2)
            def _():
                for copy in spills(j, h, slot):
                    copy.wait()

            first = jnp.bitwise_xor(me, j) * blocks
            column = lax.broadcasted_iota(jnp.int32, (BLOCK, longest), 1)
            zero = jnp.zeros((BLOCK, BLOCK), F32)
            f1_rows = pl.ds(pl.multiple_of(h * width, width), width)
            for c in range(2):
                part = slice(c * half, (c + 1) * half)
                gated, slope = silu_and_slope(mm(r.n1[part], r.big[f1_rows]) + r.f1b[pl.ds(h, 1)])
                hidden = gated.astype(BF16)
                r.hidb[slot, part] = hidden
                r.slopeb[slot, part] = slope.astype(BF16)
                scores = mm(hidden, r.f2v[h]) + r.f2b[pl.ds(h, 1)]
                for i in range(half // BLOCK):
                    b = c * (half // BLOCK) + i
                    length = r.lens[first + b]
                    own = scores[i * BLOCK : (i + 1) * BLOCK]
                    keep = column < length
                    top = jnp.max(jnp.where(keep, own, -3.0e38), -1, keepdims=True)
                    exp_val = jnp.where(keep, jnp.exp(own - top), 0.0)
                    prob = exp_val * (1.0 / jnp.sum(exp_val, -1, keepdims=True))
                    for k, cell in split_prob(cells(prob), length, longest, b, zero):
                        r.probb[
                            slot, b * BLOCK : (b + 1) * BLOCK, k * BLOCK : (k + 1) * BLOCK
                        ] = cell.astype(BF16)
            own_rows = pl.ds(pl.multiple_of(h * dim, dim), dim)
            mixed = mm_nt(r.valt[j, own_rows], r.probb[slot])
            place = pl.ds(pl.multiple_of(me * depth + h * dim, dim), dim)
            r.attt[j, place] = mixed.astype(BF16)
            for copy in spills(j, h, slot):
                copy.start()
            return carry

        lax.fori_loop(0, heads, head_step, 0)
        for k in range(slabs):

            @pl.when(j == k)
            def _(k=k):
                far[k].start()
                near[k].start()

        return carry

    lax.fori_loop(0, slabs, slab_step, 0)
    stores = [
        pltpu.make_async_copy(r.xs, r.xs_o, r.store.at[0]),
        pltpu.make_async_copy(r.n1t, r.n1t_o, r.store.at[1]),
        pltpu.make_async_copy(r.valt, r.valt_o, r.store.at[2]),
    ]
    for copy in stores:
        copy.start()
    for k in (2, 3):
        near[k].wait_recv()
        onward[k].wait_recv()
    for copy in late:
        copy.wait()
    for copy in stores:
        copy.wait()
    stores = []
    sent = moves["x3"]
    sent.wait_send()

    def residual_step(j, carry):
        residual = r.xs[j].astype(F32) + mm_tn(r.attt[j], r.owv[...])

        @pl.when(j == 0)
        def _():
            r.res[...] = residual

        scaled, _ = standardize(residual)
        r.n2s[j] = (scaled * flat_row(r.gain2) + flat_row(r.bias2)).astype(BF16)
        return carry

    lax.fori_loop(2, 4, residual_step, 0)
    moves["o2"].wait_recv()
    moves["o3"].start()

    def ffn_step(u, carry):
        j = jnp.where(u < 4, 2 + u % 2, (u - 4) // 2)
        c = jnp.where(u < 4, u // 2, u % 2)

        @pl.when(u == 1)
        def _():
            moves["o3"].wait_recv()

        @pl.when(u == 2)
        def _():
            for k in (2, 3):
                far[k].wait_recv()
                onward[k ^ 2].start()

        @pl.when(u == 4)
        def _():
            for k in (0, 1):
                near[k].wait_recv()
                onward[k].wait_recv()
            moves["o1"].wait_recv()
            lax.fori_loop(0, 2, residual_step, 0)

        part = pl.ds(pl.multiple_of(c * half, half), half)
        gated, slope = silu_and_slope(mm(r.n2s[j, part], r.upv[...]) + flat_row(r.upb))
        act = gated.astype(BF16)
        r.big[pl.ds(pl.multiple_of(j * rows + c * half, half), half)] = act
        pug = (mm_nt(r.ogs[j, part], r.downv[...]) * slope).astype(BF16)
        r.pug[j, part] = pug
        r.terms[j, part] = mm_nt(pug, r.upv[...]).astype(BF16)
        r.fterms[j, part] = mm(act, r.downv[...]).astype(BF16)

        for c in range(2):

            @pl.when(u == 2 * c + 1)
            def _(c=c):
                moves[f"t3{c}"].start()

            @pl.when(u == 2 * c + 2)
            def _(c=c):
                moves[f"t3{c}"].wait_recv()
                part = cut(c)
                r.crossb[part] = add_low(r.terms[2, part], r.near3[part])
                moves[f"c{c}"].start()

        @pl.when(u == 7)
        def _():
            moves["t1"].start()

        return carry

    lax.fori_loop(0, 8, ffn_step, 0)
    flat = (slabs * rows, width)
    r.acc[...] = mm_tn(r.ogs[...].reshape(flat), r.big[0 : slabs * rows])
    store_shards(r.dboth, r.acc)
    down_first.start()
    stores = [
        pltpu.make_async_copy(r.fterms, r.f_o, r.store.at[5]),
        pltpu.make_async_copy(r.res, r.res_o, r.store.at[6]),
    ]
    for copy in stores:
        copy.start()
    cot = r.ogs[0].astype(F32)
    r.sums[2:3] = jnp.sum(cot, 0, keepdims=True)
    moves["t1"].wait_recv()
    moves["c0"].wait_recv()
    moves["c1"].wait_recv()

    grad = r.terms[0].astype(F32) + r.near1[...].astype(F32) + r.crossr[...].astype(F32)
    scaled, inv_std = standardize(r.res[...])
    res_grad = cot + norm_back(grad, scaled, inv_std, flat_row(r.gain2))
    r.rg_o[...] = res_grad
    r.low[...] = res_grad.astype(BF16)
    r.sums[0:1] = jnp.sum(grad * scaled, 0, keepdims=True)
    r.sums[1:2] = jnp.sum(grad, 0, keepdims=True)
    r.mgt[...] = mm_nt(r.owv[...], r.low[...]).astype(BF16)
    for j in (2, 3, 1):
        moves[f"g{j}"].start()
        r.mgts[0] = r.mgt[my_rows]
    mixed = r.attt[0]
    r.acc[...] = mm(mixed, r.low[...])
    span = width // 2
    mine = pl.ds(pl.multiple_of(me % 2 * span, BLOCK), span)
    theirs = pl.ds(pl.multiple_of((1 - me % 2) * span, BLOCK), span)
    r.osent[...] = r.acc[:, theirs].astype(BF16)
    columns.start()
    r.ohalf[...] = r.acc[:, mine]
    r.acc[...] = mm_tn(r.n2s[...].reshape(flat), r.pug[...].reshape(flat))
    store_shards(r.uboth, r.acc)
    r.upb_sum[...] = jnp.sum(r.pug[...].reshape(flat).astype(F32), 0, keepdims=True)
    columns.wait_recv()
    r.ohalf[...] += r.ogot[...].astype(F32)
    store_shards(r.oboth, r.ohalf)
    more = [
        pltpu.make_async_copy(r.uboth, r.up_o, r.store.at[4]),
        pltpu.make_async_copy(r.oboth, r.ow_o, r.store.at[7]),
    ]
    for copy in more:
        copy.start()
    stores += more
    for j in range(1, slabs):
        moves[f"g{j}"].wait_recv()
    stores.append(pltpu.make_async_copy(r.mgts, r.mgt_o, r.store.at[8]))
    stores[-1].start()
    down_first.wait_recv()
    add_got(r.dboth.at[0], r.dgot)
    stores.append(pltpu.make_async_copy(r.dboth.at[0], r.down_o, r.store.at[9]))
    stores[-1].start()
    for copy in stores:
        copy.wait()
    total = slabs * heads
    for turn in (total - 2, total - 1):
        for copy in spills(turn // heads, turn % heads, turn % 2):
            copy.wait()
    for move in w.all:
        if move is not sent:
            move.wait_send()


def front(lens, x, og, gain1, bias1, gain2, bias2, upb, f1b, f2b, vt, f1, f2, ow, up, down):
    rows, width = x.shape
    heads, _, longest = f2.shape
    depth = vt.shape[0]
    units = up.shape[1]
    slabs = lax.axis_size("head")
    osh = shard_shape(width, width // 2)
    dsh = shard_shape(width, units)
    group = (slabs, rows, width)
    anywhere = pl.BlockSpec(memory_space=pl.ANY)
    vmem = pl.BlockSpec(memory_space=pltpu.VMEM)
    low = lambda *s: jax.ShapeDtypeStruct(s, BF16)
    wide = lambda *s: jax.ShapeDtypeStruct(s, F32)
    out_shape = [
        low(*group),
        low(slabs, width, rows),
        low(slabs, heads, rows, width),
        low(slabs, heads, rows, width),
        low(slabs, heads, rows, longest),
        low(slabs, depth, rows),
        low(slabs, depth, rows),
        low(*group),
        wide(rows, width),
        wide(rows, width),
        jax.ShapeDtypeStruct(dsh.shape[1:], BF16),
        dsh,
        osh,
        wide(1, units),
        wide(3, width),
    ]
    out_specs = [vmem if n in ("rg_o", "upb_sum", "sums") else anywhere for n in FRONT_OUT]
    vl = lambda *s: pltpu.VMEM(s, BF16)
    vf = lambda *s: pltpu.VMEM(s, F32)
    scratch = dict(
        xs=vl(*group),
        n1=vl(rows, width),
        n1t=vl(slabs, width, rows),
        big=vl(max(heads * width, slabs * rows), width),
        f2v=vl(heads, width, longest),
        hidb=vl(2, rows, width),
        slopeb=vl(2, rows, width),
        probb=vl(2, rows, longest),
        valt=vl(slabs, depth, rows),
        attt=vl(slabs, width, rows),
        owv=vl(width, width),
        upv=vl(width, units),
        downv=vl(units, width),
        ogs=vl(*group),
        n2s=vl(*group),
        pug=vl(slabs, rows, units),
        near1=vl(rows, width),
        near3=vl(rows, width),
        crossb=vl(rows, width),
        crossr=vl(rows, width),
        fterms=vl(*group),
        res=vf(rows, width),
        mgts=vl(slabs, depth, rows),
        acc=vf(width, width),
        ohalf=vf(width, width // 2),
        osent=vl(width, width // 2),
        ogot=vl(width, width // 2),
        dboth=vl(*dsh.shape),
        dgot=vl(*dsh.shape[1:]),
        uboth=vl(*dsh.shape),
        oboth=vl(*osh.shape),
        send=pltpu.SemaphoreType.DMA((12 + 4 * slabs,)),
        recv=pltpu.SemaphoreType.DMA((12 + 4 * slabs,)),
        load=pltpu.SemaphoreType.DMA((5 + 2 * heads,)),
        spill=pltpu.SemaphoreType.DMA((2, 3)),
        store=pltpu.SemaphoreType.DMA((10,)),
    )
    smem = pl.BlockSpec(memory_space=pltpu.SMEM)
    return pl.pallas_call(
        front_kernel,
        out_shape=out_shape,
        in_specs=[smem] + [anywhere] * 2 + [vmem] * 8 + [anywhere] * 5,
        out_specs=out_specs,
        scratch_shapes=[scratch[n] for n in FRONT_SCRATCH],
        compiler_params=pltpu.CompilerParams(
            collective_id=0, has_side_effects=True, vmem_limit_bytes=FUSED_LIMIT
        ),
        cost_estimate=cost(
            slabs * rows * width * (heads * (width + longest) + 6 * units), 60 << 20
        ),
        name="front",
    )(lens, x, og, gain1, bias1, gain2, bias2, upb, f1b, f2b, vt, f1, f2, ow, up, down)


BACK_IN = (
    "lens", "upb_sum", "sums", "gain1", "downb", "vt", "hid", "slope", "prob", "n1t", "valt", "mgt",
    "f1", "f2", "xs", "fterms", "down", "up", "ow", "res", "rg",
)
BACK_OUT = ("result", "input", "ow_o", "down_o", "up_o", "f1_o", "f2_o", "val_o", "small_o")
BACK_SCRATCH = (
    "n1tv", "valtv", "mgtv", "vgt", "f1v", "f2v", "terms", "probb", "sg", "pog",
    "acc1", "acc2", "acc3", "xb", "near3", "near1", "crossr", "fb", "fnear3",
    "fnear1", "fcrossr", "rgv", "dk", "dgot", "uk", "ugot", "ok", "ogot", "oall", "olow", "aboth",
    "agot", "bboth", "bgot", "vboth", "vgot", "small", "small_in", "send",
    "recv", "load", "fetch", "store",
)


def back_kernel(*refs):
    r = types.SimpleNamespace(**dict(zip(BACK_IN + BACK_OUT + BACK_SCRATCH, refs)))
    r.crossb = r.terms.at[3]
    r.resv = r.acc1.at[pl.ds(0, r.rgv.shape[0])]
    slabs, heads, rows, width = r.pog.shape
    longest = r.probb.shape[2]
    depth = r.vgt.shape[1]
    dim = depth // heads
    blocks = rows // BLOCK
    count = r.ok.shape[0]
    me = lax.axis_index("head")
    turns = slabs * heads
    w = Wires(r.send, r.recv)
    sems = iter(range(4 * heads + 8))

    def shards(keep, send, got, out):
        return Shards(w, keep, send, got, out, r.store.at[next(sems)], r.store.at[next(sems)])

    down_group = shards(r.dk, None, r.dgot, r.down_o)
    up_group = shards(r.uk, r.up.at[1], r.ugot, r.up_o)
    out_group = shards(r.ok, r.ow.at[1], r.ogot, r.oall)
    out_heads = [w.remote(r.olow, r.ow_o.at[j], "head", j) for j in range(1, slabs)]
    f1_group, f2_group = [], []
    for h in range(heads):
        both = r.bboth.at[h]
        f2_group.append(shards(both.at[0], both.at[1], r.bgot.at[h], r.f2_o.at[h]))
        both = r.aboth.at[h]
        f1_group.append(shards(both.at[0], both.at[1], r.agot.at[h], r.f1_o.at[h]))
    val_group = shards(r.vboth.at[0], r.vboth.at[1], r.vgot, r.val_o)
    fterm1 = w.remote(r.fterms.at[1], r.fnear1, "head", 1)
    fterm3 = w.remote(r.fterms.at[3], r.fnear3, "head", 1)
    fcross = w.remote(r.fb, r.fcrossr, "head", 2)
    term1 = w.remote(r.terms.at[1], r.near1, "head", 1)
    term3 = w.remote(r.terms.at[3], r.near3, "head", 1)
    cross = w.remote(r.crossb, r.crossr, "head", 2)
    steps = [1] + [2 * mask for mask in masks(count)]
    small_steps = [
        w.remote(r.small.at[i], r.small_in.at[i], "dp", step) for i, step in enumerate(steps)
    ]
    small_last = r.small.at[len(steps)]
    small_x = [
        w.remote(small_last, r.small_o.at[j], "head", j) for j in range(1, slabs)
    ]
    base = 4 * heads + 8
    own_low = pltpu.make_async_copy(r.olow, r.ow_o.at[0], r.store.at[base])
    own_small = pltpu.make_async_copy(small_last, r.small_o.at[0], r.store.at[base + 1])

    def load(index, src, dst):
        return pltpu.make_async_copy(src, dst, r.load.at[index])

    loads = [
        load(0, r.mgt, r.mgtv),
        load(1, r.valt, r.valtv),
        load(2, r.f2, r.f2v),
        load(3, r.n1t, r.n1tv),
        load(4, r.down, r.dk),
        load(5, r.fterms.at[2], r.fb),
        load(6, r.f1, r.f1v),
        load(7, r.xs.at[3], r.xb),
        load(9, r.rg, r.rgv),
        load(10, r.up.at[0], r.uk),
        load(11, r.ow.at[0], r.ok),
    ]

    def fetches(turn):
        h, j, slot = turn // slabs, turn % slabs, turn % 2
        return [
            pltpu.make_async_copy(r.prob.at[j, h], r.probb.at[slot], r.fetch.at[slot, 0]),
            pltpu.make_async_copy(r.slope.at[j, h], r.terms.at[2 + slot], r.fetch.at[slot, 1]),
            pltpu.make_async_copy(r.hid.at[j, h], r.terms.at[slot], r.fetch.at[slot, 2]),
        ]

    for copy in loads[:2] + fetches(0) + loads[2:]:
        copy.start()
    greet(partners(True))
    up_group.start()
    out_group.start()
    fterm3.start()
    fterm1.start()
    r.small[0] = jnp.zeros(r.small.shape[1:], F32)
    r.small[0, 2 * heads : 2 * heads + 1] = r.upb_sum[...]
    r.small[0, 2 * heads + 3 : 2 * heads + 6] = r.sums[...]
    for copy in loads[:6]:
        copy.wait()
    down_group.second()

    def turn_step(turn, carry):
        h, j, slot = turn // slabs, turn % slabs, turn % 2
        for copy in fetches(turn):
            copy.wait()

        @pl.when(turn + 1 < turns)
        def _():
            for copy in fetches(turn + 1):
                copy.start()

        @pl.when(j == 0)
        def _():
            r.acc1[...] = jnp.zeros_like(r.acc1)
            r.acc2[...] = jnp.zeros_like(r.acc2)

        head_rows = pl.ds(pl.multiple_of(h * dim, dim), dim)
        mgt = r.mgtv[j, head_rows]
        r.vgt[j, head_rows] = mm(mgt, r.probb[slot]).astype(BF16)
        probs_grad = mm_tn(mgt, r.valtv[j, head_rows])
        first = jnp.bitwise_xor(me, j) * blocks
        zero = jnp.zeros((BLOCK, BLOCK), F32)
        for b in range(blocks):
            length = r.lens[first + b]
            own = slice(b * BLOCK, (b + 1) * BLOCK)
            prob = r.probb[slot, own].astype(F32)
            grad = probs_grad[own]
            inner = jnp.sum(prob * grad, -1, keepdims=True)
            parts = cells(prob * (grad - inner))
            is_full = length == longest
            is_half = length == longest // 2
            for c in range(blocks):
                half = parts[2 * (b // 2) + c] if c < 2 else zero
                quarter = parts[b] if c == 0 else zero
                cell = jnp.where(is_full, parts[c], jnp.where(is_half, half, quarter))
                r.sg[own, c * BLOCK : (c + 1) * BLOCK] = cell.astype(BF16)
        scores_grad = r.sg[...]
        row = pl.ds(h, 1)
        pog = (mm_nt(scores_grad, r.f2v[h]) * r.terms[2 + slot].astype(F32)).astype(BF16)
        r.pog[j, h] = pog
        r.small[0, row] += jnp.sum(pog.astype(F32), 0, keepdims=True)
        row = pl.ds(heads + h, 1)
        r.small[0, row, 0:longest] += jnp.sum(scores_grad.astype(F32), 0, keepdims=True)
        r.acc2[...] += mm_tn(r.terms[slot], scores_grad)
        r.acc1[...] += mm(r.n1tv[j], pog)

        for k in range(heads):

            @pl.when(turn == slabs * k + slabs - 1)
            def _(k=k):
                store_shards(r.bboth.at[k], r.acc2)
                f2_group[k].start()
                store_shards(r.aboth.at[k], r.acc1)
                if k < heads - 1:
                    f1_group[k].start()

        @pl.when(turn == 1)
        def _():
            fterm3.wait_recv()
            r.fb[...] = add_low(r.fb[...], r.fnear3[...])
            fcross.start()

        @pl.when(turn == slabs - 1)
        def _():
            down_group.third()

        @pl.when(turn == slabs)
        def _():
            for copy in loads[9:]:
                copy.wait()
            up_group.second()

        @pl.when(turn == slabs + 2)
        def _():
            out_group.second()
            up_group.third()

        @pl.when(turn == 2 * slabs)
        def _():
            out_group.third()
            f2_group[0].second()

        @pl.when(turn == 2 * slabs + 2)
        def _():
            out_group.finish()
            r.olow[...] = (r.oall[0].astype(F32) + r.oall[1].astype(F32)).astype(BF16)
            for move in out_heads:
                move.start()
            own_low.start()
            f2_group[0].third()

        return carry

    lax.fori_loop(0, turns, turn_step, 0)
    f1_group[0].second()
    for copy in loads[6:8]:
        copy.wait()
    res_load = load(8, r.res, r.resv)
    res_load.start()

    def term_step(i, carry):
        j = slabs - 1 - i

        @pl.when(i > 0)
        def _():
            load(7, r.xs.at[j], r.xb).wait()

        term = mm_tn(r.vgt[j], r.vt[...])
        for h in range(heads):
            term += mm_nt(r.pog[j, h], r.f1v[h])
        low = term.astype(BF16)
        r.terms[j] = low
        wide = low.astype(F32)
        scaled, _ = standardize(r.xb[...].astype(F32))
        at = 2 * heads + 1
        r.small[0, at : at + 1] += jnp.sum(wide * scaled, 0, keepdims=True)
        r.small[0, at + 1 : at + 2] += jnp.sum(wide, 0, keepdims=True)

        @pl.when(i < slabs - 1)
        def _():
            load(7, r.xs.at[j - 1], r.xb).start()

        @pl.when(i == 0)
        def _():
            term3.start()

        @pl.when(i == 1)
        def _():
            term3.wait_recv()
            term3.wait_send()
            r.crossb[...] = add_low(r.terms[2], r.near3[...])
            cross.start()

        @pl.when(i == 2)
        def _():
            term1.start()
            f1_group[0].third()

        @pl.when(i == 3)
        def _():
            f2_group[1].second()

        return carry

    lax.fori_loop(0, slabs, term_step, 0)
    small_steps[0].start()
    f1_group[-1].start()
    total = mm_nt(r.n1tv[0], r.vgt[0])
    for j in range(1, slabs):
        total += mm_nt(r.n1tv[j], r.vgt[j])
    r.acc3[...] = total
    store_shards(r.vboth, r.acc3)
    val_group.start()
    fcross.wait_send()
    own_fterm = load(12, r.fterms.at[0], r.fb)
    own_fterm.start()
    for copy in [res_load, loads[8], own_fterm]:
        copy.wait()
    fterm1.wait_recv()
    fcross.wait_recv()
    others = r.fnear1[...].astype(F32) + r.fcrossr[...].astype(F32)
    r.resv[...] += r.fb[...].astype(F32) + others + flat_row(r.downb)
    finals = [pltpu.make_async_copy(r.resv, r.result, r.store.at[base + 2])]
    finals[0].start()
    f2_group[1].third()
    f1_group[1].second()
    term1.wait_recv()
    cross.wait_recv()
    grad = r.terms[0].astype(F32) + r.near1[...].astype(F32) + r.crossr[...].astype(F32)
    scaled, inv_std = standardize(r.xb[...].astype(F32))
    r.rgv[...] += norm_back(grad, scaled, inv_std, flat_row(r.gain1))
    finals.append(pltpu.make_async_copy(r.rgv, r.input, r.store.at[base + 3]))
    finals[1].start()
    f1_group[1].third()
    f2_group[2].second()
    for i, move in enumerate(small_steps):
        move.wait_recv()
        r.small[i + 1] = r.small[i] + r.small_in[i]
        for after in small_steps[i + 1 : i + 2] or small_x + [own_small]:
            after.start()
    f2_group[2].third()
    f1_group[2].second()
    val_group.second()
    f1_group[2].third()
    val_group.third()
    for group in [down_group, up_group] + f2_group + f1_group + [val_group]:
        group.finish()
    for move in out_heads + small_x:
        move.wait_recv()
    for copy in finals + [own_low, own_small]:
        copy.wait()
    for move in w.all:
        if move is not term3 and move is not fcross:
            move.wait_send()


def low_shape(*shape):
    return jax.ShapeDtypeStruct(shape, BF16)


def wide_shape(*shape):
    return jax.ShapeDtypeStruct(shape, F32)


def back(*args):
    hid, f2, vt, ow = args[6], args[13], args[5], args[18]
    slabs, heads, rows, width = hid.shape
    longest = f2.shape[2]
    depth = vt.shape[0]
    _, count, part, span = ow.shape
    small = (2 * heads + 6 + 7) // 8 * 8
    low, wide = low_shape, wide_shape
    out_shape = [
        wide(rows, width),
        wide(rows, width),
        low(slabs, part, span),
        low(count, part, width),
        low(count, part, width),
        low(heads, count, part, width),
        low(heads, count, part, longest),
        low(count, part, depth),
        wide(slabs, small, width),
    ]
    vl = lambda *s: pltpu.VMEM(s, BF16)
    vf = lambda *s: pltpu.VMEM(s, F32)
    steps = len(masks(count)) + 1
    moves = 2 * (slabs - 1) + (2 * heads + 5) * steps + 6
    scratch = dict(
        n1tv=vl(slabs, width, rows),
        valtv=vl(slabs, depth, rows),
        mgtv=vl(slabs, depth, rows),
        vgt=vl(slabs, depth, rows),
        f1v=vl(heads, width, width),
        f2v=vl(heads, width, longest),
        probb=vl(2, rows, longest),
        sg=vl(rows, longest),
        pog=vl(slabs, heads, rows, width),
        acc1=vf(width, width),
        acc2=vf(width, longest),
        acc3=vf(width, depth),
        xb=vl(rows, width),
        terms=vl(slabs, rows, width),
        near3=vl(rows, width),
        near1=vl(rows, width),
        crossr=vl(rows, width),
        fb=vl(rows, width),
        fnear3=vl(rows, width),
        fnear1=vl(rows, width),
        fcrossr=vl(rows, width),
        rgv=vf(rows, width),
        ok=vl(count, part, span),
        ogot=vl(count, part, span),
        oall=vl(count, part, span),
        olow=vl(part, span),
        dk=vl(count, part, width),
        dgot=vl(count // 2, part, width),
        uk=vl(count, part, width),
        ugot=vl(count, part, width),
        aboth=vl(heads, 2, count, part, width),
        agot=vl(heads, count, part, width),
        bboth=vl(heads, 2, count, part, longest),
        bgot=vl(heads, count, part, longest),
        vboth=vl(2, count, part, depth),
        vgot=vl(count, part, depth),
        small=vf(steps + 1, small, width),
        small_in=vf(steps, small, width),
        send=pltpu.SemaphoreType.DMA((moves,)),
        recv=pltpu.SemaphoreType.DMA((moves,)),
        load=pltpu.SemaphoreType.DMA((13,)),
        fetch=pltpu.SemaphoreType.DMA((2, 3)),
        store=pltpu.SemaphoreType.DMA((12 + 4 * heads,)),
    )
    smem = pl.BlockSpec(memory_space=pltpu.SMEM)
    anywhere = pl.BlockSpec(memory_space=pl.ANY)
    vmem = pl.BlockSpec(memory_space=pltpu.VMEM)
    return pl.pallas_call(
        back_kernel,
        out_shape=out_shape,
        in_specs=[smem] + [vmem] * 5 + [anywhere] * 15,
        out_specs=[anywhere] * len(out_shape),
        scratch_shapes=[scratch[n] for n in BACK_SCRATCH],
        compiler_params=pltpu.CompilerParams(
            collective_id=1, has_side_effects=True, vmem_limit_bytes=FUSED_LIMIT
        ),
        cost_estimate=cost(slabs * rows * width * heads * (3 * width + 2 * longest), 60 << 20),
        name="back",
    )(*args)


def finish_kernel(*refs):
    result, inp, small, down, up, ow, f1, f2, val = refs[:9]
    (
        result_o, input_o, f1b_o, f2b_o, upb_o, down_o, up_o, ow_o, f1_o, f2_o, val_o,
    ) = refs[9:20]
    shared = refs[20:25]
    result_o[...] = result[...]
    input_o[...] = inp[...]
    slabs = small.shape[0]
    heads = f1.shape[0]
    longest = f2.shape[3]
    me = lax.axis_index("head")
    for j in range(slabs):
        owner = jnp.bitwise_xor(me, j)
        units = small.shape[2]
        own = small[owner, 2 * heads : 2 * heads + 1]
        upb_o[j * units : (j + 1) * units] = own.reshape(units)
        for h in range(heads):
            f1b_o[pl.ds(owner * heads + h, 1)] = small[j, h : h + 1]
            f2b_o[pl.ds(owner * heads + h, 1)] = small[j, heads + h : heads + h + 1, 0:longest]
    first = 2 * heads + 1
    for i, ref in enumerate(shared):
        ref[...] = sum(small[j, first + i] for j in range(slabs))
    span = ow.shape[2]
    mine = pl.ds(pl.multiple_of(me % 2 * span, BLOCK), span)
    theirs = pl.ds(pl.multiple_of((1 - me % 2) * span, BLOCK), span)
    ow_o[:, mine] = sum(ow[j].astype(F32) for j in range(0, slabs, 2))
    ow_o[:, theirs] = sum(ow[j].astype(F32) for j in range(1, slabs, 2))
    total = lambda ref: ref[0].astype(F32) + ref[1].astype(F32)
    down_o[...] = total(down)
    up_o[...] = total(up)
    val_o[...] = total(val)
    for h in range(heads):
        f1_o[h] = total(f1.at[h])
        f2_o[h] = total(f2.at[h])


def finish(members, *args):
    f1, f2, val = args[6:]
    rows, width = args[0].shape
    heads, _, part, longest = f2.shape
    wide = wide_shape
    out_shape = [
        wide(rows, width),
        wide(rows, width),
        wide(members * heads, width),
        wide(members * heads, longest),
        wide(members * width),
        wide(part, width),
        wide(part, width),
        wide(part, width),
        wide(heads, part, width),
        wide(heads, part, longest),
        wide(part, val.shape[2]),
    ] + [wide(width)] * 5
    whole = lambda v: pl.BlockSpec(v.shape, lambda _: (0,) * v.ndim)
    pair = lambda v: pl.BlockSpec((2,) + v.shape[1:], lambda _: (0, 0, 0))
    heads_pair = lambda v: pl.BlockSpec((heads, 2) + v.shape[2:], lambda _: (0, 0, 0, 0))
    kinds = [whole] * 3 + [pair] * 2 + [whole] + [heads_pair] * 2 + [pair]
    return pl.pallas_call(
        finish_kernel,
        grid=(1,),
        out_shape=out_shape,
        in_specs=[kind(v) for kind, v in zip(kinds, args)],
        out_specs=[whole(v) for v in out_shape],
        compiler_params=pltpu.CompilerParams(vmem_limit_bytes=FUSED_LIMIT),
        cost_estimate=cost(0, 20 << 20),
        name="finish",
    )(*args)


def local(
    tokens,
    seq_len,
    norm1_gain,
    norm1_bias,
    f1_weight,
    f1_bias,
    f2_weight,
    f2_bias,
    value_weight,
    out_weight,
    norm2_gain,
    norm2_bias,
    up_weight,
    up_bias,
    down_weight,
    down_bias,
    out_grad,
):
    members = lax.axis_size("head")
    vt = value_weight.T
    (
        xs, n1t, hid, slope, prob, valt, mgt, fterms, res_grad, residual, down_y, up_y, ow_y, upb,
        sums2,
    ) = front(
        seq_len, tokens, out_grad, norm1_gain, norm1_bias, norm2_gain, norm2_bias, up_bias, f1_bias,
        f2_bias, vt, f1_weight, f2_weight, out_weight, up_weight, down_weight,
    )
    (
        result, input_grad, ow_parts, down_parts, up_parts, f1_parts, f2_parts, val_parts, small,
    ) = back(
        seq_len, upb, sums2, norm1_gain, down_bias, vt, hid, slope, prob, n1t, valt, mgt,
        f1_weight, f2_weight, xs, fterms, down_y, up_y, ow_y, residual, res_grad,
    )
    (
        result, input_grad, f1b_all, f2b_all, upb_all, down_piece, up_piece, out_piece, f1_piece,
        f2_piece, value_piece, gain1_g, bias1_g, gain2_g, bias2_g, downb_g,
    ) = finish(
        members, result, input_grad, small, down_parts, up_parts, ow_parts, f1_parts, f2_parts,
        val_parts,
    )
    return (
        result,
        input_grad,
        gain1_g,
        bias1_g,
        f1_piece,
        f1b_all,
        f2_piece,
        f2b_all,
        value_piece,
        out_piece,
        gain2_g,
        bias2_g,
        up_piece,
        upb_all,
        down_piece.T,
        downb_g,
    )


def solution(mesh):
    placed = (
        P(("dp", "head"), None),
        P("dp"),
        P(),
        P(),
        P("head", None, None),
        P("head", None),
        P("head", None, None),
        P("head", None),
        P(None, "head"),
        P(),
        P(),
        P(),
        P(None, "head"),
        P("head"),
        P("head", None),
        P(),
        P(("dp", "head"), None),
    )
    return jax.shard_map(
        local,
        mesh=mesh,
        in_specs=placed,
        out_specs=(
            P(("dp", "head"), None),
            P(("dp", "head"), None),
            P(),
            P(),
            P("head", "dp", None),
            P(),
            P("head", "dp", None),
            P(),
            P("dp", "head"),
            P("dp", None),
            P(),
            P(),
            P("dp", "head"),
            P(),
            P("head", "dp"),
            P(),
        ),
        check_vma=False,
    )
```

```python
import types

import jax
import jax.numpy as jnp
from jax import lax
from jax.experimental import pallas as pl
from jax.experimental.pallas import tpu as pltpu
from jax.sharding import PartitionSpec as P

F32 = jnp.float32
BF16 = jnp.bfloat16
BLOCK = 128
FUSED_LIMIT = 63 << 20


def mm(a, b):
    return lax.dot_general(a, b, (((1,), (0,)), ((), ())), preferred_element_type=F32)


def mm_nt(a, b):
    return lax.dot_general(a, b, (((1,), (1,)), ((), ())), preferred_element_type=F32)


def mm_tn(a, b):
    return lax.dot_general(a, b, (((0,), (0,)), ((), ())), preferred_element_type=F32)


def standardize(values):
    centred = values - jnp.mean(values, -1, keepdims=True)
    inv_std = lax.rsqrt(jnp.mean(centred * centred, -1, keepdims=True) + 1e-05)
    return centred * inv_std, inv_std


def norm_back(grad_out, scaled, inv_std, gain):
    grad_scaled = grad_out * gain
    centre_mean = jnp.mean(grad_scaled, -1, keepdims=True)
    cross_mean = jnp.mean(grad_scaled * scaled, -1, keepdims=True)
    return inv_std * (grad_scaled - centre_mean - scaled * cross_mean)


def silu_and_slope(pre_val):
    sigma = 0.5 + 0.5 * jnp.tanh(0.5 * pre_val)
    gated = pre_val * sigma
    return gated, sigma + gated * (1.0 - sigma)


def add_low(a, b):
    return (a.astype(F32) + b.astype(F32)).astype(BF16)


def cost(macs, bytes_accessed):
    return pl.CostEstimate(flops=2 * macs, bytes_accessed=bytes_accessed, transcendentals=0)


def store_shards(both, acc, lanes=slice(None), far_first=False):
    _, count, depth, _ = both.shape
    me = lax.axis_index("dp")
    for d in range(2 * count):
        parity = jnp.bitwise_xor(me % 2, d % 2)
        other = jnp.bitwise_xor(me // 2, d // 2)
        gray = jnp.bitwise_xor(other, other // 2)
        bits = [gray // 2**i % 2 for i in range(len(masks(count)))]
        bits = bits + [parity] if far_first else [parity] + bits
        place = 0
        for bit in bits[1:]:
            place = 2 * place + bit
        both[bits[0], place] = acc[d * depth : (d + 1) * depth, lanes].astype(BF16)


def shard_shape(width, lanes):
    members = lax.axis_size("dp")
    return jax.ShapeDtypeStruct((2, members // 2, width // members, lanes), BF16)


class Wires:
    def __init__(self, send, recv):
        self.send, self.recv, self.used = send, recv, 0
        self.all = []

    def remote(self, src, dst, axis, step):
        index = self.used
        self.used += 1
        move = pltpu.make_async_remote_copy(
            src_ref=src,
            dst_ref=dst,
            send_sem=self.send.at[index],
            recv_sem=self.recv.at[index],
            device_id={axis: jnp.bitwise_xor(lax.axis_index(axis), step)},
            device_id_type=pl.DeviceIdType.MESH,
        )
        self.all.append(move)
        return move


def masks(count):
    found = [1]
    while 2 ** (len(found) + 1) <= count:
        found.append(2 * found[-1] + 1)
    return found


class Shards:
    def __init__(self, wires, keep, send, got, out, own_sem, load_sem, far_first=False):
        self.keep, self.got, self.out, self.load_sem = keep, got, out, load_sem
        self.count = keep.shape[0]
        order = [2 * mask for mask in masks(self.count)]
        order = order + [1] if far_first else [1] + order
        self.first = None if send is None else wires.remote(send, got, "dp", order[0])
        self.steps = []
        size = self.count
        for step in order[1:]:
            size //= 2
            part = pl.ds(size, size)
            self.steps.append((size, wires.remote(keep.at[part], out.at[part], "dp", step)))
        self.own = pltpu.make_async_copy(keep.at[0], out.at[0], own_sem)

    def start(self):
        self.first.start()

    def add(self, size):
        for k in range(size):
            self.keep[k] = add_low(self.keep[k], self.got[k])

    def second(self):
        if self.first is not None:
            self.first.wait_recv()
            self.add(self.count)
        self.steps[0][1].start()

    def third(self):
        for (size, move), (_, after) in zip(self.steps, self.steps[1:]):
            move.wait_recv()
            part = pl.ds(0, size)
            copy = pltpu.make_async_copy(
                self.out.at[pl.ds(size, size)], self.got.at[part], self.load_sem
            )
            copy.start()
            copy.wait()
            self.add(size)
            after.start()
        self.own.start()

    def finish(self):
        self.steps[-1][1].wait_recv()
        self.own.wait()


def add_got(keep, got):
    for k in range(keep.shape[0]):
        keep[k] = add_low(keep[k], got[k])


def greet(axes):
    barrier = pltpu.get_barrier_semaphore()
    for axis, step in axes:
        pl.semaphore_signal(
            barrier,
            1,
            device_id={axis: jnp.bitwise_xor(lax.axis_index(axis), step)},
            device_id_type=pl.DeviceIdType.MESH,
        )
    pl.semaphore_wait(barrier, len(axes))


def partners(far):
    over_dp = [1] + [2 * mask for mask in masks(lax.axis_size("dp") // 2) if far]
    return [("head", s) for s in range(1, lax.axis_size("head"))] + [("dp", s) for s in over_dp]


FRONT_IN = (
    "lens", "x", "og", "gain1", "bias1", "gain2", "bias2", "upb", "f1b", "f2b", "vt", "f1", "f2",
    "ow", "up", "down",
)
FRONT_OUT = (
    "xs_o", "n1t_o", "hid_o", "slope_o", "prob_o", "valt_o", "mgt_o", "f_o", "rg_o", "res_o",
    "down_o", "up_o", "ow_o", "upb_sum", "sums",
)
FRONT_SCRATCH = (
    "xs", "n1", "n1t", "big", "f2v", "hidb", "slopeb", "probb", "valt", "attt", "owv", "upv",
    "downv", "ogs", "n2s", "pug", "near1", "near3", "crossb", "crossr", "fterms", "res", "mgts",
    "acc", "ohalf", "osent", "ogot", "dboth", "dgot", "uboth", "oboth", "send", "recv",
    "load", "spill", "store",
)


def flat_row(ref):
    return ref[...].reshape(1, -1)


def split_prob(parts, length, longest, b, zero):
    is_full = length == longest
    is_half = length == longest // 2
    for c in range(len(parts)):
        half = parts[c % 2] if c // 2 == b // 2 else zero
        quarter = parts[0] if c == b else zero
        yield c, jnp.where(is_full, parts[c], jnp.where(is_half, half, quarter))


def cells(row):
    return [row[:, c : c + BLOCK] for c in range(0, row.shape[1], BLOCK)]


def front_kernel(*refs):
    r = types.SimpleNamespace(**dict(zip(FRONT_IN + FRONT_OUT + FRONT_SCRATCH, refs)))
    r.low = r.n1
    r.terms = r.xs
    slabs, rows, width = r.xs.shape
    heads, _, longest = r.f2v.shape
    depth = r.valt.shape[1]
    dim = depth // heads
    half = rows // 2
    blocks = rows // BLOCK
    me = lax.axis_index("head")

    w = Wires(r.send, r.recv)
    down_first = w.remote(r.dboth.at[1], r.dgot, "dp", 1)

    def remote(src, dst, step):
        return w.remote(src, dst, "head", step)

    def cut(c):
        return pl.ds(c * half, half)

    def share(step):
        return pl.ds(pl.multiple_of(jnp.bitwise_xor(me, step) * depth, depth), depth)

    my_rows = share(0)
    r.mgt = r.n1t.at[0]
    moves = {
        "x1": remote(r.x, r.xs.at[1], 1),
        "x2": remote(r.x, r.xs.at[2], 2),
        "x3": remote(r.xs.at[2], r.xs.at[3], 1),
        "o1": remote(r.og, r.ogs.at[1], 1),
        "o2": remote(r.og, r.ogs.at[2], 2),
        "o3": remote(r.ogs.at[2], r.ogs.at[3], 1),
        "t1": remote(r.terms.at[1], r.near1, 1),
    }
    columns = remote(r.osent, r.ogot, 1)
    near, far, onward = [], [], []
    for j in range(slabs):
        near.append(remote(r.attt.at[j, my_rows], r.attt.at[j ^ 1, my_rows], 1))
        far.append(remote(r.attt.at[j, my_rows], r.attt.at[j ^ 2, my_rows], 2))
        onward.append(remote(r.attt.at[j, share(2)], r.attt.at[j ^ 1, share(2)], 1))
    for j in range(1, slabs):
        moves[f"g{j}"] = remote(r.mgt.at[share(j)], r.mgts.at[j], j)
    for c in range(2):
        part = cut(c)
        moves[f"t3{c}"] = remote(r.terms.at[3, part], r.near3.at[part], 1)
        moves[f"c{c}"] = remote(r.crossb.at[part], r.crossr.at[part], 2)

    def f1_load(h):
        rows_of = pl.ds(pl.multiple_of(h * width, width), width)
        return pltpu.make_async_copy(r.f1.at[h], r.big.at[rows_of], r.load.at[1 + 2 * h])

    def f2_load(h):
        return pltpu.make_async_copy(r.f2.at[h], r.f2v.at[h], r.load.at[2 + 2 * h])

    loads = [pltpu.make_async_copy(r.x, r.xs.at[0], r.load.at[0])]
    for h in range(heads):
        loads += [f1_load(h), f2_load(h)]
    base = 1 + 2 * heads
    late = [
        pltpu.make_async_copy(r.ow, r.owv, r.load.at[base]),
        pltpu.make_async_copy(r.up, r.upv, r.load.at[base + 1]),
        pltpu.make_async_copy(r.down, r.downv, r.load.at[base + 2]),
        pltpu.make_async_copy(r.og, r.ogs.at[0], r.load.at[base + 3]),
    ]
    for copy in loads:
        copy.start()
    greet(partners(False))
    moves["x2"].start()
    moves["x1"].start()
    for copy in late:
        copy.start()
    loads[0].wait()

    def spills(j, h, slot):
        return [
            pltpu.make_async_copy(r.hidb.at[slot], r.hid_o.at[j, h], r.spill.at[slot, 0]),
            pltpu.make_async_copy(r.slopeb.at[slot], r.slope_o.at[j, h], r.spill.at[slot, 1]),
            pltpu.make_async_copy(r.probb.at[slot], r.prob_o.at[j, h], r.spill.at[slot, 2]),
        ]

    def slab_step(j, carry):
        @pl.when(j == 1)
        def _():
            moves["x1"].wait_recv()

        @pl.when(j == 2)
        def _():
            moves["x2"].wait_recv()
            moves["x3"].start()
            moves["o2"].start()
            moves["o1"].start()

        @pl.when(j == 3)
        def _():
            moves["x3"].wait_recv()
            for k in range(2):
                far[k].wait_recv()
                onward[k ^ 2].start()

        scaled, _ = standardize(r.xs[j].astype(F32))
        low = (scaled * flat_row(r.gain1) + flat_row(r.bias1)).astype(BF16)
        r.n1[...] = low
        r.n1t[j] = low.T
        r.valt[j] = mm(r.vt[...], r.n1t[j]).astype(BF16)

        def head_step(h, carry):
            turn = j * heads + h
            slot = turn % 2

            @pl.when(j == 0)
            def _():
                f1_load(h).wait()
                f2_load(h).wait()

            @pl.when(turn >= 2)
            def _():
                for copy in spills(j, h, slot):
                    copy.wait()

            first = jnp.bitwise_xor(me, j) * blocks
            column = lax.broadcasted_iota(jnp.int32, (BLOCK, longest), 1)
            zero = jnp.zeros((BLOCK, BLOCK), F32)
            f1_rows = pl.ds(pl.multiple_of(h * width, width), width)
            for c in range(2):
                part = slice(c * half, (c + 1) * half)
                gated, slope = silu_and_slope(mm(r.n1[part], r.big[f1_rows]) + r.f1b[pl.ds(h, 1)])
                hidden = gated.astype(BF16)
                r.hidb[slot, part] = hidden
                r.slopeb[slot, part] = slope.astype(BF16)
                scores = mm(hidden, r.f2v[h]) + r.f2b[pl.ds(h, 1)]
                for i in range(half // BLOCK):
                    b = c * (half // BLOCK) + i
                    length = r.lens[first + b]
                    own = scores[i * BLOCK : (i + 1) * BLOCK]
                    keep = column < length
                    top = jnp.max(jnp.where(keep, own, -3.0e38), -1, keepdims=True)
                    exp_val = jnp.where(keep, jnp.exp(own - top), 0.0)
                    prob = exp_val * (1.0 / jnp.sum(exp_val, -1, keepdims=True))
                    for k, cell in split_prob(cells(prob), length, longest, b, zero):
                        r.probb[
                            slot, b * BLOCK : (b + 1) * BLOCK, k * BLOCK : (k + 1) * BLOCK
                        ] = cell.astype(BF16)
            own_rows = pl.ds(pl.multiple_of(h * dim, dim), dim)
            mixed = mm_nt(r.valt[j, own_rows], r.probb[slot])
            place = pl.ds(pl.multiple_of(me * depth + h * dim, dim), dim)
            r.attt[j, place] = mixed.astype(BF16)
            for copy in spills(j, h, slot):
                copy.start()
            return carry

        lax.fori_loop(0, heads, head_step, 0)
        for k in range(slabs):

            @pl.when(j == k)
            def _(k=k):
                far[k].start()
                near[k].start()

        return carry

    lax.fori_loop(0, slabs, slab_step, 0)
    stores = [
        pltpu.make_async_copy(r.xs, r.xs_o, r.store.at[0]),
        pltpu.make_async_copy(r.n1t, r.n1t_o, r.store.at[1]),
        pltpu.make_async_copy(r.valt, r.valt_o, r.store.at[2]),
    ]
    for copy in stores:
        copy.start()
    for k in (2, 3):
        near[k].wait_recv()
        onward[k].wait_recv()
    for copy in late:
        copy.wait()
    for copy in stores:
        copy.wait()
    stores = []
    sent = moves["x3"]
    sent.wait_send()

    def residual_step(j, carry):
        residual = r.xs[j].astype(F32) + mm_tn(r.attt[j], r.owv[...])

        @pl.when(j == 0)
        def _():
            r.res[...] = residual

        scaled, _ = standardize(residual)
        r.n2s[j] = (scaled * flat_row(r.gain2) + flat_row(r.bias2)).astype(BF16)
        return carry

    lax.fori_loop(2, 4, residual_step, 0)
    moves["o2"].wait_recv()
    moves["o3"].start()

    def ffn_step(u, carry):
        j = jnp.where(u < 4, 2 + u % 2, (u - 4) // 2)
        c = jnp.where(u < 4, u // 2, u % 2)

        @pl.when(u == 1)
        def _():
            moves["o3"].wait_recv()

        @pl.when(u == 2)
        def _():
            for k in (2, 3):
                far[k].wait_recv()
                onward[k ^ 2].start()

        @pl.when(u == 4)
        def _():
            for k in (0, 1):
                near[k].wait_recv()
                onward[k].wait_recv()
            moves["o1"].wait_recv()
            lax.fori_loop(0, 2, residual_step, 0)

        part = pl.ds(pl.multiple_of(c * half, half), half)
        gated, slope = silu_and_slope(mm(r.n2s[j, part], r.upv[...]) + flat_row(r.upb))
        act = gated.astype(BF16)
        r.big[pl.ds(pl.multiple_of(j * rows + c * half, half), half)] = act
        pug = (mm_nt(r.ogs[j, part], r.downv[...]) * slope).astype(BF16)
        r.pug[j, part] = pug
        r.terms[j, part] = mm_nt(pug, r.upv[...]).astype(BF16)
        r.fterms[j, part] = mm(act, r.downv[...]).astype(BF16)

        for c in range(2):

            @pl.when(u == 2 * c + 1)
            def _(c=c):
                moves[f"t3{c}"].start()

            @pl.when(u == 2 * c + 2)
            def _(c=c):
                moves[f"t3{c}"].wait_recv()
                part = cut(c)
                r.crossb[part] = add_low(r.terms[2, part], r.near3[part])
                moves[f"c{c}"].start()

        @pl.when(u == 7)
        def _():
            moves["t1"].start()

        return carry

    lax.fori_loop(0, 8, ffn_step, 0)
    flat = (slabs * rows, width)
    r.acc[...] = mm_tn(r.ogs[...].reshape(flat), r.big[0 : slabs * rows])
    store_shards(r.dboth, r.acc)
    down_first.start()
    stores = [
        pltpu.make_async_copy(r.fterms, r.f_o, r.store.at[5]),
        pltpu.make_async_copy(r.res, r.res_o, r.store.at[6]),
    ]
    for copy in stores:
        copy.start()
    cot = r.ogs[0].astype(F32)
    r.sums[2:3] = jnp.sum(cot, 0, keepdims=True)
    moves["t1"].wait_recv()
    moves["c0"].wait_recv()
    moves["c1"].wait_recv()

    grad = r.terms[0].astype(F32) + r.near1[...].astype(F32) + r.crossr[...].astype(F32)
    scaled, inv_std = standardize(r.res[...])
    res_grad = cot + norm_back(grad, scaled, inv_std, flat_row(r.gain2))
    r.rg_o[...] = res_grad
    r.low[...] = res_grad.astype(BF16)
    r.sums[0:1] = jnp.sum(grad * scaled, 0, keepdims=True)
    r.sums[1:2] = jnp.sum(grad, 0, keepdims=True)
    r.mgt[...] = mm_nt(r.owv[...], r.low[...]).astype(BF16)
    for j in (2, 3, 1):
        moves[f"g{j}"].start()
        r.mgts[0] = r.mgt[my_rows]
    mixed = r.attt[0]
    r.acc[...] = mm(mixed, r.low[...])
    span = width // 2
    mine = pl.ds(pl.multiple_of(me % 2 * span, BLOCK), span)
    theirs = pl.ds(pl.multiple_of((1 - me % 2) * span, BLOCK), span)
    r.osent[...] = r.acc[:, theirs].astype(BF16)
    columns.start()
    r.ohalf[...] = r.acc[:, mine]
    r.acc[...] = mm_tn(r.n2s[...].reshape(flat), r.pug[...].reshape(flat))
    store_shards(r.uboth, r.acc)
    r.upb_sum[...] = jnp.sum(r.pug[...].reshape(flat).astype(F32), 0, keepdims=True)
    columns.wait_recv()
    r.ohalf[...] += r.ogot[...].astype(F32)
    store_shards(r.oboth, r.ohalf)
    more = [
        pltpu.make_async_copy(r.uboth, r.up_o, r.store.at[4]),
        pltpu.make_async_copy(r.oboth, r.ow_o, r.store.at[7]),
    ]
    for copy in more:
        copy.start()
    stores += more
    for j in range(1, slabs):
        moves[f"g{j}"].wait_recv()
    stores.append(pltpu.make_async_copy(r.mgts, r.mgt_o, r.store.at[8]))
    stores[-1].start()
    down_first.wait_recv()
    add_got(r.dboth.at[0], r.dgot)
    stores.append(pltpu.make_async_copy(r.dboth.at[0], r.down_o, r.store.at[9]))
    stores[-1].start()
    for copy in stores:
        copy.wait()
    total = slabs * heads
    for turn in (total - 2, total - 1):
        for copy in spills(turn // heads, turn % heads, turn % 2):
            copy.wait()
    for move in w.all:
        if move is not sent:
            move.wait_send()


def front(lens, x, og, gain1, bias1, gain2, bias2, upb, f1b, f2b, vt, f1, f2, ow, up, down):
    rows, width = x.shape
    heads, _, longest = f2.shape
    depth = vt.shape[0]
    units = up.shape[1]
    slabs = lax.axis_size("head")
    osh = shard_shape(width, width // 2)
    dsh = shard_shape(width, units)
    group = (slabs, rows, width)
    anywhere = pl.BlockSpec(memory_space=pl.ANY)
    vmem = pl.BlockSpec(memory_space=pltpu.VMEM)
    low = lambda *s: jax.ShapeDtypeStruct(s, BF16)
    wide = lambda *s: jax.ShapeDtypeStruct(s, F32)
    out_shape = [
        low(*group),
        low(slabs, width, rows),
        low(slabs, heads, rows, width),
        low(slabs, heads, rows, width),
        low(slabs, heads, rows, longest),
        low(slabs, depth, rows),
        low(slabs, depth, rows),
        low(*group),
        wide(rows, width),
        wide(rows, width),
        jax.ShapeDtypeStruct(dsh.shape[1:], BF16),
        dsh,
        osh,
        wide(1, units),
        wide(3, width),
    ]
    out_specs = [vmem if n in ("rg_o", "upb_sum", "sums") else anywhere for n in FRONT_OUT]
    vl = lambda *s: pltpu.VMEM(s, BF16)
    vf = lambda *s: pltpu.VMEM(s, F32)
    scratch = dict(
        xs=vl(*group),
        n1=vl(rows, width),
        n1t=vl(slabs, width, rows),
        big=vl(max(heads * width, slabs * rows), width),
        f2v=vl(heads, width, longest),
        hidb=vl(2, rows, width),
        slopeb=vl(2, rows, width),
        probb=vl(2, rows, longest),
        valt=vl(slabs, depth, rows),
        attt=vl(slabs, width, rows),
        owv=vl(width, width),
        upv=vl(width, units),
        downv=vl(units, width),
        ogs=vl(*group),
        n2s=vl(*group),
        pug=vl(slabs, rows, units),
        near1=vl(rows, width),
        near3=vl(rows, width),
        crossb=vl(rows, width),
        crossr=vl(rows, width),
        fterms=vl(*group),
        res=vf(rows, width),
        mgts=vl(slabs, depth, rows),
        acc=vf(width, width),
        ohalf=vf(width, width // 2),
        osent=vl(width, width // 2),
        ogot=vl(width, width // 2),
        dboth=vl(*dsh.shape),
        dgot=vl(*dsh.shape[1:]),
        uboth=vl(*dsh.shape),
        oboth=vl(*osh.shape),
        send=pltpu.SemaphoreType.DMA((12 + 4 * slabs,)),
        recv=pltpu.SemaphoreType.DMA((12 + 4 * slabs,)),
        load=pltpu.SemaphoreType.DMA((5 + 2 * heads,)),
        spill=pltpu.SemaphoreType.DMA((2, 3)),
        store=pltpu.SemaphoreType.DMA((10,)),
    )
    smem = pl.BlockSpec(memory_space=pltpu.SMEM)
    return pl.pallas_call(
        front_kernel,
        out_shape=out_shape,
        in_specs=[smem] + [anywhere] * 2 + [vmem] * 8 + [anywhere] * 5,
        out_specs=out_specs,
        scratch_shapes=[scratch[n] for n in FRONT_SCRATCH],
        compiler_params=pltpu.CompilerParams(
            collective_id=0, has_side_effects=True, vmem_limit_bytes=FUSED_LIMIT
        ),
        cost_estimate=cost(
            slabs * rows * width * (heads * (width + longest) + 6 * units), 60 << 20
        ),
        name="front",
    )(lens, x, og, gain1, bias1, gain2, bias2, upb, f1b, f2b, vt, f1, f2, ow, up, down)


BACK_IN = (
    "lens", "upb_sum", "sums", "gain1", "downb", "vt", "hid", "slope", "prob", "n1t", "valt", "mgt",
    "f1", "f2", "xs", "fterms", "down", "up", "ow", "res", "rg",
)
BACK_OUT = ("result", "input", "ow_o", "down_o", "up_o", "f1_o", "f2_o", "val_o", "small_o")
BACK_SCRATCH = (
    "n1tv", "valtv", "mgtv", "vgt", "f1v", "f2v", "terms", "probb", "sg", "pog",
    "acc1", "acc2", "acc3", "xb", "near3", "near1", "crossr", "fb", "fnear3",
    "fnear1", "fcrossr", "rgv", "dk", "dgot", "uk", "ugot", "ok", "ogot", "oall", "olow", "aboth",
    "agot", "bboth", "bgot", "vboth", "vgot", "small", "small_in", "send",
    "recv", "load", "fetch", "store",
)


def back_kernel(*refs):
    r = types.SimpleNamespace(**dict(zip(BACK_IN + BACK_OUT + BACK_SCRATCH, refs)))
    r.crossb = r.terms.at[3]
    r.resv = r.acc1.at[pl.ds(0, r.rgv.shape[0])]
    slabs, heads, rows, width = r.pog.shape
    longest = r.probb.shape[2]
    depth = r.vgt.shape[1]
    dim = depth // heads
    blocks = rows // BLOCK
    count = r.ok.shape[0]
    me = lax.axis_index("head")
    turns = slabs * heads
    w = Wires(r.send, r.recv)
    sems = iter(range(6 * heads + 8))

    def shards(keep, send, got, out, far_first=False):
        own_sem, load_sem = r.store.at[next(sems)], r.store.at[next(sems)]
        return Shards(w, keep, send, got, out, own_sem, load_sem, far_first)

    down_group = shards(r.dk, None, r.dgot, r.down_o)
    up_group = shards(r.uk, r.up.at[1], r.ugot, r.up_o)
    out_group = shards(r.ok, r.ow.at[1], r.ogot, r.oall)
    out_heads = [w.remote(r.olow, r.ow_o.at[j], "head", j) for j in range(1, slabs)]
    f1_group, f2_group = [], []
    for h in range(heads):
        both = r.bboth.at[h]
        f2_group.append(shards(both.at[0], both.at[1], r.bgot.at[h], r.f2_o.at[h]))
        for i in range(2):
            both = r.aboth.at[h, i]
            f1_group.append(shards(both.at[0], both.at[1], r.agot.at[h, i], r.f1_o.at[h, i]))
    val_group = shards(r.vboth.at[0], r.vboth.at[1], r.vgot, r.val_o)
    fterm1 = w.remote(r.fterms.at[1], r.fnear1, "head", 1)
    fterm3 = w.remote(r.fterms.at[3], r.fnear3, "head", 1)
    fcross = w.remote(r.fb, r.fcrossr, "head", 2)
    term1 = w.remote(r.terms.at[1], r.near1, "head", 1)
    term3 = w.remote(r.terms.at[3], r.near3, "head", 1)
    cross = w.remote(r.crossb, r.crossr, "head", 2)
    steps = [1] + [2 * mask for mask in masks(count)]
    small_steps = [
        w.remote(r.small.at[i], r.small_in.at[i], "dp", step) for i, step in enumerate(steps)
    ]
    small_last = r.small.at[len(steps)]
    small_x = [
        w.remote(small_last, r.small_o.at[j], "head", j) for j in range(1, slabs)
    ]
    base = 6 * heads + 8
    own_low = pltpu.make_async_copy(r.olow, r.ow_o.at[0], r.store.at[base])
    own_small = pltpu.make_async_copy(small_last, r.small_o.at[0], r.store.at[base + 1])

    def load(index, src, dst):
        return pltpu.make_async_copy(src, dst, r.load.at[index])

    loads = [
        load(0, r.mgt, r.mgtv),
        load(1, r.valt, r.valtv),
        load(2, r.f2, r.f2v),
        load(3, r.n1t, r.n1tv),
        load(4, r.down, r.dk),
        load(5, r.fterms.at[2], r.fb),
        load(6, r.f1, r.f1v),
        load(7, r.xs.at[3], r.xb),
        load(9, r.rg, r.rgv),
        load(10, r.up.at[0], r.uk),
        load(11, r.ow.at[0], r.ok),
    ]

    def fetches(turn):
        h, j, slot = turn // slabs, turn % slabs, turn % 2
        return [
            pltpu.make_async_copy(r.prob.at[j, h], r.probb.at[slot], r.fetch.at[slot, 0]),
            pltpu.make_async_copy(r.slope.at[j, h], r.terms.at[2 + slot], r.fetch.at[slot, 1]),
            pltpu.make_async_copy(r.hid.at[j, h], r.terms.at[slot], r.fetch.at[slot, 2]),
        ]

    for copy in loads[:2] + fetches(0) + loads[2:]:
        copy.start()
    greet(partners(True))
    up_group.start()
    out_group.start()
    fterm3.start()
    fterm1.start()
    r.small[0] = jnp.zeros(r.small.shape[1:], F32)
    r.small[0, 2 * heads : 2 * heads + 1] = r.upb_sum[...]
    r.small[0, 2 * heads + 3 : 2 * heads + 6] = r.sums[...]
    for copy in loads[:6]:
        copy.wait()
    down_group.second()

    def turn_step(turn, carry):
        h, j, slot = turn // slabs, turn % slabs, turn % 2
        for copy in fetches(turn):
            copy.wait()

        @pl.when(turn + 1 < turns)
        def _():
            for copy in fetches(turn + 1):
                copy.start()

        @pl.when(j == 0)
        def _():
            r.acc1[...] = jnp.zeros_like(r.acc1)
            r.acc2[...] = jnp.zeros_like(r.acc2)

        head_rows = pl.ds(pl.multiple_of(h * dim, dim), dim)
        mgt = r.mgtv[j, head_rows]
        r.vgt[j, head_rows] = mm(mgt, r.probb[slot]).astype(BF16)
        probs_grad = mm_tn(mgt, r.valtv[j, head_rows])
        first = jnp.bitwise_xor(me, j) * blocks
        zero = jnp.zeros((BLOCK, BLOCK), F32)
        for b in range(blocks):
            length = r.lens[first + b]
            own = slice(b * BLOCK, (b + 1) * BLOCK)
            prob = r.probb[slot, own].astype(F32)
            grad = probs_grad[own]
            inner = jnp.sum(prob * grad, -1, keepdims=True)
            parts = cells(prob * (grad - inner))
            is_full = length == longest
            is_half = length == longest // 2
            for c in range(blocks):
                half = parts[2 * (b // 2) + c] if c < 2 else zero
                quarter = parts[b] if c == 0 else zero
                cell = jnp.where(is_full, parts[c], jnp.where(is_half, half, quarter))
                r.sg[own, c * BLOCK : (c + 1) * BLOCK] = cell.astype(BF16)
        scores_grad = r.sg[...]
        row = pl.ds(h, 1)
        pog = (mm_nt(scores_grad, r.f2v[h]) * r.terms[2 + slot].astype(F32)).astype(BF16)
        r.pog[j, h] = pog
        r.small[0, row] += jnp.sum(pog.astype(F32), 0, keepdims=True)
        row = pl.ds(heads + h, 1)
        r.small[0, row, 0:longest] += jnp.sum(scores_grad.astype(F32), 0, keepdims=True)
        r.acc2[...] += mm_tn(r.terms[slot], scores_grad)
        r.acc1[...] += mm(r.n1tv[j], pog)

        for k in range(heads):

            @pl.when(turn == slabs * k + slabs - 1)
            def _(k=k):
                store_shards(r.bboth.at[k], r.acc2)
                if k < heads - 1:
                    f2_group[k].start()
                for i in range(2):
                    span = width // 2
                    store_shards(r.aboth.at[k, i], r.acc1, slice(i * span, (i + 1) * span))
                    if k < heads - 1:
                        f1_group[2 * k + i].start()

        @pl.when(turn == 1)
        def _():
            fterm3.wait_recv()
            r.fb[...] = add_low(r.fb[...], r.fnear3[...])
            fcross.start()

        @pl.when(turn == 2)
        def _():
            down_group.third()

        @pl.when(turn == 4)
        def _():
            for copy in loads[9:]:
                copy.wait()
            up_group.second()

        @pl.when(turn == 6)
        def _():
            out_group.second()

        @pl.when(turn == 7)
        def _():
            up_group.third()

        @pl.when(turn == 8)
        def _():
            f2_group[0].second()

        @pl.when(turn == 9)
        def _():
            out_group.third()

        @pl.when(turn == 10)
        def _():
            f1_group[0].second()

        @pl.when(turn == 11)
        def _():
            f2_group[0].third()
            out_group.finish()
            r.olow[...] = (r.oall[0].astype(F32) + r.oall[1].astype(F32)).astype(BF16)
            for move in out_heads:
                move.start()
            own_low.start()

        return carry

    lax.fori_loop(0, turns, turn_step, 0)
    for copy in loads[6:8]:
        copy.wait()
    res_load = load(8, r.res, r.resv)
    res_load.start()

    def term_step(i, carry):
        j = slabs - 1 - i

        @pl.when(i > 0)
        def _():
            load(7, r.xs.at[j], r.xb).wait()

        term = mm_tn(r.vgt[j], r.vt[...])
        for h in range(heads):
            term += mm_nt(r.pog[j, h], r.f1v[h])
        low = term.astype(BF16)
        r.terms[j] = low
        wide = low.astype(F32)
        scaled, _ = standardize(r.xb[...].astype(F32))
        at = 2 * heads + 1
        r.small[0, at : at + 1] += jnp.sum(wide * scaled, 0, keepdims=True)
        r.small[0, at + 1 : at + 2] += jnp.sum(wide, 0, keepdims=True)

        @pl.when(i < slabs - 1)
        def _():
            load(7, r.xs.at[j - 1], r.xb).start()

        @pl.when(i == 0)
        def _():
            term3.start()
            f1_group[1].second()
            f1_group[0].third()

        @pl.when(i == 1)
        def _():
            term3.wait_recv()
            term3.wait_send()
            r.crossb[...] = add_low(r.terms[2], r.near3[...])
            cross.start()
            f1_group[1].third()

        @pl.when(i == 2)
        def _():
            term1.start()
            f2_group[1].second()

        return carry

    lax.fori_loop(0, slabs, term_step, 0)
    small_steps[0].start()
    f2_group[2].start()
    f1_group[4].start()
    f1_group[5].start()
    f1_group[2].second()
    f2_group[1].third()
    total = mm_nt(r.n1tv[0], r.vgt[0])
    for j in range(1, slabs):
        total += mm_nt(r.n1tv[j], r.vgt[j])
    r.acc3[...] = total
    store_shards(r.vboth, r.acc3)
    val_group.start()
    fcross.wait_send()
    own_fterm = load(12, r.fterms.at[0], r.fb)
    own_fterm.start()
    for copy in [res_load, loads[8], own_fterm]:
        copy.wait()
    fterm1.wait_recv()
    fcross.wait_recv()
    others = r.fnear1[...].astype(F32) + r.fcrossr[...].astype(F32)
    r.resv[...] += r.fb[...].astype(F32) + others + flat_row(r.downb)
    finals = [pltpu.make_async_copy(r.resv, r.result, r.store.at[base + 2])]
    finals[0].start()

    def small_step(i):
        small_steps[i].wait_recv()
        r.small[i + 1] = r.small[i] + r.small_in[i]
        for after in small_steps[i + 1 : i + 2] or small_x + [own_small]:
            after.start()

    f1_group[3].second()
    f1_group[2].third()
    small_step(0)
    term1.wait_recv()
    cross.wait_recv()
    grad = r.terms[0].astype(F32) + r.near1[...].astype(F32) + r.crossr[...].astype(F32)
    scaled, inv_std = standardize(r.xb[...].astype(F32))
    r.rgv[...] += norm_back(grad, scaled, inv_std, flat_row(r.gain1))
    finals.append(pltpu.make_async_copy(r.rgv, r.input, r.store.at[base + 3]))
    finals[1].start()
    small_step(1)
    f1_group[3].third()
    f2_group[2].second()
    for i in range(2, len(steps)):
        small_step(i)
    f1_group[4].second()
    f2_group[2].third()
    f1_group[5].second()
    f1_group[4].third()
    val_group.second()
    f1_group[5].third()
    val_group.third()
    for group in [down_group, up_group] + f2_group + f1_group + [val_group]:
        group.finish()
    for move in out_heads + small_x:
        move.wait_recv()
    for copy in finals + [own_low, own_small]:
        copy.wait()
    for move in w.all:
        if move is not term3 and move is not fcross:
            move.wait_send()


def low_shape(*shape):
    return jax.ShapeDtypeStruct(shape, BF16)


def wide_shape(*shape):
    return jax.ShapeDtypeStruct(shape, F32)


def back(*args):
    hid, f2, vt, ow = args[6], args[13], args[5], args[18]
    slabs, heads, rows, width = hid.shape
    longest = f2.shape[2]
    depth = vt.shape[0]
    _, count, part, span = ow.shape
    small = (2 * heads + 6 + 7) // 8 * 8
    low, wide = low_shape, wide_shape
    out_shape = [
        wide(rows, width),
        wide(rows, width),
        low(slabs, part, span),
        low(count, part, width),
        low(count, part, width),
        low(heads, 2, count, part, span),
        low(heads, count, part, longest),
        low(count, part, depth),
        wide(slabs, small, width),
    ]
    vl = lambda *s: pltpu.VMEM(s, BF16)
    vf = lambda *s: pltpu.VMEM(s, F32)
    steps = len(masks(count)) + 1
    moves = 2 * (slabs - 1) + (3 * heads + 5) * steps + 6
    scratch = dict(
        n1tv=vl(slabs, width, rows),
        valtv=vl(slabs, depth, rows),
        mgtv=vl(slabs, depth, rows),
        vgt=vl(slabs, depth, rows),
        f1v=vl(heads, width, width),
        f2v=vl(heads, width, longest),
        probb=vl(2, rows, longest),
        sg=vl(rows, longest),
        pog=vl(slabs, heads, rows, width),
        acc1=vf(width, width),
        acc2=vf(width, longest),
        acc3=vf(width, depth),
        xb=vl(rows, width),
        terms=vl(slabs, rows, width),
        near3=vl(rows, width),
        near1=vl(rows, width),
        crossr=vl(rows, width),
        fb=vl(rows, width),
        fnear3=vl(rows, width),
        fnear1=vl(rows, width),
        fcrossr=vl(rows, width),
        rgv=vf(rows, width),
        ok=vl(count, part, span),
        ogot=vl(count, part, span),
        oall=vl(count, part, span),
        olow=vl(part, span),
        dk=vl(count, part, width),
        dgot=vl(count // 2, part, width),
        uk=vl(count, part, width),
        ugot=vl(count, part, width),
        aboth=vl(heads, 2, 2, count, part, span),
        agot=vl(heads, 2, count, part, span),
        bboth=vl(heads, 2, count, part, longest),
        bgot=vl(heads, count, part, longest),
        vboth=vl(2, count, part, depth),
        vgot=vl(count, part, depth),
        small=vf(steps + 1, small, width),
        small_in=vf(steps, small, width),
        send=pltpu.SemaphoreType.DMA((moves,)),
        recv=pltpu.SemaphoreType.DMA((moves,)),
        load=pltpu.SemaphoreType.DMA((13,)),
        fetch=pltpu.SemaphoreType.DMA((2, 3)),
        store=pltpu.SemaphoreType.DMA((12 + 6 * heads,)),
    )
    smem = pl.BlockSpec(memory_space=pltpu.SMEM)
    anywhere = pl.BlockSpec(memory_space=pl.ANY)
    vmem = pl.BlockSpec(memory_space=pltpu.VMEM)
    return pl.pallas_call(
        back_kernel,
        out_shape=out_shape,
        in_specs=[smem] + [vmem] * 5 + [anywhere] * 15,
        out_specs=[anywhere] * len(out_shape),
        scratch_shapes=[scratch[n] for n in BACK_SCRATCH],
        compiler_params=pltpu.CompilerParams(
            collective_id=1, has_side_effects=True, vmem_limit_bytes=FUSED_LIMIT
        ),
        cost_estimate=cost(slabs * rows * width * heads * (3 * width + 2 * longest), 60 << 20),
        name="back",
    )(*args)


def finish_kernel(*refs):
    result, inp, small, down, up, ow, f1, f2, val = refs[:9]
    (
        result_o, input_o, f1b_o, f2b_o, upb_o, down_o, up_o, ow_o, f1_o, f2_o, val_o,
    ) = refs[9:20]
    shared = refs[20:25]
    result_o[...] = result[...]
    input_o[...] = inp[...]
    slabs = small.shape[0]
    heads = f1.shape[0]
    longest = f2.shape[3]
    me = lax.axis_index("head")
    for j in range(slabs):
        owner = jnp.bitwise_xor(me, j)
        units = small.shape[2]
        own = small[owner, 2 * heads : 2 * heads + 1]
        upb_o[j * units : (j + 1) * units] = own.reshape(units)
        for h in range(heads):
            f1b_o[pl.ds(owner * heads + h, 1)] = small[j, h : h + 1]
            f2b_o[pl.ds(owner * heads + h, 1)] = small[j, heads + h : heads + h + 1, 0:longest]
    first = 2 * heads + 1
    for i, ref in enumerate(shared):
        ref[...] = sum(small[j, first + i] for j in range(slabs))
    span = ow.shape[2]
    mine = pl.ds(pl.multiple_of(me % 2 * span, BLOCK), span)
    theirs = pl.ds(pl.multiple_of((1 - me % 2) * span, BLOCK), span)
    ow_o[:, mine] = sum(ow[j].astype(F32) for j in range(0, slabs, 2))
    ow_o[:, theirs] = sum(ow[j].astype(F32) for j in range(1, slabs, 2))
    total = lambda ref: ref[0].astype(F32) + ref[1].astype(F32)
    down_o[...] = total(down)
    up_o[...] = total(up)
    val_o[...] = total(val)
    for h in range(heads):
        for i in range(2):
            f1_o[h, :, i * span : (i + 1) * span] = total(f1.at[h, i])
        f2_o[h] = total(f2.at[h])


def finish(members, *args):
    f1, f2, val = args[6:]
    rows, width = args[0].shape
    heads, _, part, longest = f2.shape
    wide = wide_shape
    out_shape = [
        wide(rows, width),
        wide(rows, width),
        wide(members * heads, width),
        wide(members * heads, longest),
        wide(members * width),
        wide(part, width),
        wide(part, width),
        wide(part, width),
        wide(heads, part, width),
        wide(heads, part, longest),
        wide(part, val.shape[2]),
    ] + [wide(width)] * 5
    whole = lambda v: pl.BlockSpec(v.shape, lambda _: (0,) * v.ndim)
    pair = lambda v: pl.BlockSpec((2,) + v.shape[1:], lambda _: (0, 0, 0))
    heads_pair = lambda v: pl.BlockSpec((heads, 2) + v.shape[2:], lambda _: (0, 0, 0, 0))
    halves = lambda v: pl.BlockSpec((heads, 2, 2) + v.shape[3:], lambda _: (0,) * 5)
    kinds = [whole] * 3 + [pair] * 2 + [whole, halves, heads_pair, pair]
    return pl.pallas_call(
        finish_kernel,
        grid=(1,),
        out_shape=out_shape,
        in_specs=[kind(v) for kind, v in zip(kinds, args)],
        out_specs=[whole(v) for v in out_shape],
        compiler_params=pltpu.CompilerParams(vmem_limit_bytes=FUSED_LIMIT),
        cost_estimate=cost(0, 20 << 20),
        name="finish",
    )(*args)


def local(
    tokens,
    seq_len,
    norm1_gain,
    norm1_bias,
    f1_weight,
    f1_bias,
    f2_weight,
    f2_bias,
    value_weight,
    out_weight,
    norm2_gain,
    norm2_bias,
    up_weight,
    up_bias,
    down_weight,
    down_bias,
    out_grad,
):
    members = lax.axis_size("head")
    vt = value_weight.T
    (
        xs, n1t, hid, slope, prob, valt, mgt, fterms, res_grad, residual, down_y, up_y, ow_y, upb,
        sums2,
    ) = front(
        seq_len, tokens, out_grad, norm1_gain, norm1_bias, norm2_gain, norm2_bias, up_bias, f1_bias,
        f2_bias, vt, f1_weight, f2_weight, out_weight, up_weight, down_weight,
    )
    (
        result, input_grad, ow_parts, down_parts, up_parts, f1_parts, f2_parts, val_parts, small,
    ) = back(
        seq_len, upb, sums2, norm1_gain, down_bias, vt, hid, slope, prob, n1t, valt, mgt,
        f1_weight, f2_weight, xs, fterms, down_y, up_y, ow_y, residual, res_grad,
    )
    (
        result, input_grad, f1b_all, f2b_all, upb_all, down_piece, up_piece, out_piece, f1_piece,
        f2_piece, value_piece, gain1_g, bias1_g, gain2_g, bias2_g, downb_g,
    ) = finish(
        members, result, input_grad, small, down_parts, up_parts, ow_parts, f1_parts, f2_parts,
        val_parts,
    )
    return (
        result,
        input_grad,
        gain1_g,
        bias1_g,
        f1_piece,
        f1b_all,
        f2_piece,
        f2b_all,
        value_piece,
        out_piece,
        gain2_g,
        bias2_g,
        up_piece,
        upb_all,
        down_piece.T,
        downb_g,
    )


def solution(mesh):
    placed = (
        P(("dp", "head"), None),
        P("dp"),
        P(),
        P(),
        P("head", None, None),
        P("head", None),
        P("head", None, None),
        P("head", None),
        P(None, "head"),
        P(),
        P(),
        P(),
        P(None, "head"),
        P("head"),
        P("head", None),
        P(),
        P(("dp", "head"), None),
    )
    return jax.shard_map(
        local,
        mesh=mesh,
        in_specs=placed,
        out_specs=(
            P(("dp", "head"), None),
            P(("dp", "head"), None),
            P(),
            P(),
            P("head", "dp", None),
            P(),
            P("head", "dp", None),
            P(),
            P("dp", "head"),
            P("dp", None),
            P(),
            P(),
            P("dp", "head"),
            P(),
            P("head", "dp"),
            P(),
        ),
        check_vma=False,
    )
```

```python
import types

import jax
import jax.numpy as jnp
from jax import lax
from jax.experimental import pallas as pl
from jax.experimental.pallas import tpu as pltpu
from jax.sharding import PartitionSpec as P

F32 = jnp.float32
BF16 = jnp.bfloat16
BLOCK = 128
FUSED_LIMIT = 63 << 20


def mm(a, b):
    return lax.dot_general(a, b, (((1,), (0,)), ((), ())), preferred_element_type=F32)


def mm_nt(a, b):
    return lax.dot_general(a, b, (((1,), (1,)), ((), ())), preferred_element_type=F32)


def mm_tn(a, b):
    return lax.dot_general(a, b, (((0,), (0,)), ((), ())), preferred_element_type=F32)


def standardize(values):
    centred = values - jnp.mean(values, -1, keepdims=True)
    inv_std = lax.rsqrt(jnp.mean(centred * centred, -1, keepdims=True) + 1e-05)
    return centred * inv_std, inv_std


def norm_back(grad_out, scaled, inv_std, gain):
    grad_scaled = grad_out * gain
    centre_mean = jnp.mean(grad_scaled, -1, keepdims=True)
    cross_mean = jnp.mean(grad_scaled * scaled, -1, keepdims=True)
    return inv_std * (grad_scaled - centre_mean - scaled * cross_mean)


def silu_and_slope(pre_val):
    sigma = 0.5 + 0.5 * jnp.tanh(0.5 * pre_val)
    gated = pre_val * sigma
    return gated, sigma + gated * (1.0 - sigma)


def add_low(a, b):
    return (a.astype(F32) + b.astype(F32)).astype(BF16)


def cost(macs, bytes_accessed):
    return pl.CostEstimate(flops=2 * macs, bytes_accessed=bytes_accessed, transcendentals=0)


def store_shards(both, acc, lanes=slice(None), far_first=False):
    _, count, depth, _ = both.shape
    me = lax.axis_index("dp")
    for d in range(2 * count):
        parity = jnp.bitwise_xor(me % 2, d % 2)
        other = jnp.bitwise_xor(me // 2, d // 2)
        gray = jnp.bitwise_xor(other, other // 2)
        bits = [gray // 2**i % 2 for i in range(len(masks(count)))]
        bits = bits + [parity] if far_first else [parity] + bits
        place = 0
        for bit in bits[1:]:
            place = 2 * place + bit
        both[bits[0], place] = acc[d * depth : (d + 1) * depth, lanes].astype(BF16)


def shard_shape(width, lanes):
    members = lax.axis_size("dp")
    return jax.ShapeDtypeStruct((2, members // 2, width // members, lanes), BF16)


class Wires:
    def __init__(self, send, recv):
        self.send, self.recv, self.used = send, recv, 0
        self.all = []

    def remote(self, src, dst, axis, step):
        index = self.used
        self.used += 1
        move = pltpu.make_async_remote_copy(
            src_ref=src,
            dst_ref=dst,
            send_sem=self.send.at[index],
            recv_sem=self.recv.at[index],
            device_id={axis: jnp.bitwise_xor(lax.axis_index(axis), step)},
            device_id_type=pl.DeviceIdType.MESH,
        )
        self.all.append(move)
        return move


def masks(count):
    found = [1]
    while 2 ** (len(found) + 1) <= count:
        found.append(2 * found[-1] + 1)
    return found


class Shards:
    def __init__(self, wires, keep, send, got, out, own_sem, load_sem, far_first=False):
        self.keep, self.got, self.out, self.load_sem = keep, got, out, load_sem
        self.count = keep.shape[0]
        order = [2 * mask for mask in masks(self.count)]
        order = order + [1] if far_first else [1] + order
        self.first = None if send is None else wires.remote(send, got, "dp", order[0])
        self.steps = []
        size = self.count
        for step in order[1:]:
            size //= 2
            part = pl.ds(size, size)
            self.steps.append((size, wires.remote(keep.at[part], out.at[part], "dp", step)))
        self.own = pltpu.make_async_copy(keep.at[0], out.at[0], own_sem)

    def start(self):
        self.first.start()

    def add(self, size):
        for k in range(size):
            self.keep[k] = add_low(self.keep[k], self.got[k])

    def second(self):
        if self.first is not None:
            self.first.wait_recv()
            self.add(self.count)
        self.steps[0][1].start()

    def third(self):
        for (size, move), (_, after) in zip(self.steps, self.steps[1:]):
            move.wait_recv()
            part = pl.ds(0, size)
            copy = pltpu.make_async_copy(
                self.out.at[pl.ds(size, size)], self.got.at[part], self.load_sem
            )
            copy.start()
            copy.wait()
            self.add(size)
            after.start()
        self.own.start()

    def finish(self):
        self.steps[-1][1].wait_recv()
        self.own.wait()


def add_got(keep, got):
    for k in range(keep.shape[0]):
        keep[k] = add_low(keep[k], got[k])


def greet(axes):
    barrier = pltpu.get_barrier_semaphore()
    for axis, step in axes:
        pl.semaphore_signal(
            barrier,
            1,
            device_id={axis: jnp.bitwise_xor(lax.axis_index(axis), step)},
            device_id_type=pl.DeviceIdType.MESH,
        )
    pl.semaphore_wait(barrier, len(axes))


def partners(far):
    over_dp = [1] + [2 * mask for mask in masks(lax.axis_size("dp") // 2) if far]
    return [("head", s) for s in range(1, lax.axis_size("head"))] + [("dp", s) for s in over_dp]


FRONT_IN = (
    "lens", "x", "og", "gain1", "bias1", "gain2", "bias2", "upb", "f1b", "f2b", "vt", "f1", "f2",
    "ow", "up", "down",
)
FRONT_OUT = (
    "xs_o", "n1t_o", "hid_o", "slope_o", "prob_o", "valt_o", "mgt_o", "f_o", "rg_o", "res_o",
    "down_o", "up1_o", "up2_o", "ow_o", "upb_sum", "sums",
)
FRONT_SCRATCH = (
    "xs", "n1", "n1t", "big", "f2v", "hidb", "slopeb", "probb", "valt", "attt", "owv", "upv",
    "downv", "ogs", "n2s", "pug", "near1", "near3", "crossb", "crossr", "fterms", "res", "mgts",
    "acc", "ohalf", "osent", "ogot", "dboth", "dgot", "uboth", "ugot", "oboth", "send", "recv",
    "load", "spill", "store",
)


def flat_row(ref):
    return ref[...].reshape(1, -1)


def split_prob(parts, length, longest, b, zero):
    is_full = length == longest
    is_half = length == longest // 2
    for c in range(len(parts)):
        half = parts[c % 2] if c // 2 == b // 2 else zero
        quarter = parts[0] if c == b else zero
        yield c, jnp.where(is_full, parts[c], jnp.where(is_half, half, quarter))


def cells(row):
    return [row[:, c : c + BLOCK] for c in range(0, row.shape[1], BLOCK)]


def front_kernel(*refs):
    r = types.SimpleNamespace(**dict(zip(FRONT_IN + FRONT_OUT + FRONT_SCRATCH, refs)))
    r.low = r.n1
    r.terms = r.xs
    slabs, rows, width = r.xs.shape
    heads, _, longest = r.f2v.shape
    depth = r.valt.shape[1]
    dim = depth // heads
    half = rows // 2
    blocks = rows // BLOCK
    me = lax.axis_index("head")

    w = Wires(r.send, r.recv)
    down_first = w.remote(r.dboth.at[1], r.dgot, "dp", 1)
    up_first = w.remote(r.uboth.at[0, 1], r.ugot, "dp", 1)

    def remote(src, dst, step):
        return w.remote(src, dst, "head", step)

    def cut(c):
        return pl.ds(c * half, half)

    def share(step):
        return pl.ds(pl.multiple_of(jnp.bitwise_xor(me, step) * depth, depth), depth)

    my_rows = share(0)
    r.mgt = r.n1t.at[0]
    moves = {
        "x1": remote(r.x, r.xs.at[1], 1),
        "x2": remote(r.x, r.xs.at[2], 2),
        "x3": remote(r.xs.at[2], r.xs.at[3], 1),
        "o1": remote(r.og, r.ogs.at[1], 1),
        "t1": remote(r.terms.at[1], r.near1, 1),
    }
    columns = remote(r.osent, r.ogot, 1)
    near, far, onward = [], [], []
    for j in range(slabs):
        near.append(remote(r.attt.at[j, my_rows], r.attt.at[j ^ 1, my_rows], 1))
        far.append(remote(r.attt.at[j, my_rows], r.attt.at[j ^ 2, my_rows], 2))
        onward.append(remote(r.attt.at[j, share(2)], r.attt.at[j ^ 1, share(2)], 1))
    for j in range(1, slabs):
        moves[f"g{j}"] = remote(r.mgt.at[share(j)], r.mgts.at[j], j)
    for c in range(2):
        part = cut(c)
        moves[f"o2{c}"] = remote(r.og.at[part], r.ogs.at[2, part], 2)
        moves[f"o3{c}"] = remote(r.ogs.at[2, part], r.ogs.at[3, part], 1)
        moves[f"t3{c}"] = remote(r.terms.at[3, part], r.near3.at[part], 1)
        moves[f"c{c}"] = remote(r.crossb.at[part], r.crossr.at[part], 2)

    def f1_load(h):
        rows_of = pl.ds(pl.multiple_of(h * width, width), width)
        return pltpu.make_async_copy(r.f1.at[h], r.big.at[rows_of], r.load.at[1 + 2 * h])

    def f2_load(h):
        return pltpu.make_async_copy(r.f2.at[h], r.f2v.at[h], r.load.at[2 + 2 * h])

    loads = [pltpu.make_async_copy(r.x, r.xs.at[0], r.load.at[0])]
    for h in range(heads):
        loads += [f1_load(h), f2_load(h)]
    base = 1 + 2 * heads
    late = [
        pltpu.make_async_copy(r.ow, r.owv, r.load.at[base]),
        pltpu.make_async_copy(r.up, r.upv, r.load.at[base + 1]),
        pltpu.make_async_copy(r.down, r.downv, r.load.at[base + 2]),
        pltpu.make_async_copy(r.og, r.ogs.at[0], r.load.at[base + 3]),
    ]
    for copy in loads:
        copy.start()
    greet(partners(False))
    moves["x2"].start()
    moves["x1"].start()
    for copy in late:
        copy.start()
    loads[0].wait()

    def spills(j, h, slot):
        return [
            pltpu.make_async_copy(r.hidb.at[slot], r.hid_o.at[j, h], r.spill.at[slot, 0]),
            pltpu.make_async_copy(r.slopeb.at[slot], r.slope_o.at[j, h], r.spill.at[slot, 1]),
            pltpu.make_async_copy(r.probb.at[slot], r.prob_o.at[j, h], r.spill.at[slot, 2]),
        ]

    def slab_step(j, carry):
        @pl.when(j == 1)
        def _():
            moves["x1"].wait_recv()

        @pl.when(j == 2)
        def _():
            moves["x2"].wait_recv()
            moves["x3"].start()
            moves["o20"].start()
            moves["o1"].start()

        @pl.when(j == 3)
        def _():
            moves["x3"].wait_recv()
            for k in range(2):
                far[k].wait_recv()
                onward[k ^ 2].start()

        scaled, _ = standardize(r.xs[j].astype(F32))
        low = (scaled * flat_row(r.gain1) + flat_row(r.bias1)).astype(BF16)
        r.n1[...] = low
        r.n1t[j] = low.T
        r.valt[j] = mm(r.vt[...], r.n1t[j]).astype(BF16)

        def head_step(h, carry):
            turn = j * heads + h
            slot = turn % 2

            @pl.when(j == 0)
            def _():
                f1_load(h).wait()
                f2_load(h).wait()

            @pl.when(turn >= 2)
            def _():
                for copy in spills(j, h, slot):
                    copy.wait()

            first = jnp.bitwise_xor(me, j) * blocks
            column = lax.broadcasted_iota(jnp.int32, (BLOCK, longest), 1)
            zero = jnp.zeros((BLOCK, BLOCK), F32)
            f1_rows = pl.ds(pl.multiple_of(h * width, width), width)
            for c in range(2):
                part = slice(c * half, (c + 1) * half)
                gated, slope = silu_and_slope(mm(r.n1[part], r.big[f1_rows]) + r.f1b[pl.ds(h, 1)])
                hidden = gated.astype(BF16)
                r.hidb[slot, part] = hidden
                r.slopeb[slot, part] = slope.astype(BF16)
                scores = mm(hidden, r.f2v[h]) + r.f2b[pl.ds(h, 1)]
                for i in range(half // BLOCK):
                    b = c * (half // BLOCK) + i
                    length = r.lens[first + b]
                    own = scores[i * BLOCK : (i + 1) * BLOCK]
                    keep = column < length
                    top = jnp.max(jnp.where(keep, own, -3.0e38), -1, keepdims=True)
                    exp_val = jnp.where(keep, jnp.exp(own - top), 0.0)
                    prob = exp_val * (1.0 / jnp.sum(exp_val, -1, keepdims=True))
                    for k, cell in split_prob(cells(prob), length, longest, b, zero):
                        r.probb[
                            slot, b * BLOCK : (b + 1) * BLOCK, k * BLOCK : (k + 1) * BLOCK
                        ] = cell.astype(BF16)
            own_rows = pl.ds(pl.multiple_of(h * dim, dim), dim)
            mixed = mm_nt(r.valt[j, own_rows], r.probb[slot])
            place = pl.ds(pl.multiple_of(me * depth + h * dim, dim), dim)
            r.attt[j, place] = mixed.astype(BF16)
            for copy in spills(j, h, slot):
                copy.start()
            return carry

        lax.fori_loop(0, heads, head_step, 0)
        for k in range(slabs):

            @pl.when(j == k)
            def _(k=k):
                far[k].start()
                near[k].start()
                if k == slabs - 1:
                    moves["o21"].start()

        return carry

    lax.fori_loop(0, slabs, slab_step, 0)
    stores = [
        pltpu.make_async_copy(r.xs, r.xs_o, r.store.at[0]),
        pltpu.make_async_copy(r.n1t, r.n1t_o, r.store.at[1]),
        pltpu.make_async_copy(r.valt, r.valt_o, r.store.at[2]),
    ]
    for copy in stores:
        copy.start()
    moves["o20"].wait_recv()
    moves["o30"].start()
    for k in (2, 3):
        near[k].wait_recv()
        onward[k].wait_recv()
    for copy in late:
        copy.wait()
    for copy in stores:
        copy.wait()
    stores = []
    sent = moves["x3"]
    sent.wait_send()

    def residual_step(j, carry):
        residual = r.xs[j].astype(F32) + mm_tn(r.attt[j], r.owv[...])

        @pl.when(j == 0)
        def _():
            r.res[...] = residual

        scaled, _ = standardize(residual)
        r.n2s[j] = (scaled * flat_row(r.gain2) + flat_row(r.bias2)).astype(BF16)
        return carry

    lax.fori_loop(2, 4, residual_step, 0)

    def send_cross(c):
        part = cut(c)
        moves[f"t3{c}"].wait_recv()
        r.crossb[part] = add_low(r.terms[2, part], r.near3[part])
        moves[f"c{c}"].start()

    def ffn_step(u, carry):
        j = jnp.where(u < 2, 2 + u, jnp.where(u < 6, (u - 2) // 2, u - 4))
        c = jnp.where(u < 2, 0, jnp.where(u < 6, u % 2, 1))

        @pl.when(u == 1)
        def _():
            moves["o30"].wait_recv()
            for k in (2, 3):
                far[k].wait_recv()
                onward[k ^ 2].start()

        @pl.when(u == 2)
        def _():
            for k in (0, 1):
                near[k].wait_recv()
                onward[k].wait_recv()
            moves["o1"].wait_recv()
            lax.fori_loop(0, 2, residual_step, 0)

        @pl.when(u == 6)
        def _():
            moves["o21"].wait_recv()
            moves["o31"].start()

        @pl.when(u == 7)
        def _():
            moves["o31"].wait_recv()

        part = pl.ds(pl.multiple_of(c * half, half), half)
        gated, slope = silu_and_slope(mm(r.n2s[j, part], r.upv[...]) + flat_row(r.upb))
        act = gated.astype(BF16)
        r.big[pl.ds(pl.multiple_of(j * rows + c * half, half), half)] = act
        pug = (mm_nt(r.ogs[j, part], r.downv[...]) * slope).astype(BF16)
        r.pug[j, part] = pug
        r.terms[j, part] = mm_nt(pug, r.upv[...]).astype(BF16)
        r.fterms[j, part] = mm(act, r.downv[...]).astype(BF16)

        @pl.when(u == 1)
        def _():
            moves["t30"].start()

        @pl.when(u == 2)
        def _():
            send_cross(0)

        @pl.when(u == 5)
        def _():
            moves["t1"].start()

        @pl.when(u == 7)
        def _():
            moves["t31"].start()

        return carry

    lax.fori_loop(0, 8, ffn_step, 0)
    send_cross(1)
    flat = (slabs * rows, width)
    r.acc[...] = mm_tn(r.ogs[...].reshape(flat), r.big[0 : slabs * rows])
    store_shards(r.dboth, r.acc)
    down_first.start()
    stores = [
        pltpu.make_async_copy(r.fterms, r.f_o, r.store.at[5]),
        pltpu.make_async_copy(r.res, r.res_o, r.store.at[6]),
    ]
    for copy in stores:
        copy.start()
    cot = r.ogs[0].astype(F32)
    r.sums[2:3] = jnp.sum(cot, 0, keepdims=True)
    moves["t1"].wait_recv()
    moves["c0"].wait_recv()
    moves["c1"].wait_recv()

    grad = r.terms[0].astype(F32) + r.near1[...].astype(F32) + r.crossr[...].astype(F32)
    scaled, inv_std = standardize(r.res[...])
    res_grad = cot + norm_back(grad, scaled, inv_std, flat_row(r.gain2))
    r.rg_o[...] = res_grad
    r.low[...] = res_grad.astype(BF16)
    r.sums[0:1] = jnp.sum(grad * scaled, 0, keepdims=True)
    r.sums[1:2] = jnp.sum(grad, 0, keepdims=True)
    r.mgt[...] = mm_nt(r.owv[...], r.low[...]).astype(BF16)
    for j in (2, 3, 1):
        moves[f"g{j}"].start()
        r.mgts[0] = r.mgt[my_rows]
    mixed = r.attt[0]
    r.acc[...] = mm(mixed, r.low[...])
    span = width // 2
    mine = pl.ds(pl.multiple_of(me % 2 * span, BLOCK), span)
    theirs = pl.ds(pl.multiple_of((1 - me % 2) * span, BLOCK), span)
    r.osent[...] = r.acc[:, theirs].astype(BF16)
    columns.start()
    r.ohalf[...] = r.acc[:, mine]
    r.acc[...] = mm_tn(r.n2s[...].reshape(flat), r.pug[...].reshape(flat))
    for i in range(2):
        store_shards(r.uboth.at[i], r.acc, slice(i * span, (i + 1) * span))
        if i == 0:
            up_first.start()
    r.upb_sum[...] = jnp.sum(r.pug[...].reshape(flat).astype(F32), 0, keepdims=True)
    columns.wait_recv()
    r.ohalf[...] += r.ogot[...].astype(F32)
    store_shards(r.oboth, r.ohalf)
    more = [
        pltpu.make_async_copy(r.uboth.at[1], r.up2_o, r.store.at[4]),
        pltpu.make_async_copy(r.oboth, r.ow_o, r.store.at[7]),
    ]
    for copy in more:
        copy.start()
    stores += more
    for j in range(1, slabs):
        moves[f"g{j}"].wait_recv()
    stores.append(pltpu.make_async_copy(r.mgts, r.mgt_o, r.store.at[8]))
    stores[-1].start()
    down_first.wait_recv()
    add_got(r.dboth.at[0], r.dgot)
    stores.append(pltpu.make_async_copy(r.dboth.at[0], r.down_o, r.store.at[9]))
    stores[-1].start()
    up_first.wait_recv()
    add_got(r.uboth.at[0, 0], r.ugot)
    stores.append(pltpu.make_async_copy(r.uboth.at[0, 0], r.up1_o, r.store.at[10]))
    stores[-1].start()
    for copy in stores:
        copy.wait()
    total = slabs * heads
    for turn in (total - 2, total - 1):
        for copy in spills(turn // heads, turn % heads, turn % 2):
            copy.wait()
    for move in w.all:
        if move is not sent:
            move.wait_send()


def front(lens, x, og, gain1, bias1, gain2, bias2, upb, f1b, f2b, vt, f1, f2, ow, up, down):
    rows, width = x.shape
    heads, _, longest = f2.shape
    depth = vt.shape[0]
    units = up.shape[1]
    slabs = lax.axis_size("head")
    osh = shard_shape(width, width // 2)
    dsh = shard_shape(width, units)
    group = (slabs, rows, width)
    anywhere = pl.BlockSpec(memory_space=pl.ANY)
    vmem = pl.BlockSpec(memory_space=pltpu.VMEM)
    low = lambda *s: jax.ShapeDtypeStruct(s, BF16)
    wide = lambda *s: jax.ShapeDtypeStruct(s, F32)
    out_shape = [
        low(*group),
        low(slabs, width, rows),
        low(slabs, heads, rows, width),
        low(slabs, heads, rows, width),
        low(slabs, heads, rows, longest),
        low(slabs, depth, rows),
        low(slabs, depth, rows),
        low(*group),
        wide(rows, width),
        wide(rows, width),
        jax.ShapeDtypeStruct(dsh.shape[1:], BF16),
        jax.ShapeDtypeStruct(osh.shape[1:], BF16),
        osh,
        osh,
        wide(1, units),
        wide(3, width),
    ]
    out_specs = [vmem if n in ("rg_o", "upb_sum", "sums") else anywhere for n in FRONT_OUT]
    vl = lambda *s: pltpu.VMEM(s, BF16)
    vf = lambda *s: pltpu.VMEM(s, F32)
    scratch = dict(
        xs=vl(*group),
        n1=vl(rows, width),
        n1t=vl(slabs, width, rows),
        big=vl(max(heads * width, slabs * rows), width),
        f2v=vl(heads, width, longest),
        hidb=vl(2, rows, width),
        slopeb=vl(2, rows, width),
        probb=vl(2, rows, longest),
        valt=vl(slabs, depth, rows),
        attt=vl(slabs, width, rows),
        owv=vl(width, width),
        upv=vl(width, units),
        downv=vl(units, width),
        ogs=vl(*group),
        n2s=vl(*group),
        pug=vl(slabs, rows, units),
        near1=vl(rows, width),
        near3=vl(rows, width),
        crossb=vl(rows, width),
        crossr=vl(rows, width),
        fterms=vl(*group),
        res=vf(rows, width),
        mgts=vl(slabs, depth, rows),
        acc=vf(width, width),
        ohalf=vf(width, width // 2),
        osent=vl(width, width // 2),
        ogot=vl(width, width // 2),
        dboth=vl(*dsh.shape),
        dgot=vl(*dsh.shape[1:]),
        uboth=vl(2, *osh.shape),
        ugot=vl(*osh.shape[1:]),
        oboth=vl(*osh.shape),
        send=pltpu.SemaphoreType.DMA((15 + 4 * slabs,)),
        recv=pltpu.SemaphoreType.DMA((15 + 4 * slabs,)),
        load=pltpu.SemaphoreType.DMA((5 + 2 * heads,)),
        spill=pltpu.SemaphoreType.DMA((2, 3)),
        store=pltpu.SemaphoreType.DMA((11,)),
    )
    smem = pl.BlockSpec(memory_space=pltpu.SMEM)
    return pl.pallas_call(
        front_kernel,
        out_shape=out_shape,
        in_specs=[smem] + [anywhere] * 2 + [vmem] * 8 + [anywhere] * 5,
        out_specs=out_specs,
        scratch_shapes=[scratch[n] for n in FRONT_SCRATCH],
        compiler_params=pltpu.CompilerParams(
            collective_id=0, has_side_effects=True, vmem_limit_bytes=FUSED_LIMIT
        ),
        cost_estimate=cost(
            slabs * rows * width * (heads * (width + longest) + 6 * units), 60 << 20
        ),
        name="front",
    )(lens, x, og, gain1, bias1, gain2, bias2, upb, f1b, f2b, vt, f1, f2, ow, up, down)


BACK_IN = (
    "lens", "upb_sum", "sums", "gain1", "downb", "vt", "hid", "slope", "prob", "n1t", "valt", "mgt",
    "f1", "f2", "xs", "fterms", "down", "up1", "up2", "ow", "res", "rg",
)
BACK_OUT = ("result", "input", "ow_o", "down_o", "up_o", "f1_o", "f2_o", "val_o", "small_o")
BACK_SCRATCH = (
    "n1tv", "valtv", "mgtv", "vgt", "f1v", "f2v", "terms", "probb", "sg", "pog",
    "acc1", "acc2", "acc3", "xb", "near3", "near1", "crossr", "fb", "fnear3",
    "fnear1", "fcrossr", "rgv", "dk", "dgot", "uk", "ugot", "vk", "vhalf", "ok", "ogot", "oall", "olow", "aboth",
    "agot", "bboth", "bgot", "vboth", "vgot", "small", "small_in", "send",
    "recv", "load", "fetch", "store",
)


def back_kernel(*refs):
    r = types.SimpleNamespace(**dict(zip(BACK_IN + BACK_OUT + BACK_SCRATCH, refs)))
    r.crossb = r.terms.at[3]
    r.resv = r.acc1.at[pl.ds(0, r.rgv.shape[0])]
    slabs, heads, rows, width = r.pog.shape
    longest = r.probb.shape[2]
    depth = r.vgt.shape[1]
    dim = depth // heads
    blocks = rows // BLOCK
    count = r.ok.shape[0]
    me = lax.axis_index("head")
    turns = slabs * heads
    w = Wires(r.send, r.recv)
    sems = iter(range(6 * heads + 10))

    def shards(keep, send, got, out, far_first=False):
        own_sem, load_sem = r.store.at[next(sems)], r.store.at[next(sems)]
        return Shards(w, keep, send, got, out, own_sem, load_sem, far_first)

    down_group = shards(r.dk, None, r.dgot, r.down_o)
    up1_group = shards(r.vk, None, r.vhalf, r.up_o.at[0])
    up2_group = shards(r.uk, r.up2.at[1], r.ugot, r.up_o.at[1])
    out_group = shards(r.ok, r.ow.at[1], r.ogot, r.oall)
    out_heads = [w.remote(r.olow, r.ow_o.at[j], "head", j) for j in range(1, slabs)]
    f1_group, f2_group = [], []
    for h in range(heads):
        both = r.bboth.at[h]
        f2_group.append(shards(both.at[0], both.at[1], r.bgot.at[h], r.f2_o.at[h]))
        for i in range(2):
            both = r.aboth.at[h, i]
            f1_group.append(shards(both.at[0], both.at[1], r.agot.at[h, i], r.f1_o.at[h, i]))
    val_group = shards(r.vboth.at[0], r.vboth.at[1], r.vgot, r.val_o)
    fterm1 = w.remote(r.fterms.at[1], r.fnear1, "head", 1)
    fterm3 = w.remote(r.fterms.at[3], r.fnear3, "head", 1)
    fcross = w.remote(r.fb, r.fcrossr, "head", 2)
    term1 = w.remote(r.terms.at[1], r.near1, "head", 1)
    term3 = w.remote(r.terms.at[3], r.near3, "head", 1)
    cross = w.remote(r.crossb, r.crossr, "head", 2)
    steps = [1] + [2 * mask for mask in masks(count)]
    small_steps = [
        w.remote(r.small.at[i], r.small_in.at[i], "dp", step) for i, step in enumerate(steps)
    ]
    small_last = r.small.at[len(steps)]
    small_x = [
        w.remote(small_last, r.small_o.at[j], "head", j) for j in range(1, slabs)
    ]
    base = 6 * heads + 10
    own_low = pltpu.make_async_copy(r.olow, r.ow_o.at[0], r.store.at[base])
    own_small = pltpu.make_async_copy(small_last, r.small_o.at[0], r.store.at[base + 1])

    def load(index, src, dst):
        return pltpu.make_async_copy(src, dst, r.load.at[index])

    loads = [
        load(0, r.mgt, r.mgtv),
        load(1, r.valt, r.valtv),
        load(2, r.f2, r.f2v),
        load(3, r.n1t, r.n1tv),
        load(4, r.down, r.dk),
        load(5, r.fterms.at[2], r.fb),
        load(6, r.f1, r.f1v),
        load(7, r.xs.at[3], r.xb),
        load(9, r.rg, r.rgv),
        load(10, r.up2.at[0], r.uk),
        load(11, r.ow.at[0], r.ok),
    ]

    def fetches(turn):
        h, j, slot = turn // slabs, turn % slabs, turn % 2
        return [
            pltpu.make_async_copy(r.prob.at[j, h], r.probb.at[slot], r.fetch.at[slot, 0]),
            pltpu.make_async_copy(r.slope.at[j, h], r.terms.at[2 + slot], r.fetch.at[slot, 1]),
            pltpu.make_async_copy(r.hid.at[j, h], r.terms.at[slot], r.fetch.at[slot, 2]),
        ]

    up1_load = load(13, r.up1, r.vk)
    for copy in loads[:2] + fetches(0) + loads[2:] + [up1_load]:
        copy.start()
    greet(partners(True))
    up2_group.start()
    out_group.start()
    fterm3.start()
    fterm1.start()
    r.small[0] = jnp.zeros(r.small.shape[1:], F32)
    r.small[0, 2 * heads : 2 * heads + 1] = r.upb_sum[...]
    r.small[0, 2 * heads + 3 : 2 * heads + 6] = r.sums[...]
    for copy in loads[:6]:
        copy.wait()
    down_group.second()
    up1_load.wait()
    up1_group.second()

    def turn_step(turn, carry):
        h, j, slot = turn // slabs, turn % slabs, turn % 2
        for copy in fetches(turn):
            copy.wait()

        @pl.when(turn + 1 < turns)
        def _():
            for copy in fetches(turn + 1):
                copy.start()

        @pl.when(j == 0)
        def _():
            r.acc1[...] = jnp.zeros_like(r.acc1)
            r.acc2[...] = jnp.zeros_like(r.acc2)

        head_rows = pl.ds(pl.multiple_of(h * dim, dim), dim)
        mgt = r.mgtv[j, head_rows]
        r.vgt[j, head_rows] = mm(mgt, r.probb[slot]).astype(BF16)
        probs_grad = mm_tn(mgt, r.valtv[j, head_rows])
        first = jnp.bitwise_xor(me, j) * blocks
        zero = jnp.zeros((BLOCK, BLOCK), F32)
        for b in range(blocks):
            length = r.lens[first + b]
            own = slice(b * BLOCK, (b + 1) * BLOCK)
            prob = r.probb[slot, own].astype(F32)
            grad = probs_grad[own]
            inner = jnp.sum(prob * grad, -1, keepdims=True)
            parts = cells(prob * (grad - inner))
            is_full = length == longest
            is_half = length == longest // 2
            for c in range(blocks):
                half = parts[2 * (b // 2) + c] if c < 2 else zero
                quarter = parts[b] if c == 0 else zero
                cell = jnp.where(is_full, parts[c], jnp.where(is_half, half, quarter))
                r.sg[own, c * BLOCK : (c + 1) * BLOCK] = cell.astype(BF16)
        scores_grad = r.sg[...]
        row = pl.ds(h, 1)
        pog = (mm_nt(scores_grad, r.f2v[h]) * r.terms[2 + slot].astype(F32)).astype(BF16)
        r.pog[j, h] = pog
        r.small[0, row] += jnp.sum(pog.astype(F32), 0, keepdims=True)
        row = pl.ds(heads + h, 1)
        r.small[0, row, 0:longest] += jnp.sum(scores_grad.astype(F32), 0, keepdims=True)
        r.acc2[...] += mm_tn(r.terms[slot], scores_grad)
        r.acc1[...] += mm(r.n1tv[j], pog)

        for k in range(heads):

            @pl.when(turn == slabs * k + slabs - 1)
            def _(k=k):
                store_shards(r.bboth.at[k], r.acc2)
                if k < heads - 1:
                    f2_group[k].start()
                for i in range(2):
                    span = width // 2
                    store_shards(r.aboth.at[k, i], r.acc1, slice(i * span, (i + 1) * span))
                    if k < heads - 1:
                        f1_group[2 * k + i].start()

        @pl.when(turn == 1)
        def _():
            fterm3.wait_recv()
            r.fb[...] = add_low(r.fb[...], r.fnear3[...])
            fcross.start()

        @pl.when(turn == 2)
        def _():
            for copy in loads[9:]:
                copy.wait()
            down_group.third()
            up2_group.second()

        @pl.when(turn == 3)
        def _():
            up1_group.third()

        @pl.when(turn == 4)
        def _():
            out_group.second()
            up2_group.third()

        @pl.when(turn == 6)
        def _():
            out_group.third()
            f2_group[0].second()

        @pl.when(turn == 8)
        def _():
            f1_group[0].second()
            f2_group[0].third()

        @pl.when(turn == 9)
        def _():
            out_group.finish()
            r.olow[...] = (r.oall[0].astype(F32) + r.oall[1].astype(F32)).astype(BF16)
            for move in out_heads:
                move.start()
            own_low.start()

        @pl.when(turn == 10)
        def _():
            f1_group[1].second()
            f1_group[0].third()

        return carry

    lax.fori_loop(0, turns, turn_step, 0)
    for copy in loads[6:8]:
        copy.wait()
    res_load = load(8, r.res, r.resv)
    res_load.start()

    def term_step(i, carry):
        j = slabs - 1 - i

        @pl.when(i > 0)
        def _():
            load(7, r.xs.at[j], r.xb).wait()

        term = mm_tn(r.vgt[j], r.vt[...])
        for h in range(heads):
            term += mm_nt(r.pog[j, h], r.f1v[h])
        low = term.astype(BF16)
        r.terms[j] = low
        wide = low.astype(F32)
        scaled, _ = standardize(r.xb[...].astype(F32))
        at = 2 * heads + 1
        r.small[0, at : at + 1] += jnp.sum(wide * scaled, 0, keepdims=True)
        r.small[0, at + 1 : at + 2] += jnp.sum(wide, 0, keepdims=True)

        @pl.when(i < slabs - 1)
        def _():
            load(7, r.xs.at[j - 1], r.xb).start()

        @pl.when(i == 0)
        def _():
            term3.start()
            f1_group[1].third()

        @pl.when(i == 1)
        def _():
            term3.wait_recv()
            term3.wait_send()
            r.crossb[...] = add_low(r.terms[2], r.near3[...])
            cross.start()
            f2_group[1].second()

        @pl.when(i == 2)
        def _():
            term1.start()
            f1_group[2].second()
            f2_group[1].third()

        return carry

    lax.fori_loop(0, slabs, term_step, 0)
    small_steps[0].start()
    f2_group[2].start()
    f1_group[4].start()
    f1_group[5].start()
    f1_group[3].second()
    f1_group[2].third()
    total = mm_nt(r.n1tv[0], r.vgt[0])
    for j in range(1, slabs):
        total += mm_nt(r.n1tv[j], r.vgt[j])
    r.acc3[...] = total
    store_shards(r.vboth, r.acc3)
    val_group.start()
    fcross.wait_send()
    own_fterm = load(12, r.fterms.at[0], r.fb)
    own_fterm.start()
    for copy in [res_load, loads[8], own_fterm]:
        copy.wait()
    fterm1.wait_recv()
    fcross.wait_recv()
    others = r.fnear1[...].astype(F32) + r.fcrossr[...].astype(F32)
    r.resv[...] += r.fb[...].astype(F32) + others + flat_row(r.downb)
    finals = [pltpu.make_async_copy(r.resv, r.result, r.store.at[base + 2])]
    finals[0].start()

    def small_step(i):
        small_steps[i].wait_recv()
        r.small[i + 1] = r.small[i] + r.small_in[i]
        for after in small_steps[i + 1 : i + 2] or small_x + [own_small]:
            after.start()

    small_step(0)
    f1_group[3].third()
    term1.wait_recv()
    cross.wait_recv()
    grad = r.terms[0].astype(F32) + r.near1[...].astype(F32) + r.crossr[...].astype(F32)
    scaled, inv_std = standardize(r.xb[...].astype(F32))
    r.rgv[...] += norm_back(grad, scaled, inv_std, flat_row(r.gain1))
    finals.append(pltpu.make_async_copy(r.rgv, r.input, r.store.at[base + 3]))
    finals[1].start()
    small_step(1)
    f2_group[2].second()
    for i in range(2, len(steps)):
        small_step(i)
    f1_group[4].second()
    f2_group[2].third()
    f1_group[5].second()
    f1_group[4].third()
    val_group.second()
    f1_group[5].third()
    val_group.third()
    for group in [down_group, up1_group, up2_group] + f2_group + f1_group + [val_group]:
        group.finish()
    for move in out_heads + small_x:
        move.wait_recv()
    for copy in finals + [own_low, own_small]:
        copy.wait()
    for move in w.all:
        if move is not term3 and move is not fcross:
            move.wait_send()


def low_shape(*shape):
    return jax.ShapeDtypeStruct(shape, BF16)


def wide_shape(*shape):
    return jax.ShapeDtypeStruct(shape, F32)


def back(*args):
    hid, f2, vt, ow = args[6], args[13], args[5], args[19]
    slabs, heads, rows, width = hid.shape
    longest = f2.shape[2]
    depth = vt.shape[0]
    _, count, part, span = ow.shape
    small = (2 * heads + 6 + 7) // 8 * 8
    low, wide = low_shape, wide_shape
    out_shape = [
        wide(rows, width),
        wide(rows, width),
        low(slabs, part, span),
        low(count, part, width),
        low(2, count, part, span),
        low(heads, 2, count, part, span),
        low(heads, count, part, longest),
        low(count, part, depth),
        wide(slabs, small, width),
    ]
    vl = lambda *s: pltpu.VMEM(s, BF16)
    vf = lambda *s: pltpu.VMEM(s, F32)
    steps = len(masks(count)) + 1
    moves = 2 * (slabs - 1) + (3 * heads + 6) * steps + 6
    scratch = dict(
        n1tv=vl(slabs, width, rows),
        valtv=vl(slabs, depth, rows),
        mgtv=vl(slabs, depth, rows),
        vgt=vl(slabs, depth, rows),
        f1v=vl(heads, width, width),
        f2v=vl(heads, width, longest),
        probb=vl(2, rows, longest),
        sg=vl(rows, longest),
        pog=vl(slabs, heads, rows, width),
        acc1=vf(width, width),
        acc2=vf(width, longest),
        acc3=vf(width, depth),
        xb=vl(rows, width),
        terms=vl(slabs, rows, width),
        near3=vl(rows, width),
        near1=vl(rows, width),
        crossr=vl(rows, width),
        fb=vl(rows, width),
        fnear3=vl(rows, width),
        fnear1=vl(rows, width),
        fcrossr=vl(rows, width),
        rgv=vf(rows, width),
        ok=vl(count, part, span),
        ogot=vl(count, part, span),
        oall=vl(count, part, span),
        olow=vl(part, span),
        dk=vl(count, part, width),
        dgot=vl(count // 2, part, width),
        uk=vl(count, part, span),
        ugot=vl(count, part, span),
        vk=vl(count, part, span),
        vhalf=vl(count // 2, part, span),
        aboth=vl(heads, 2, 2, count, part, span),
        agot=vl(heads, 2, count, part, span),
        bboth=vl(heads, 2, count, part, longest),
        bgot=vl(heads, count, part, longest),
        vboth=vl(2, count, part, depth),
        vgot=vl(count, part, depth),
        small=vf(steps + 1, small, width),
        small_in=vf(steps, small, width),
        send=pltpu.SemaphoreType.DMA((moves,)),
        recv=pltpu.SemaphoreType.DMA((moves,)),
        load=pltpu.SemaphoreType.DMA((14,)),
        fetch=pltpu.SemaphoreType.DMA((2, 3)),
        store=pltpu.SemaphoreType.DMA((14 + 6 * heads,)),
    )
    smem = pl.BlockSpec(memory_space=pltpu.SMEM)
    anywhere = pl.BlockSpec(memory_space=pl.ANY)
    vmem = pl.BlockSpec(memory_space=pltpu.VMEM)
    return pl.pallas_call(
        back_kernel,
        out_shape=out_shape,
        in_specs=[smem] + [vmem] * 5 + [anywhere] * 16,
        out_specs=[anywhere] * len(out_shape),
        scratch_shapes=[scratch[n] for n in BACK_SCRATCH],
        compiler_params=pltpu.CompilerParams(
            collective_id=1, has_side_effects=True, vmem_limit_bytes=FUSED_LIMIT
        ),
        cost_estimate=cost(slabs * rows * width * heads * (3 * width + 2 * longest), 60 << 20),
        name="back",
    )(*args)


def finish_kernel(*refs):
    result, inp, small, down, up, ow, f1, f2, val = refs[:9]
    (
        result_o, input_o, f1b_o, f2b_o, upb_o, down_o, up_o, ow_o, f1_o, f2_o, val_o,
    ) = refs[9:20]
    shared = refs[20:25]
    result_o[...] = result[...]
    input_o[...] = inp[...]
    slabs = small.shape[0]
    heads = f1.shape[0]
    longest = f2.shape[3]
    me = lax.axis_index("head")
    for j in range(slabs):
        owner = jnp.bitwise_xor(me, j)
        units = small.shape[2]
        own = small[owner, 2 * heads : 2 * heads + 1]
        upb_o[j * units : (j + 1) * units] = own.reshape(units)
        for h in range(heads):
            f1b_o[pl.ds(owner * heads + h, 1)] = small[j, h : h + 1]
            f2b_o[pl.ds(owner * heads + h, 1)] = small[j, heads + h : heads + h + 1, 0:longest]
    first = 2 * heads + 1
    for i, ref in enumerate(shared):
        ref[...] = sum(small[j, first + i] for j in range(slabs))
    span = ow.shape[2]
    mine = pl.ds(pl.multiple_of(me % 2 * span, BLOCK), span)
    theirs = pl.ds(pl.multiple_of((1 - me % 2) * span, BLOCK), span)
    ow_o[:, mine] = sum(ow[j].astype(F32) for j in range(0, slabs, 2))
    ow_o[:, theirs] = sum(ow[j].astype(F32) for j in range(1, slabs, 2))
    total = lambda ref: ref[0].astype(F32) + ref[1].astype(F32)
    down_o[...] = total(down)
    for i in range(2):
        up_o[:, i * span : (i + 1) * span] = total(up.at[i])
    val_o[...] = total(val)
    for h in range(heads):
        for i in range(2):
            f1_o[h, :, i * span : (i + 1) * span] = total(f1.at[h, i])
        f2_o[h] = total(f2.at[h])


def finish(members, *args):
    f1, f2, val = args[6:]
    rows, width = args[0].shape
    heads, _, part, longest = f2.shape
    wide = wide_shape
    out_shape = [
        wide(rows, width),
        wide(rows, width),
        wide(members * heads, width),
        wide(members * heads, longest),
        wide(members * width),
        wide(part, width),
        wide(part, width),
        wide(part, width),
        wide(heads, part, width),
        wide(heads, part, longest),
        wide(part, val.shape[2]),
    ] + [wide(width)] * 5
    whole = lambda v: pl.BlockSpec(v.shape, lambda _: (0,) * v.ndim)
    pair = lambda v: pl.BlockSpec((2,) + v.shape[1:], lambda _: (0, 0, 0))
    heads_pair = lambda v: pl.BlockSpec((heads, 2) + v.shape[2:], lambda _: (0, 0, 0, 0))
    sides = lambda v: pl.BlockSpec((2, 2) + v.shape[2:], lambda _: (0,) * 4)
    halves = lambda v: pl.BlockSpec((heads, 2, 2) + v.shape[3:], lambda _: (0,) * 5)
    kinds = [whole] * 3 + [pair, sides, whole, halves, heads_pair, pair]
    return pl.pallas_call(
        finish_kernel,
        grid=(1,),
        out_shape=out_shape,
        in_specs=[kind(v) for kind, v in zip(kinds, args)],
        out_specs=[whole(v) for v in out_shape],
        compiler_params=pltpu.CompilerParams(vmem_limit_bytes=FUSED_LIMIT),
        cost_estimate=cost(0, 20 << 20),
        name="finish",
    )(*args)


def local(
    tokens,
    seq_len,
    norm1_gain,
    norm1_bias,
    f1_weight,
    f1_bias,
    f2_weight,
    f2_bias,
    value_weight,
    out_weight,
    norm2_gain,
    norm2_bias,
    up_weight,
    up_bias,
    down_weight,
    down_bias,
    out_grad,
):
    members = lax.axis_size("head")
    vt = value_weight.T
    (
        xs, n1t, hid, slope, prob, valt, mgt, fterms, res_grad, residual, down_y, up1_y, up2_y, ow_y,
        upb, sums2,
    ) = front(
        seq_len, tokens, out_grad, norm1_gain, norm1_bias, norm2_gain, norm2_bias, up_bias, f1_bias,
        f2_bias, vt, f1_weight, f2_weight, out_weight, up_weight, down_weight,
    )
    (
        result, input_grad, ow_parts, down_parts, up_parts, f1_parts, f2_parts, val_parts, small,
    ) = back(
        seq_len, upb, sums2, norm1_gain, down_bias, vt, hid, slope, prob, n1t, valt, mgt,
        f1_weight, f2_weight, xs, fterms, down_y, up1_y, up2_y, ow_y, residual, res_grad,
    )
    (
        result, input_grad, f1b_all, f2b_all, upb_all, down_piece, up_piece, out_piece, f1_piece,
        f2_piece, value_piece, gain1_g, bias1_g, gain2_g, bias2_g, downb_g,
    ) = finish(
        members, result, input_grad, small, down_parts, up_parts, ow_parts, f1_parts, f2_parts,
        val_parts,
    )
    return (
        result,
        input_grad,
        gain1_g,
        bias1_g,
        f1_piece,
        f1b_all,
        f2_piece,
        f2b_all,
        value_piece,
        out_piece,
        gain2_g,
        bias2_g,
        up_piece,
        upb_all,
        down_piece.T,
        downb_g,
    )


def solution(mesh):
    placed = (
        P(("dp", "head"), None),
        P("dp"),
        P(),
        P(),
        P("head", None, None),
        P("head", None),
        P("head", None, None),
        P("head", None),
        P(None, "head"),
        P(),
        P(),
        P(),
        P(None, "head"),
        P("head"),
        P("head", None),
        P(),
        P(("dp", "head"), None),
    )
    return jax.shard_map(
        local,
        mesh=mesh,
        in_specs=placed,
        out_specs=(
            P(("dp", "head"), None),
            P(("dp", "head"), None),
            P(),
            P(),
            P("head", "dp", None),
            P(),
            P("head", "dp", None),
            P(),
            P("dp", "head"),
            P("dp", None),
            P(),
            P(),
            P("dp", "head"),
            P(),
            P("head", "dp"),
            P(),
        ),
        check_vma=False,
    )
```

```python
import types

import jax
import jax.numpy as jnp
from jax import lax
from jax.experimental import pallas as pl
from jax.experimental.pallas import tpu as pltpu
from jax.sharding import PartitionSpec as P

F32 = jnp.float32
BF16 = jnp.bfloat16
BLOCK = 128
FUSED_LIMIT = 63 << 20


def mm(a, b):
    return lax.dot_general(a, b, (((1,), (0,)), ((), ())), preferred_element_type=F32)


def mm_nt(a, b):
    return lax.dot_general(a, b, (((1,), (1,)), ((), ())), preferred_element_type=F32)


def mm_tn(a, b):
    return lax.dot_general(a, b, (((0,), (0,)), ((), ())), preferred_element_type=F32)


def standardize(values):
    centred = values - jnp.mean(values, -1, keepdims=True)
    inv_std = lax.rsqrt(jnp.mean(centred * centred, -1, keepdims=True) + 1e-05)
    return centred * inv_std, inv_std


def norm_back(grad_out, scaled, inv_std, gain):
    grad_scaled = grad_out * gain
    centre_mean = jnp.mean(grad_scaled, -1, keepdims=True)
    cross_mean = jnp.mean(grad_scaled * scaled, -1, keepdims=True)
    return inv_std * (grad_scaled - centre_mean - scaled * cross_mean)


def silu_and_slope(pre_val):
    sigma = 0.5 + 0.5 * jnp.tanh(0.5 * pre_val)
    gated = pre_val * sigma
    return gated, sigma + gated * (1.0 - sigma)


def add_low(a, b):
    return (a.astype(F32) + b.astype(F32)).astype(BF16)


def cost(macs, bytes_accessed):
    return pl.CostEstimate(flops=2 * macs, bytes_accessed=bytes_accessed, transcendentals=0)


def store_shards(both, acc, lanes=slice(None), far_first=False):
    _, count, depth, _ = both.shape
    me = lax.axis_index("dp")
    for d in range(2 * count):
        parity = jnp.bitwise_xor(me % 2, d % 2)
        other = jnp.bitwise_xor(me // 2, d // 2)
        gray = jnp.bitwise_xor(other, other // 2)
        bits = [gray // 2**i % 2 for i in range(len(masks(count)))]
        bits = bits + [parity] if far_first else [parity] + bits
        place = 0
        for bit in bits[1:]:
            place = 2 * place + bit
        both[bits[0], place] = acc[d * depth : (d + 1) * depth, lanes].astype(BF16)


def shard_shape(width, lanes):
    members = lax.axis_size("dp")
    return jax.ShapeDtypeStruct((2, members // 2, width // members, lanes), BF16)


class Wires:
    def __init__(self, send, recv):
        self.send, self.recv, self.used = send, recv, 0
        self.all = []

    def remote(self, src, dst, axis, step):
        index = self.used
        self.used += 1
        move = pltpu.make_async_remote_copy(
            src_ref=src,
            dst_ref=dst,
            send_sem=self.send.at[index],
            recv_sem=self.recv.at[index],
            device_id={axis: jnp.bitwise_xor(lax.axis_index(axis), step)},
            device_id_type=pl.DeviceIdType.MESH,
        )
        self.all.append(move)
        return move


def masks(count):
    found = [1]
    while 2 ** (len(found) + 1) <= count:
        found.append(2 * found[-1] + 1)
    return found


class Shards:
    def __init__(self, wires, keep, send, got, out, own_sem, load_sem, far_first=False):
        self.keep, self.got, self.out, self.load_sem = keep, got, out, load_sem
        self.count = keep.shape[0]
        order = [2 * mask for mask in masks(self.count)]
        order = order + [1] if far_first else [1] + order
        self.first = None if send is None else wires.remote(send, got, "dp", order[0])
        self.steps = []
        size = self.count
        for step in order[1:]:
            size //= 2
            part = pl.ds(size, size)
            self.steps.append((size, wires.remote(keep.at[part], out.at[part], "dp", step)))
        self.own = pltpu.make_async_copy(keep.at[0], out.at[0], own_sem)

    def start(self):
        self.first.start()

    def add(self, size):
        for k in range(size):
            self.keep[k] = add_low(self.keep[k], self.got[k])

    def second(self):
        if self.first is not None:
            self.first.wait_recv()
            self.add(self.count)
        self.steps[0][1].start()

    def third(self):
        for (size, move), (_, after) in zip(self.steps, self.steps[1:]):
            move.wait_recv()
            part = pl.ds(0, size)
            copy = pltpu.make_async_copy(
                self.out.at[pl.ds(size, size)], self.got.at[part], self.load_sem
            )
            copy.start()
            copy.wait()
            self.add(size)
            after.start()
        self.own.start()

    def finish(self):
        self.steps[-1][1].wait_recv()
        self.own.wait()


def add_got(keep, got):
    for k in range(keep.shape[0]):
        keep[k] = add_low(keep[k], got[k])


def greet(axes):
    barrier = pltpu.get_barrier_semaphore()
    for axis, step in axes:
        pl.semaphore_signal(
            barrier,
            1,
            device_id={axis: jnp.bitwise_xor(lax.axis_index(axis), step)},
            device_id_type=pl.DeviceIdType.MESH,
        )
    pl.semaphore_wait(barrier, len(axes))


def partners(far):
    over_dp = [1] + [2 * mask for mask in masks(lax.axis_size("dp") // 2) if far]
    return [("head", s) for s in range(1, lax.axis_size("head"))] + [("dp", s) for s in over_dp]


FRONT_IN = (
    "lens", "x", "og", "gain1", "bias1", "gain2", "bias2", "upb", "f1b", "f2b", "vt", "f1", "f2",
    "ow", "up", "down",
)
FRONT_OUT = (
    "xs_o", "n1t_o", "hid_o", "slope_o", "prob_o", "valt_o", "mgt_o", "f_o", "rg_o", "res_o",
    "down_o", "up1_o", "up2_o", "ow_o", "upb_sum", "sums",
)
FRONT_SCRATCH = (
    "xs", "n1", "n1t", "big", "f2v", "hidb", "slopeb", "probb", "valt", "attt", "owv", "upv",
    "downv", "ogs", "n2s", "pug", "near1", "near3", "crossb", "crossr", "fterms", "res", "mgts",
    "acc", "ohalf", "osent", "ogot", "dboth", "dgot", "uboth", "ugot", "oboth", "send", "recv",
    "load", "spill", "store",
)


def flat_row(ref):
    return ref[...].reshape(1, -1)


def split_prob(parts, length, longest, b, zero):
    is_full = length == longest
    is_half = length == longest // 2
    for c in range(len(parts)):
        half = parts[c % 2] if c // 2 == b // 2 else zero
        quarter = parts[0] if c == b else zero
        yield c, jnp.where(is_full, parts[c], jnp.where(is_half, half, quarter))


def cells(row):
    return [row[:, c : c + BLOCK] for c in range(0, row.shape[1], BLOCK)]


def front_kernel(*refs):
    r = types.SimpleNamespace(**dict(zip(FRONT_IN + FRONT_OUT + FRONT_SCRATCH, refs)))
    r.low = r.n1
    r.terms = r.xs
    slabs, rows, width = r.xs.shape
    heads, _, longest = r.f2v.shape
    depth = r.valt.shape[1]
    dim = depth // heads
    half = rows // 2
    blocks = rows // BLOCK
    me = lax.axis_index("head")

    w = Wires(r.send, r.recv)
    down_first = w.remote(r.dboth.at[1], r.dgot, "dp", 1)
    up_first = w.remote(r.uboth.at[0, 1], r.ugot, "dp", 1)

    def remote(src, dst, step):
        return w.remote(src, dst, "head", step)

    def cut(c):
        return pl.ds(c * half, half)

    def share(step):
        return pl.ds(pl.multiple_of(jnp.bitwise_xor(me, step) * depth, depth), depth)

    my_rows = share(0)
    r.mgt = r.n1t.at[0]
    moves = {
        "x1": remote(r.x, r.xs.at[1], 1),
        "x2": remote(r.x, r.xs.at[2], 2),
        "x3": remote(r.xs.at[2], r.xs.at[3], 1),
        "o1": remote(r.og, r.ogs.at[1], 1),
        "t1": remote(r.terms.at[1], r.near1, 1),
    }
    columns = remote(r.osent, r.ogot, 1)
    near, far, onward = [], [], []
    for j in range(slabs):
        near.append(remote(r.attt.at[j, my_rows], r.attt.at[j ^ 1, my_rows], 1))
        far.append(remote(r.attt.at[j, my_rows], r.attt.at[j ^ 2, my_rows], 2))
        onward.append(remote(r.attt.at[j, share(2)], r.attt.at[j ^ 1, share(2)], 1))
    for j in range(1, slabs):
        for c in range(2):
            part = cut(c)
            moves[f"g{j}{c}"] = remote(r.mgt.at[share(j), part], r.mgts.at[j, :, part], j)
    for c in range(2):
        part = cut(c)
        moves[f"o2{c}"] = remote(r.og.at[part], r.ogs.at[2, part], 2)
        moves[f"o3{c}"] = remote(r.ogs.at[2, part], r.ogs.at[3, part], 1)
        moves[f"t3{c}"] = remote(r.terms.at[3, part], r.near3.at[part], 1)
        moves[f"c{c}"] = remote(r.crossb.at[part], r.crossr.at[part], 2)

    def f1_load(h):
        rows_of = pl.ds(pl.multiple_of(h * width, width), width)
        return pltpu.make_async_copy(r.f1.at[h], r.big.at[rows_of], r.load.at[1 + 2 * h])

    def f2_load(h):
        return pltpu.make_async_copy(r.f2.at[h], r.f2v.at[h], r.load.at[2 + 2 * h])

    loads = [pltpu.make_async_copy(r.x, r.xs.at[0], r.load.at[0])]
    for h in range(heads):
        loads += [f1_load(h), f2_load(h)]
    base = 1 + 2 * heads
    late = [
        pltpu.make_async_copy(r.ow, r.owv, r.load.at[base]),
        pltpu.make_async_copy(r.up, r.upv, r.load.at[base + 1]),
        pltpu.make_async_copy(r.down, r.downv, r.load.at[base + 2]),
        pltpu.make_async_copy(r.og, r.ogs.at[0], r.load.at[base + 3]),
    ]
    for copy in loads:
        copy.start()
    greet(partners(False))
    moves["x2"].start()
    moves["x1"].start()
    for copy in late:
        copy.start()
    loads[0].wait()

    def spills(j, h, slot):
        return [
            pltpu.make_async_copy(r.hidb.at[slot], r.hid_o.at[j, h], r.spill.at[slot, 0]),
            pltpu.make_async_copy(r.slopeb.at[slot], r.slope_o.at[j, h], r.spill.at[slot, 1]),
            pltpu.make_async_copy(r.probb.at[slot], r.prob_o.at[j, h], r.spill.at[slot, 2]),
        ]

    def slab_step(j, carry):
        @pl.when(j == 1)
        def _():
            moves["x1"].wait_recv()

        @pl.when(j == 2)
        def _():
            moves["x2"].wait_recv()
            moves["x3"].start()
            moves["o20"].start()
            moves["o1"].start()

        @pl.when(j == 3)
        def _():
            moves["x3"].wait_recv()
            for k in range(2):
                far[k].wait_recv()
                onward[k ^ 2].start()

        scaled, _ = standardize(r.xs[j].astype(F32))
        low = (scaled * flat_row(r.gain1) + flat_row(r.bias1)).astype(BF16)
        r.n1[...] = low
        r.n1t[j] = low.T
        r.valt[j] = mm(r.vt[...], r.n1t[j]).astype(BF16)

        def head_step(h, carry):
            turn = j * heads + h
            slot = turn % 2

            @pl.when(j == 0)
            def _():
                f1_load(h).wait()
                f2_load(h).wait()

            @pl.when(turn >= 2)
            def _():
                for copy in spills(j, h, slot):
                    copy.wait()

            first = jnp.bitwise_xor(me, j) * blocks
            column = lax.broadcasted_iota(jnp.int32, (BLOCK, longest), 1)
            zero = jnp.zeros((BLOCK, BLOCK), F32)
            f1_rows = pl.ds(pl.multiple_of(h * width, width), width)
            for c in range(2):
                part = slice(c * half, (c + 1) * half)
                gated, slope = silu_and_slope(mm(r.n1[part], r.big[f1_rows]) + r.f1b[pl.ds(h, 1)])
                hidden = gated.astype(BF16)
                r.hidb[slot, part] = hidden
                r.slopeb[slot, part] = slope.astype(BF16)
                scores = mm(hidden, r.f2v[h]) + r.f2b[pl.ds(h, 1)]
                for i in range(half // BLOCK):
                    b = c * (half // BLOCK) + i
                    length = r.lens[first + b]
                    own = scores[i * BLOCK : (i + 1) * BLOCK]
                    keep = column < length
                    top = jnp.max(jnp.where(keep, own, -3.0e38), -1, keepdims=True)
                    exp_val = jnp.where(keep, jnp.exp(own - top), 0.0)
                    prob = exp_val * (1.0 / jnp.sum(exp_val, -1, keepdims=True))
                    for k, cell in split_prob(cells(prob), length, longest, b, zero):
                        r.probb[
                            slot, b * BLOCK : (b + 1) * BLOCK, k * BLOCK : (k + 1) * BLOCK
                        ] = cell.astype(BF16)
            own_rows = pl.ds(pl.multiple_of(h * dim, dim), dim)
            mixed = mm_nt(r.valt[j, own_rows], r.probb[slot])
            place = pl.ds(pl.multiple_of(me * depth + h * dim, dim), dim)
            r.attt[j, place] = mixed.astype(BF16)
            for copy in spills(j, h, slot):
                copy.start()
            return carry

        lax.fori_loop(0, heads, head_step, 0)
        for k in range(slabs):

            @pl.when(j == k)
            def _(k=k):
                far[k].start()
                near[k].start()
                if k == slabs - 1:
                    moves["o21"].start()

        return carry

    lax.fori_loop(0, slabs, slab_step, 0)
    stores = [
        pltpu.make_async_copy(r.xs, r.xs_o, r.store.at[0]),
        pltpu.make_async_copy(r.n1t, r.n1t_o, r.store.at[1]),
        pltpu.make_async_copy(r.valt, r.valt_o, r.store.at[2]),
    ]
    for copy in stores:
        copy.start()
    moves["o20"].wait_recv()
    moves["o30"].start()
    for k in (2, 3):
        near[k].wait_recv()
        onward[k].wait_recv()
    for copy in late:
        copy.wait()
    for copy in stores:
        copy.wait()
    stores = []
    sent = moves["x3"]
    sent.wait_send()

    def residual_step(j, carry):
        residual = r.xs[j].astype(F32) + mm_tn(r.attt[j], r.owv[...])

        @pl.when(j == 0)
        def _():
            r.res[...] = residual

        scaled, _ = standardize(residual)
        r.n2s[j] = (scaled * flat_row(r.gain2) + flat_row(r.bias2)).astype(BF16)
        return carry

    lax.fori_loop(2, 4, residual_step, 0)

    def send_cross(c):
        part = cut(c)
        moves[f"t3{c}"].wait_recv()
        r.crossb[part] = add_low(r.terms[2, part], r.near3[part])
        moves[f"c{c}"].start()

    def ffn_step(u, carry):
        j = jnp.where(u < 2, 2 + u, jnp.where(u < 6, (u - 2) // 2, u - 4))
        c = jnp.where(u < 2, 0, jnp.where(u < 6, u % 2, 1))

        @pl.when(u == 1)
        def _():
            moves["o30"].wait_recv()
            for k in (2, 3):
                far[k].wait_recv()
                onward[k ^ 2].start()

        @pl.when(u == 2)
        def _():
            for k in (0, 1):
                near[k].wait_recv()
                onward[k].wait_recv()
            moves["o1"].wait_recv()
            lax.fori_loop(0, 2, residual_step, 0)

        @pl.when(u == 6)
        def _():
            moves["o21"].wait_recv()
            moves["o31"].start()

        @pl.when(u == 7)
        def _():
            moves["o31"].wait_recv()

        part = pl.ds(pl.multiple_of(c * half, half), half)
        gated, slope = silu_and_slope(mm(r.n2s[j, part], r.upv[...]) + flat_row(r.upb))
        act = gated.astype(BF16)
        r.big[pl.ds(pl.multiple_of(j * rows + c * half, half), half)] = act
        pug = (mm_nt(r.ogs[j, part], r.downv[...]) * slope).astype(BF16)
        r.pug[j, part] = pug
        r.terms[j, part] = mm_nt(pug, r.upv[...]).astype(BF16)
        r.fterms[j, part] = mm(act, r.downv[...]).astype(BF16)

        @pl.when(u == 1)
        def _():
            moves["t30"].start()

        @pl.when(u == 2)
        def _():
            send_cross(0)

        @pl.when(u == 5)
        def _():
            moves["t1"].start()

        @pl.when(u == 7)
        def _():
            moves["t31"].start()

        return carry

    lax.fori_loop(0, 8, ffn_step, 0)
    send_cross(1)
    flat = (slabs * rows, width)
    r.acc[...] = mm_tn(r.ogs[...].reshape(flat), r.big[0 : slabs * rows])
    store_shards(r.dboth, r.acc)
    down_first.start()
    stores = [
        pltpu.make_async_copy(r.fterms, r.f_o, r.store.at[5]),
        pltpu.make_async_copy(r.res, r.res_o, r.store.at[6]),
    ]
    for copy in stores:
        copy.start()
    moves["t1"].wait_recv()

    for c in range(2):
        part = slice(c * half, (c + 1) * half)
        moves[f"c{c}"].wait_recv()
        cot = r.ogs[0, part].astype(F32)
        grad = r.terms[0, part].astype(F32) + r.near1[part].astype(F32)
        grad += r.crossr[part].astype(F32)
        scaled, inv_std = standardize(r.res[part])
        res_grad = cot + norm_back(grad, scaled, inv_std, flat_row(r.gain2))
        r.rg_o[part] = res_grad
        r.low[part] = res_grad.astype(BF16)
        r.mgt[:, part] = mm_nt(r.owv[...], r.low[part]).astype(BF16)
        for j in (2, 3, 1):
            moves[f"g{j}{c}"].start()
        r.mgts[0, :, part] = r.mgt[my_rows, part]
        for i, value in enumerate((grad * scaled, grad, cot)):
            total = jnp.sum(value, 0, keepdims=True)
            r.sums[i : i + 1] = total if c == 0 else r.sums[i : i + 1] + total

    mixed = r.attt[0]
    r.acc[...] = mm(mixed, r.low[...])
    span = width // 2
    mine = pl.ds(pl.multiple_of(me % 2 * span, BLOCK), span)
    theirs = pl.ds(pl.multiple_of((1 - me % 2) * span, BLOCK), span)
    r.osent[...] = r.acc[:, theirs].astype(BF16)
    columns.start()
    r.ohalf[...] = r.acc[:, mine]
    r.acc[...] = mm_tn(r.n2s[...].reshape(flat), r.pug[...].reshape(flat))
    for i in range(2):
        store_shards(r.uboth.at[i], r.acc, slice(i * span, (i + 1) * span))
        if i == 0:
            up_first.start()
    r.upb_sum[...] = jnp.sum(r.pug[...].reshape(flat).astype(F32), 0, keepdims=True)
    columns.wait_recv()
    r.ohalf[...] += r.ogot[...].astype(F32)
    store_shards(r.oboth, r.ohalf)
    more = [
        pltpu.make_async_copy(r.uboth.at[1], r.up2_o, r.store.at[4]),
        pltpu.make_async_copy(r.oboth, r.ow_o, r.store.at[7]),
    ]
    for copy in more:
        copy.start()
    stores += more
    for j in range(1, slabs):
        for c in range(2):
            moves[f"g{j}{c}"].wait_recv()
    stores.append(pltpu.make_async_copy(r.mgts, r.mgt_o, r.store.at[8]))
    stores[-1].start()
    down_first.wait_recv()
    add_got(r.dboth.at[0], r.dgot)
    stores.append(pltpu.make_async_copy(r.dboth.at[0], r.down_o, r.store.at[9]))
    stores[-1].start()
    up_first.wait_recv()
    add_got(r.uboth.at[0, 0], r.ugot)
    stores.append(pltpu.make_async_copy(r.uboth.at[0, 0], r.up1_o, r.store.at[10]))
    stores[-1].start()
    for copy in stores:
        copy.wait()
    total = slabs * heads
    for turn in (total - 2, total - 1):
        for copy in spills(turn // heads, turn % heads, turn % 2):
            copy.wait()
    for move in w.all:
        if move is not sent:
            move.wait_send()


def front(lens, x, og, gain1, bias1, gain2, bias2, upb, f1b, f2b, vt, f1, f2, ow, up, down):
    rows, width = x.shape
    heads, _, longest = f2.shape
    depth = vt.shape[0]
    units = up.shape[1]
    slabs = lax.axis_size("head")
    osh = shard_shape(width, width // 2)
    dsh = shard_shape(width, units)
    group = (slabs, rows, width)
    anywhere = pl.BlockSpec(memory_space=pl.ANY)
    vmem = pl.BlockSpec(memory_space=pltpu.VMEM)
    low = lambda *s: jax.ShapeDtypeStruct(s, BF16)
    wide = lambda *s: jax.ShapeDtypeStruct(s, F32)
    out_shape = [
        low(*group),
        low(slabs, width, rows),
        low(slabs, heads, rows, width),
        low(slabs, heads, rows, width),
        low(slabs, heads, rows, longest),
        low(slabs, depth, rows),
        low(slabs, depth, rows),
        low(*group),
        wide(rows, width),
        wide(rows, width),
        jax.ShapeDtypeStruct(dsh.shape[1:], BF16),
        jax.ShapeDtypeStruct(osh.shape[1:], BF16),
        osh,
        osh,
        wide(1, units),
        wide(3, width),
    ]
    out_specs = [vmem if n in ("rg_o", "upb_sum", "sums") else anywhere for n in FRONT_OUT]
    vl = lambda *s: pltpu.VMEM(s, BF16)
    vf = lambda *s: pltpu.VMEM(s, F32)
    scratch = dict(
        xs=vl(*group),
        n1=vl(rows, width),
        n1t=vl(slabs, width, rows),
        big=vl(max(heads * width, slabs * rows), width),
        f2v=vl(heads, width, longest),
        hidb=vl(2, rows, width),
        slopeb=vl(2, rows, width),
        probb=vl(2, rows, longest),
        valt=vl(slabs, depth, rows),
        attt=vl(slabs, width, rows),
        owv=vl(width, width),
        upv=vl(width, units),
        downv=vl(units, width),
        ogs=vl(*group),
        n2s=vl(*group),
        pug=vl(slabs, rows, units),
        near1=vl(rows, width),
        near3=vl(rows, width),
        crossb=vl(rows, width),
        crossr=vl(rows, width),
        fterms=vl(*group),
        res=vf(rows, width),
        mgts=vl(slabs, depth, rows),
        acc=vf(width, width),
        ohalf=vf(width, width // 2),
        osent=vl(width, width // 2),
        ogot=vl(width, width // 2),
        dboth=vl(*dsh.shape),
        dgot=vl(*dsh.shape[1:]),
        uboth=vl(2, *osh.shape),
        ugot=vl(*osh.shape[1:]),
        oboth=vl(*osh.shape),
        send=pltpu.SemaphoreType.DMA((14 + 5 * slabs,)),
        recv=pltpu.SemaphoreType.DMA((14 + 5 * slabs,)),
        load=pltpu.SemaphoreType.DMA((5 + 2 * heads,)),
        spill=pltpu.SemaphoreType.DMA((2, 3)),
        store=pltpu.SemaphoreType.DMA((11,)),
    )
    smem = pl.BlockSpec(memory_space=pltpu.SMEM)
    return pl.pallas_call(
        front_kernel,
        out_shape=out_shape,
        in_specs=[smem] + [anywhere] * 2 + [vmem] * 8 + [anywhere] * 5,
        out_specs=out_specs,
        scratch_shapes=[scratch[n] for n in FRONT_SCRATCH],
        compiler_params=pltpu.CompilerParams(
            collective_id=0, has_side_effects=True, vmem_limit_bytes=FUSED_LIMIT
        ),
        cost_estimate=cost(
            slabs * rows * width * (heads * (width + longest) + 6 * units), 60 << 20
        ),
        name="front",
    )(lens, x, og, gain1, bias1, gain2, bias2, upb, f1b, f2b, vt, f1, f2, ow, up, down)


BACK_IN = (
    "lens", "upb_sum", "sums", "gain1", "downb", "vt", "hid", "slope", "prob", "n1t", "valt", "mgt",
    "f1", "f2", "xs", "fterms", "down", "up1", "up2", "ow", "res", "rg",
)
BACK_OUT = ("result", "input", "ow_o", "down_o", "up_o", "f1_o", "f2_o", "val_o", "small_o")
BACK_SCRATCH = (
    "n1tv", "valtv", "mgtv", "vgt", "f1v", "f2v", "terms", "probb", "sg", "pog",
    "acc1", "acc2", "acc3", "xb", "near3", "near1", "crossr", "fb", "fnear3",
    "fnear1", "fcrossr", "rgv", "dk", "dgot", "uk", "ugot", "vk", "vhalf", "ok", "ogot", "oall", "olow", "aboth",
    "agot", "bboth", "bgot", "vboth", "vgot", "small", "small_in", "send",
    "recv", "load", "fetch", "store",
)


def back_kernel(*refs):
    r = types.SimpleNamespace(**dict(zip(BACK_IN + BACK_OUT + BACK_SCRATCH, refs)))
    r.crossb = r.terms.at[3]
    r.resv = r.acc1.at[pl.ds(0, r.rgv.shape[0])]
    slabs, heads, rows, width = r.pog.shape
    longest = r.probb.shape[2]
    depth = r.vgt.shape[1]
    dim = depth // heads
    blocks = rows // BLOCK
    count = r.ok.shape[0]
    me = lax.axis_index("head")
    turns = slabs * heads
    w = Wires(r.send, r.recv)
    sems = iter(range(6 * heads + 10))

    def shards(keep, send, got, out, far_first=False):
        own_sem, load_sem = r.store.at[next(sems)], r.store.at[next(sems)]
        return Shards(w, keep, send, got, out, own_sem, load_sem, far_first)

    down_group = shards(r.dk, None, r.dgot, r.down_o)
    up1_group = shards(r.vk, None, r.vhalf, r.up_o.at[0])
    up2_group = shards(r.uk, r.up2.at[1], r.ugot, r.up_o.at[1])
    out_group = shards(r.ok, r.ow.at[1], r.ogot, r.oall)
    out_heads = [w.remote(r.olow, r.ow_o.at[j], "head", j) for j in range(1, slabs)]
    f1_group, f2_group = [], []
    for h in range(heads):
        both = r.bboth.at[h]
        f2_group.append(shards(both.at[0], both.at[1], r.bgot.at[h], r.f2_o.at[h]))
        for i in range(2):
            both = r.aboth.at[h, i]
            f1_group.append(shards(both.at[0], both.at[1], r.agot.at[h, i], r.f1_o.at[h, i]))
    val_group = shards(r.vboth.at[0], r.vboth.at[1], r.vgot, r.val_o)
    fterm1 = w.remote(r.fterms.at[1], r.fnear1, "head", 1)
    fterm3 = w.remote(r.fterms.at[3], r.fnear3, "head", 1)
    fcross = w.remote(r.fb, r.fcrossr, "head", 2)
    term1 = w.remote(r.terms.at[1], r.near1, "head", 1)
    term3 = w.remote(r.terms.at[3], r.near3, "head", 1)
    cross = w.remote(r.crossb, r.crossr, "head", 2)
    steps = [1] + [2 * mask for mask in masks(count)]
    small_steps = [
        w.remote(r.small.at[i], r.small_in.at[i], "dp", step) for i, step in enumerate(steps)
    ]
    small_last = r.small.at[len(steps)]
    small_x = [
        w.remote(small_last, r.small_o.at[j], "head", j) for j in range(1, slabs)
    ]
    base = 6 * heads + 10
    own_low = pltpu.make_async_copy(r.olow, r.ow_o.at[0], r.store.at[base])
    own_small = pltpu.make_async_copy(small_last, r.small_o.at[0], r.store.at[base + 1])

    def load(index, src, dst):
        return pltpu.make_async_copy(src, dst, r.load.at[index])

    loads = [
        load(0, r.mgt, r.mgtv),
        load(1, r.valt, r.valtv),
        load(2, r.f2, r.f2v),
        load(3, r.n1t, r.n1tv),
        load(4, r.down, r.dk),
        load(5, r.fterms.at[2], r.fb),
        load(6, r.f1, r.f1v),
        load(7, r.xs.at[3], r.xb),
        load(9, r.rg, r.rgv),
        load(10, r.up2.at[0], r.uk),
        load(11, r.ow.at[0], r.ok),
    ]

    def fetches(turn):
        h, j, slot = turn // slabs, turn % slabs, turn % 2
        return [
            pltpu.make_async_copy(r.prob.at[j, h], r.probb.at[slot], r.fetch.at[slot, 0]),
            pltpu.make_async_copy(r.slope.at[j, h], r.terms.at[2 + slot], r.fetch.at[slot, 1]),
            pltpu.make_async_copy(r.hid.at[j, h], r.terms.at[slot], r.fetch.at[slot, 2]),
        ]

    up1_load = load(13, r.up1, r.vk)
    for copy in loads[:2] + fetches(0) + loads[2:] + [up1_load]:
        copy.start()
    greet(partners(True))
    up2_group.start()
    out_group.start()
    fterm3.start()
    fterm1.start()
    r.small[0] = jnp.zeros(r.small.shape[1:], F32)
    r.small[0, 2 * heads : 2 * heads + 1] = r.upb_sum[...]
    r.small[0, 2 * heads + 3 : 2 * heads + 6] = r.sums[...]
    for copy in loads[:6]:
        copy.wait()
    down_group.second()
    up1_load.wait()
    up1_group.second()

    def turn_step(turn, carry):
        h, j, slot = turn // slabs, turn % slabs, turn % 2
        for copy in fetches(turn):
            copy.wait()

        @pl.when(turn + 1 < turns)
        def _():
            for copy in fetches(turn + 1):
                copy.start()

        @pl.when(j == 0)
        def _():
            r.acc1[...] = jnp.zeros_like(r.acc1)
            r.acc2[...] = jnp.zeros_like(r.acc2)

        head_rows = pl.ds(pl.multiple_of(h * dim, dim), dim)
        mgt = r.mgtv[j, head_rows]
        r.vgt[j, head_rows] = mm(mgt, r.probb[slot]).astype(BF16)
        probs_grad = mm_tn(mgt, r.valtv[j, head_rows])
        first = jnp.bitwise_xor(me, j) * blocks
        zero = jnp.zeros((BLOCK, BLOCK), F32)
        for b in range(blocks):
            length = r.lens[first + b]
            own = slice(b * BLOCK, (b + 1) * BLOCK)
            prob = r.probb[slot, own].astype(F32)
            grad = probs_grad[own]
            inner = jnp.sum(prob * grad, -1, keepdims=True)
            parts = cells(prob * (grad - inner))
            is_full = length == longest
            is_half = length == longest // 2
            for c in range(blocks):
                half = parts[2 * (b // 2) + c] if c < 2 else zero
                quarter = parts[b] if c == 0 else zero
                cell = jnp.where(is_full, parts[c], jnp.where(is_half, half, quarter))
                r.sg[own, c * BLOCK : (c + 1) * BLOCK] = cell.astype(BF16)
        scores_grad = r.sg[...]
        row = pl.ds(h, 1)
        pog = (mm_nt(scores_grad, r.f2v[h]) * r.terms[2 + slot].astype(F32)).astype(BF16)
        r.pog[j, h] = pog
        r.small[0, row] += jnp.sum(pog.astype(F32), 0, keepdims=True)
        row = pl.ds(heads + h, 1)
        r.small[0, row, 0:longest] += jnp.sum(scores_grad.astype(F32), 0, keepdims=True)
        r.acc2[...] += mm_tn(r.terms[slot], scores_grad)
        r.acc1[...] += mm(r.n1tv[j], pog)

        for k in range(heads):

            @pl.when(turn == slabs * k + slabs - 1)
            def _(k=k):
                store_shards(r.bboth.at[k], r.acc2)
                f2_group[k].start()
                for i in range(2):
                    span = width // 2
                    store_shards(r.aboth.at[k, i], r.acc1, slice(i * span, (i + 1) * span))
                    if k < heads - 1:
                        f1_group[2 * k + i].start()

        @pl.when(turn == 1)
        def _():
            fterm3.wait_recv()
            r.fb[...] = add_low(r.fb[...], r.fnear3[...])
            fcross.start()

        @pl.when(turn == 2)
        def _():
            for copy in loads[9:]:
                copy.wait()
            down_group.third()
            up2_group.second()

        @pl.when(turn == 3)
        def _():
            up1_group.third()

        @pl.when(turn == 4)
        def _():
            out_group.second()
            up2_group.third()

        @pl.when(turn == 6)
        def _():
            out_group.third()
            f2_group[0].second()

        @pl.when(turn == 8)
        def _():
            f1_group[0].second()
            f2_group[0].third()

        @pl.when(turn == 9)
        def _():
            out_group.finish()
            r.olow[...] = (r.oall[0].astype(F32) + r.oall[1].astype(F32)).astype(BF16)
            for move in out_heads:
                move.start()
            own_low.start()

        @pl.when(turn == 10)
        def _():
            f1_group[1].second()
            f1_group[0].third()

        return carry

    lax.fori_loop(0, turns, turn_step, 0)
    for copy in loads[6:8]:
        copy.wait()
    res_load = load(8, r.res, r.resv)
    res_load.start()

    def term_step(i, carry):
        j = slabs - 1 - i

        @pl.when(i > 0)
        def _():
            load(7, r.xs.at[j], r.xb).wait()

        term = mm_tn(r.vgt[j], r.vt[...])
        for h in range(heads):
            term += mm_nt(r.pog[j, h], r.f1v[h])
        low = term.astype(BF16)
        r.terms[j] = low
        wide = low.astype(F32)
        scaled, _ = standardize(r.xb[...].astype(F32))
        at = 2 * heads + 1
        r.small[0, at : at + 1] += jnp.sum(wide * scaled, 0, keepdims=True)
        r.small[0, at + 1 : at + 2] += jnp.sum(wide, 0, keepdims=True)

        @pl.when(i < slabs - 1)
        def _():
            load(7, r.xs.at[j - 1], r.xb).start()

        @pl.when(i == 0)
        def _():
            term3.start()
            f1_group[1].third()

        @pl.when(i == 1)
        def _():
            term3.wait_recv()
            term3.wait_send()
            r.crossb[...] = add_low(r.terms[2], r.near3[...])
            cross.start()
            f2_group[1].second()

        @pl.when(i == 2)
        def _():
            term1.start()
            f1_group[2].second()
            f2_group[1].third()

        return carry

    lax.fori_loop(0, slabs, term_step, 0)
    small_steps[0].start()
    f1_group[4].start()
    f1_group[5].start()
    f1_group[3].second()
    f1_group[2].third()
    total = mm_nt(r.n1tv[0], r.vgt[0])
    for j in range(1, slabs):
        total += mm_nt(r.n1tv[j], r.vgt[j])
    r.acc3[...] = total
    store_shards(r.vboth, r.acc3)
    val_group.start()
    fcross.wait_send()
    own_fterm = load(12, r.fterms.at[0], r.fb)
    own_fterm.start()
    for copy in [res_load, loads[8], own_fterm]:
        copy.wait()
    fterm1.wait_recv()
    fcross.wait_recv()
    others = r.fnear1[...].astype(F32) + r.fcrossr[...].astype(F32)
    r.resv[...] += r.fb[...].astype(F32) + others + flat_row(r.downb)
    finals = [pltpu.make_async_copy(r.resv, r.result, r.store.at[base + 2])]
    finals[0].start()

    def small_step(i):
        small_steps[i].wait_recv()
        r.small[i + 1] = r.small[i] + r.small_in[i]
        for after in small_steps[i + 1 : i + 2] or small_x + [own_small]:
            after.start()

    small_step(0)
    f1_group[3].third()
    term1.wait_recv()
    cross.wait_recv()
    grad = r.terms[0].astype(F32) + r.near1[...].astype(F32) + r.crossr[...].astype(F32)
    scaled, inv_std = standardize(r.xb[...].astype(F32))
    r.rgv[...] += norm_back(grad, scaled, inv_std, flat_row(r.gain1))
    finals.append(pltpu.make_async_copy(r.rgv, r.input, r.store.at[base + 3]))
    finals[1].start()
    small_step(1)
    f2_group[2].second()
    for i in range(2, len(steps)):
        small_step(i)
    f1_group[4].second()
    f2_group[2].third()
    f1_group[5].second()
    f1_group[4].third()
    val_group.second()
    f1_group[5].third()
    val_group.third()
    for group in [down_group, up1_group, up2_group] + f2_group + f1_group + [val_group]:
        group.finish()
    for move in out_heads + small_x:
        move.wait_recv()
    for copy in finals + [own_low, own_small]:
        copy.wait()
    for move in w.all:
        if move is not term3 and move is not fcross:
            move.wait_send()


def low_shape(*shape):
    return jax.ShapeDtypeStruct(shape, BF16)


def wide_shape(*shape):
    return jax.ShapeDtypeStruct(shape, F32)


def back(*args):
    hid, f2, vt, ow = args[6], args[13], args[5], args[19]
    slabs, heads, rows, width = hid.shape
    longest = f2.shape[2]
    depth = vt.shape[0]
    _, count, part, span = ow.shape
    small = (2 * heads + 6 + 7) // 8 * 8
    low, wide = low_shape, wide_shape
    out_shape = [
        wide(rows, width),
        wide(rows, width),
        low(slabs, part, span),
        low(count, part, width),
        low(2, count, part, span),
        low(heads, 2, count, part, span),
        low(heads, count, part, longest),
        low(count, part, depth),
        wide(slabs, small, width),
    ]
    vl = lambda *s: pltpu.VMEM(s, BF16)
    vf = lambda *s: pltpu.VMEM(s, F32)
    steps = len(masks(count)) + 1
    moves = 2 * (slabs - 1) + (3 * heads + 6) * steps + 6
    scratch = dict(
        n1tv=vl(slabs, width, rows),
        valtv=vl(slabs, depth, rows),
        mgtv=vl(slabs, depth, rows),
        vgt=vl(slabs, depth, rows),
        f1v=vl(heads, width, width),
        f2v=vl(heads, width, longest),
        probb=vl(2, rows, longest),
        sg=vl(rows, longest),
        pog=vl(slabs, heads, rows, width),
        acc1=vf(width, width),
        acc2=vf(width, longest),
        acc3=vf(width, depth),
        xb=vl(rows, width),
        terms=vl(slabs, rows, width),
        near3=vl(rows, width),
        near1=vl(rows, width),
        crossr=vl(rows, width),
        fb=vl(rows, width),
        fnear3=vl(rows, width),
        fnear1=vl(rows, width),
        fcrossr=vl(rows, width),
        rgv=vf(rows, width),
        ok=vl(count, part, span),
        ogot=vl(count, part, span),
        oall=vl(count, part, span),
        olow=vl(part, span),
        dk=vl(count, part, width),
        dgot=vl(count // 2, part, width),
        uk=vl(count, part, span),
        ugot=vl(count, part, span),
        vk=vl(count, part, span),
        vhalf=vl(count // 2, part, span),
        aboth=vl(heads, 2, 2, count, part, span),
        agot=vl(heads, 2, count, part, span),
        bboth=vl(heads, 2, count, part, longest),
        bgot=vl(heads, count, part, longest),
        vboth=vl(2, count, part, depth),
        vgot=vl(count, part, depth),
        small=vf(steps + 1, small, width),
        small_in=vf(steps, small, width),
        send=pltpu.SemaphoreType.DMA((moves,)),
        recv=pltpu.SemaphoreType.DMA((moves,)),
        load=pltpu.SemaphoreType.DMA((14,)),
        fetch=pltpu.SemaphoreType.DMA((2, 3)),
        store=pltpu.SemaphoreType.DMA((14 + 6 * heads,)),
    )
    smem = pl.BlockSpec(memory_space=pltpu.SMEM)
    anywhere = pl.BlockSpec(memory_space=pl.ANY)
    vmem = pl.BlockSpec(memory_space=pltpu.VMEM)
    return pl.pallas_call(
        back_kernel,
        out_shape=out_shape,
        in_specs=[smem] + [vmem] * 5 + [anywhere] * 16,
        out_specs=[anywhere] * len(out_shape),
        scratch_shapes=[scratch[n] for n in BACK_SCRATCH],
        compiler_params=pltpu.CompilerParams(
            collective_id=1, has_side_effects=True, vmem_limit_bytes=FUSED_LIMIT
        ),
        cost_estimate=cost(slabs * rows * width * heads * (3 * width + 2 * longest), 60 << 20),
        name="back",
    )(*args)


def finish_kernel(*refs):
    result, inp, small, down, up, ow, f1, f2, val = refs[:9]
    (
        result_o, input_o, f1b_o, f2b_o, upb_o, down_o, up_o, ow_o, f1_o, f2_o, val_o,
    ) = refs[9:20]
    shared = refs[20:25]
    result_o[...] = result[...]
    input_o[...] = inp[...]
    slabs = small.shape[0]
    heads = f1.shape[0]
    longest = f2.shape[3]
    me = lax.axis_index("head")
    for j in range(slabs):
        owner = jnp.bitwise_xor(me, j)
        units = small.shape[2]
        own = small[owner, 2 * heads : 2 * heads + 1]
        upb_o[j * units : (j + 1) * units] = own.reshape(units)
        for h in range(heads):
            f1b_o[pl.ds(owner * heads + h, 1)] = small[j, h : h + 1]
            f2b_o[pl.ds(owner * heads + h, 1)] = small[j, heads + h : heads + h + 1, 0:longest]
    first = 2 * heads + 1
    for i, ref in enumerate(shared):
        ref[...] = sum(small[j, first + i] for j in range(slabs))
    span = ow.shape[2]
    mine = pl.ds(pl.multiple_of(me % 2 * span, BLOCK), span)
    theirs = pl.ds(pl.multiple_of((1 - me % 2) * span, BLOCK), span)
    ow_o[:, mine] = sum(ow[j].astype(F32) for j in range(0, slabs, 2))
    ow_o[:, theirs] = sum(ow[j].astype(F32) for j in range(1, slabs, 2))
    total = lambda ref: ref[0].astype(F32) + ref[1].astype(F32)
    down_o[...] = total(down)
    for i in range(2):
        up_o[:, i * span : (i + 1) * span] = total(up.at[i])
    val_o[...] = total(val)
    for h in range(heads):
        for i in range(2):
            f1_o[h, :, i * span : (i + 1) * span] = total(f1.at[h, i])
        f2_o[h] = total(f2.at[h])


def finish(members, *args):
    f1, f2, val = args[6:]
    rows, width = args[0].shape
    heads, _, part, longest = f2.shape
    wide = wide_shape
    out_shape = [
        wide(rows, width),
        wide(rows, width),
        wide(members * heads, width),
        wide(members * heads, longest),
        wide(members * width),
        wide(part, width),
        wide(part, width),
        wide(part, width),
        wide(heads, part, width),
        wide(heads, part, longest),
        wide(part, val.shape[2]),
    ] + [wide(width)] * 5
    whole = lambda v: pl.BlockSpec(v.shape, lambda _: (0,) * v.ndim)
    pair = lambda v: pl.BlockSpec((2,) + v.shape[1:], lambda _: (0, 0, 0))
    heads_pair = lambda v: pl.BlockSpec((heads, 2) + v.shape[2:], lambda _: (0, 0, 0, 0))
    sides = lambda v: pl.BlockSpec((2, 2) + v.shape[2:], lambda _: (0,) * 4)
    halves = lambda v: pl.BlockSpec((heads, 2, 2) + v.shape[3:], lambda _: (0,) * 5)
    kinds = [whole] * 3 + [pair, sides, whole, halves, heads_pair, pair]
    return pl.pallas_call(
        finish_kernel,
        grid=(1,),
        out_shape=out_shape,
        in_specs=[kind(v) for kind, v in zip(kinds, args)],
        out_specs=[whole(v) for v in out_shape],
        compiler_params=pltpu.CompilerParams(vmem_limit_bytes=FUSED_LIMIT),
        cost_estimate=cost(0, 20 << 20),
        name="finish",
    )(*args)


def local(
    tokens,
    seq_len,
    norm1_gain,
    norm1_bias,
    f1_weight,
    f1_bias,
    f2_weight,
    f2_bias,
    value_weight,
    out_weight,
    norm2_gain,
    norm2_bias,
    up_weight,
    up_bias,
    down_weight,
    down_bias,
    out_grad,
):
    members = lax.axis_size("head")
    vt = value_weight.T
    (
        xs, n1t, hid, slope, prob, valt, mgt, fterms, res_grad, residual, down_y, up1_y, up2_y, ow_y,
        upb, sums2,
    ) = front(
        seq_len, tokens, out_grad, norm1_gain, norm1_bias, norm2_gain, norm2_bias, up_bias, f1_bias,
        f2_bias, vt, f1_weight, f2_weight, out_weight, up_weight, down_weight,
    )
    (
        result, input_grad, ow_parts, down_parts, up_parts, f1_parts, f2_parts, val_parts, small,
    ) = back(
        seq_len, upb, sums2, norm1_gain, down_bias, vt, hid, slope, prob, n1t, valt, mgt,
        f1_weight, f2_weight, xs, fterms, down_y, up1_y, up2_y, ow_y, residual, res_grad,
    )
    (
        result, input_grad, f1b_all, f2b_all, upb_all, down_piece, up_piece, out_piece, f1_piece,
        f2_piece, value_piece, gain1_g, bias1_g, gain2_g, bias2_g, downb_g,
    ) = finish(
        members, result, input_grad, small, down_parts, up_parts, ow_parts, f1_parts, f2_parts,
        val_parts,
    )
    return (
        result,
        input_grad,
        gain1_g,
        bias1_g,
        f1_piece,
        f1b_all,
        f2_piece,
        f2b_all,
        value_piece,
        out_piece,
        gain2_g,
        bias2_g,
        up_piece,
        upb_all,
        down_piece.T,
        downb_g,
    )


def solution(mesh):
    placed = (
        P(("dp", "head"), None),
        P("dp"),
        P(),
        P(),
        P("head", None, None),
        P("head", None),
        P("head", None, None),
        P("head", None),
        P(None, "head"),
        P(),
        P(),
        P(),
        P(None, "head"),
        P("head"),
        P("head", None),
        P(),
        P(("dp", "head"), None),
    )
    return jax.shard_map(
        local,
        mesh=mesh,
        in_specs=placed,
        out_specs=(
            P(("dp", "head"), None),
            P(("dp", "head"), None),
            P(),
            P(),
            P("head", "dp", None),
            P(),
            P("head", "dp", None),
            P(),
            P("dp", "head"),
            P("dp", None),
            P(),
            P(),
            P("dp", "head"),
            P(),
            P("head", "dp"),
            P(),
        ),
        check_vma=False,
    )
```
